32 devices in a mesh: rep: 8 (over y, x, core), seq: 4 (over z).
Axes of the slice: x: 2, y: 2, z: 4, core: 2. Of those that a mesh axis runs over, the one named last changes fastest.
Arguments:
- block_input: bfloat16 [8192, 1536], P(('rep', 'seq')), may hold values from -6 to 6
- cotangent: bfloat16 [8192, 1536], P(('rep', 'seq')), may hold values from -6 to 6
- lengths: int32 [8], P('rep'), may hold values from 256 to 1024, as said below
- offsets: int32 [8], P('rep'), may hold values from 0 to 768, as said below
- norm_gains: bfloat16 [2, 2, 1536], P(None, None, 'seq'), may hold values from 0.5 to 1.5
- branch_proj: bfloat16 [2, 1536, 2048], P(None, 'seq'), may hold values from -0.15625 to 0.15625
- stream_proj: bfloat16 [2, 1536, 2048], P(None, 'seq'), may hold values from -0.15625 to 0.15625
- conv_kernel: bfloat16 [2, 4, 2048], P(None, None, 'seq'), may hold values from -3 to 3
- conv_bias: bfloat16 [2, 2048], P(None, 'seq'), may hold values from -2 to 2
- rate_proj: bfloat16 [2, 2048, 256], P(None, 'seq'), may hold values from -0.375 to 0.375
- admit_proj: bfloat16 [2, 2048, 256], P(None, 'seq'), may hold values from -0.375 to 0.375
- gate_bias: bfloat16 [2, 2, 2048], P(None, None, 'seq'), may hold values from -3 to 3
- decay_logit: bfloat16 [2, 2048], P(None, 'seq'), may hold values from 2.1875 to 9.1875
- out_proj: bfloat16 [2, 2048, 1536], P(None, 'seq'), may hold values from -0.25 to 0.25
- mlp_gate: bfloat16 [2, 1536, 4608], P(None, 'seq'), may hold values from -0.15625 to 0.15625
- mlp_up: bfloat16 [2, 1536, 4608], P(None, 'seq'), may hold values from -0.15625 to 0.15625
- mlp_down: bfloat16 [2, 4608, 1536], P(None, 'seq'), may hold values from -0.125 to 0.125
Outputs:
- block_output: bfloat16 [8192, 1536], P(('rep', 'seq'))
- input_grad: float32 [8192, 1536], P(('rep', 'seq'))
- grad_norm_gains: float32 [2, 2, 1536], P(None, None, ('rep', 'seq'))
- grad_branch_proj: float32 [2, 1536, 2048], P(None, ('rep', 'seq'))
- grad_stream_proj: float32 [2, 1536, 2048], P(None, ('rep', 'seq'))
- grad_conv_kernel: float32 [2, 4, 2048], P(None, None, ('rep', 'seq'))
- grad_conv_bias: float32 [2, 2048], P(None, ('rep', 'seq'))
- grad_rate_proj: float32 [2, 2048, 256], P(None, ('rep', 'seq'))
- grad_admit_proj: float32 [2, 2048, 256], P(None, ('rep', 'seq'))
- grad_gate_bias: float32 [2, 2, 2048], P(None, None, ('rep', 'seq'))
- grad_decay_logit: float32 [2, 2048], P(None, ('rep', 'seq'))
- grad_out_proj: float32 [2, 2048, 1536], P(None, ('rep', 'seq'))
- grad_mlp_gate: float32 [2, 1536, 4608], P(None, ('rep', 'seq'))
- grad_mlp_up: float32 [2, 1536, 4608], P(None, ('rep', 'seq'))
- grad_mlp_down: float32 [2, 4608, 1536], P(None, ('rep', 'seq'))
The draws below stay inside these ranges and needn't reach their ends.
Inputs may be any that keep to these rules, and one draw needn't show every extreme that they name: `lengths`: some group's sequence fills its whole slot of 1024 positions and some group's has 256 positions. offsets[g] + lengths[g] <= 1024; some group's sequence ends at the slot's last position.
All inputs are finite; a program needn't handle non-finite values.
Results may differ from the reference program's by a relative error of at most 0.015.
Values may be sent and summed in bfloat16 or wider, within the bound.
A program may use at most 512 MiB of HBM per device.

```python
import jax
import jax.numpy as jnp
from jax import lax

D = 1536
R = 2048
FF = 4608
BLOCK = 256
CONV = 4
LAYERS = 2
SLOT = 1024
TOKENS = 8192
N_REP = 8


def slot_layout(key):
    folded = jax.random.fold_in(key, 11)
    key_len, key_full, key_off = jax.random.split(folded, 3)
    lengths = jax.random.randint(key_len, (N_REP,), SLOT // 4, SLOT + 1, dtype=jnp.int32)
    longest = jax.random.randint(key_full, (), 0, N_REP, dtype=jnp.int32)
    groups = jnp.arange(N_REP, dtype=jnp.int32)
    shortest = (longest + 1) % N_REP
    lengths = jnp.where(groups == longest, SLOT, lengths)
    lengths = jnp.where(groups == shortest, SLOT // 4, lengths)
    fraction = jax.random.randint(key_off, (N_REP,), 0, 4096, dtype=jnp.int32)
    offsets = fraction * (SLOT - lengths + 1) // 4096
    offsets = jnp.where(groups == shortest, SLOT - SLOT // 4, offsets)
    return (lengths, offsets)


def draw_lengths(key, part):
    return slot_layout(key)[0]


def draw_offsets(key, part):
    return slot_layout(key)[1]


def with_spikes(values, key, source, target, shards_of, factor):
    owner, partner = [(jnp.arange(values.shape[position]) // (values.shape[position] // shards_of)).reshape([-1 if axis == position else 1 for axis in range(values.ndim)]) for position in (source, target)]
    chosen = jax.random.permutation(key, shards_of)[partner]
    strong = (owner == chosen) | (owner == (partner + shards_of // 2) % shards_of)
    return jnp.where(strong, factor * values, values)


def steps_of(own_key, shape, cuts, least, largest):
    loudness, own = 1.0, jax.random.fold_in(own_key, 6)
    for position, shards_of in cuts:
        steps = jnp.exp(jax.random.uniform(jax.random.fold_in(own, position), (shards_of,), jnp.float32, least / len(cuts), largest / len(cuts)))
        loudness = loudness * jnp.repeat(steps, shape[position] // shards_of).reshape([-1 if axis == position else 1 for axis in range(len(shape))])
    return loudness


def centred(own_key, extent, deviation, limit, cuts=(), kind=jnp.bfloat16):
    entries = deviation * jax.random.normal(own_key, extent, jnp.float32)
    if cuts:
        entries = entries * steps_of(own_key, extent, cuts, -0.22, 0.18)
    return jnp.clip(entries, -limit, limit).astype(kind)


def bell_draw_with(stream_key, extent, scale, limit, shards, heavy, held_as=jnp.bfloat16):
    values = scale * jax.random.normal(stream_key, extent, jnp.float32)
    if shards:
        values = values * steps_of(stream_key, extent, shards, -0.22, 0.18)
    return jnp.clip(with_spikes(values, jax.random.fold_in(stream_key, 3), *heavy), -limit, limit).astype(held_as)


def setup_inputs(seed: int = 0) -> dict:
    streams_of = jax.random.split(jax.random.key(seed), 18)
    block_input = centred(streams_of[0], (TOKENS, D), 1.0, 6.0, ((0, 32),))
    cotangent = bell_draw_with(streams_of[1], (TOKENS, D), 1.0, 6.0, ((0, 32),), (0, 1, 32, 2.75))
    lengths = draw_lengths(jax.random.fold_in(streams_of[17], 71), 0)
    offsets = draw_offsets(jax.random.fold_in(streams_of[17], 71), 0)
    norm_gains = jnp.clip(1.0 + 0.1 * jax.random.normal(streams_of[4], (LAYERS, 2, D), jnp.float32), 0.5, 1.5).astype(jnp.bfloat16)
    branch_proj = centred(streams_of[5], (LAYERS, D, R), D ** -0.5, 0.15625, ((1, 4),))
    stream_proj = centred(streams_of[6], (LAYERS, D, R), D ** -0.5, 0.15625, ((1, 4),))
    conv_kernel = centred(streams_of[7], (LAYERS, CONV, R), CONV ** -0.5, 3.0, ((2, 4),))
    conv_bias = centred(streams_of[8], (LAYERS, R), 0.3, 2.0, ((1, 4),))
    rate_proj = centred(streams_of[9], (LAYERS, R, BLOCK), BLOCK ** -0.5, 0.375, ((1, 4),))
    admit_proj = centred(streams_of[10], (LAYERS, R, BLOCK), BLOCK ** -0.5, 0.375, ((1, 4),))
    gate_bias = centred(streams_of[11], (LAYERS, 2, R), 1.0, 3.0, ((2, 4),))
    decay_logit = jnp.clip(2.1875 + 7.0 * jax.random.uniform(streams_of[12], (LAYERS, R), jnp.float32) ** steps_of(streams_of[12], (LAYERS, R), ((1, 4),), -0.2, 0.2), 2.1875, 9.1875).astype(jnp.bfloat16)
    out_proj = centred(streams_of[13], (LAYERS, R, D), (R // 4) ** -0.5, 0.25, ((1, 4),))
    mlp_gate = centred(streams_of[14], (LAYERS, D, FF), D ** -0.5, 0.15625, ((1, 4),))
    mlp_up = centred(streams_of[15], (LAYERS, D, FF), D ** -0.5, 0.15625, ((1, 4),))
    mlp_down = centred(streams_of[16], (LAYERS, FF, D), (FF // 2) ** -0.5, 0.125, ((1, 4),))
    return dict(block_input=block_input, cotangent=cotangent, lengths=lengths, offsets=offsets, norm_gains=norm_gains, branch_proj=branch_proj, stream_proj=stream_proj, conv_kernel=conv_kernel, conv_bias=conv_bias, rate_proj=rate_proj, admit_proj=admit_proj, gate_bias=gate_bias, decay_logit=decay_logit, out_proj=out_proj, mlp_gate=mlp_gate, mlp_up=mlp_up, mlp_down=mlp_down)


EPSILON = 1e-06
HIGHEST = lax.Precision.HIGHEST

@jax.custom_vjp
def low(v):
    return lax.optimization_barrier(v.astype(jnp.bfloat16)).astype(jnp.float32)

@jax.custom_vjp
def low_back(v):
    return v

def low_keep(v):
    return (low(v), None)

def low_pass(kept, grad):
    return (grad,)

def back_keep(v):
    return (v, None)

def back_low(kept, grad):
    return (low(grad),)
low.defvjp(low_keep, low_pass)
low_back.defvjp(back_keep, back_low)

def matmul(left, right):
    return jnp.dot(left, right, precision=HIGHEST, preferred_element_type=jnp.float32)

def blockwise(values, weight):
    head_width = weight.shape[1]
    head_count = weight.shape[0] // head_width
    result = jnp.einsum('thi,hij->thj', values.reshape(values.shape[0], head_count, head_width), weight.reshape(head_count, head_width, head_width), precision=HIGHEST)
    return result.reshape(values.shape[0], head_count * head_width)

def rms_scale(values, scale_vec):
    return values * lax.rsqrt(lax.optimization_barrier(jnp.mean(values * values, axis=-1, keepdims=True)) + EPSILON) * scale_vec

def gate_terms(pre_rate, pre_admit, conv_value, decay_logit, gate_bias, restart):
    rate_gate = jax.nn.sigmoid(pre_rate + gate_bias[0])
    admit_gate = jax.nn.sigmoid(pre_admit + gate_bias[1])
    log_retain = -8.0 * rate_gate * jax.nn.softplus(-decay_logit)
    retain = jnp.where(restart, 0.0, jnp.exp(log_retain))
    input_scale = jnp.where(restart, 1.0, jnp.sqrt(-jnp.expm1(2.0 * log_retain)))
    return (retain, input_scale * admit_gate * conv_value)

def recurrence(retain, inflow):

    def advance(state, record):
        state = record[0] * state + record[1]
        return (state, state)
    _, states = lax.scan(advance, jnp.zeros((retain.shape[1],), retain.dtype), (retain, inflow))
    return states

def layer_forward(residual, params, restart, same_list):
    norm_gain, branch_proj, stream_proj, conv_kernel, conv_bias, rate_proj, admit_proj, gate_bias, decay_logit, out_proj, mlp_gate, mlp_up, mlp_down = params
    normed = low(rms_scale(residual, norm_gain[0]))
    branch = low_back(matmul(normed, branch_proj))
    stream = low_back(matmul(normed, stream_proj))
    mixed = conv_bias + conv_kernel[0] * stream
    for back_steps in range(1, CONV):
        moved = jnp.pad(stream, ((back_steps, 0), (0, 0)))[:-back_steps]
        mixed = mixed + conv_kernel[back_steps] * moved * same_list[back_steps - 1]
    conv_low = low(mixed)
    pre_rate = low_back(blockwise(conv_low, rate_proj))
    pre_admit = low_back(blockwise(conv_low, admit_proj))
    retain, inflow = gate_terms(pre_rate, pre_admit, conv_low, decay_logit, gate_bias, restart)
    states = recurrence(retain, inflow)
    joined = low(jax.nn.gelu(branch, approximate=True) * states)
    middle = residual + low_back(matmul(joined, out_proj))
    normed_two = low(rms_scale(middle, norm_gain[1]))
    up_gate = low_back(matmul(normed_two, mlp_gate))
    up_value = low_back(matmul(normed_two, mlp_up))
    hidden = low(jax.nn.gelu(up_gate, approximate=True) * up_value)
    return middle + low_back(matmul(hidden, mlp_down))

def reference(block_input, cotangent, lengths, offsets, norm_gains, branch_proj, stream_proj, conv_kernel, conv_bias, rate_proj, admit_proj, gate_bias, decay_logit, out_proj, mlp_gate, mlp_up, mlp_down):
    weights = tuple((weight.astype(jnp.float32) for weight in (norm_gains, branch_proj, stream_proj, conv_kernel, conv_bias, rate_proj, admit_proj, gate_bias, decay_logit, out_proj, mlp_gate, mlp_up, mlp_down)))
    positions = jnp.arange(SLOT, dtype=jnp.int32)

    def one_group(totals, record):
        slot_input, slot_cot, length, offset = record
        inside = (positions >= offset) & (positions < offset + length)
        restart = ((positions == 0) | (inside != jnp.roll(inside, 1)))[:, None]
        same_list = [(inside == jnp.roll(inside, back_steps)).astype(jnp.float32)[:, None] for back_steps in range(1, CONV)]

        def forward(start_value, params):
            residual = start_value
            for layer_idx in range(LAYERS):
                residual = layer_forward(residual, tuple((param[layer_idx] for param in params)), restart, same_list)
            return residual
        result, pullback = jax.vjp(forward, slot_input.astype(jnp.float32), weights)
        grad_in, grad_weights = pullback(slot_cot.astype(jnp.float32) * inside.astype(jnp.float32)[:, None])
        totals = jax.tree.map(lambda first, second: first + second, totals, grad_weights)
        return (totals, (result.astype(jnp.bfloat16), grad_in))
    zero_grads = jax.tree.map(jnp.zeros_like, weights)
    grads, (outputs, input_grads) = lax.scan(one_group, zero_grads, (block_input.reshape(N_REP, SLOT, D), cotangent.reshape(N_REP, SLOT, D), lengths, offsets))
    return (outputs.reshape(N_REP * SLOT, D), input_grads.reshape(N_REP * SLOT, D), grads[0], grads[1], grads[2], grads[3], grads[4], grads[5], grads[6], grads[7], grads[8], grads[9], grads[10], grads[11], grads[12])
```

```python
from functools import partial

import jax
import jax.numpy as jnp
from jax import lax
from jax.experimental import pallas as pl
from jax.experimental.pallas import tpu as pltpu
from jax.sharding import PartitionSpec as P

CONV = 4
LAYERS = 2
EPSILON = 1e-06
BF = jnp.bfloat16
F32 = jnp.float32


def dot(a, b):
    return jnp.dot(a, b, preferred_element_type=F32)


def dot_tn(a, b):
    return lax.dot_general(a, b, (((0,), (0,)), ((), ())), preferred_element_type=F32)


def dot_nt(a, b):
    return lax.dot_general(a, b, (((1,), (1,)), ((), ())), preferred_element_type=F32)


def rms_scale(values, scale_vec):
    return (
        values * lax.rsqrt(jnp.mean(values * values, axis=-1, keepdims=True) + EPSILON) * scale_vec
    )


def gate_terms(pre_rate, pre_admit, conv_value, decay_logit, gate_bias, restart):
    rate_gate = jax.nn.sigmoid(pre_rate + gate_bias[0])
    admit_gate = jax.nn.sigmoid(pre_admit + gate_bias[1])
    log_retain = -8.0 * rate_gate * jax.nn.softplus(-decay_logit)
    retain = jnp.where(restart, 0.0, jnp.exp(log_retain))
    input_scale = jnp.where(restart, 1.0, jnp.sqrt(-jnp.expm1(2.0 * log_retain)))
    return (retain, input_scale * admit_gate * conv_value)


def glu_product(gate_in, value_in):
    return jax.nn.gelu(gate_in, approximate=True) * value_in


class Plan:
    def __init__(self, mesh, heads):
        self.rep = mesh.shape["rep"]
        self.seq = mesh.shape["seq"]
        self.tp = min(heads, self.rep)
        self.dp = self.rep // self.tp
        tp, dp = self.tp, self.dp
        self.tp_groups = None if dp == 1 else [[d * tp + t for t in range(tp)] for d in range(dp)]
        self.dp_groups = [[d * tp + t for d in range(dp)] for t in range(tp)]


def gather_plane(plan, value):
    return lax.all_gather(value, "rep", axis=0, tiled=True, axis_index_groups=plan.tp_groups)


def scatter_plane(plan, value):
    return lax.psum_scatter(
        value, "rep", scatter_dimension=0, tiled=True, axis_index_groups=plan.tp_groups
    )


def owner_chunks(plan, value):
    tp, seq = plan.tp, plan.seq
    pairs = []
    for d in range(plan.dp):
        for j in range(tp):
            for z in range(seq):
                o = tp * z + j
                pairs.append(((d * tp + j) * seq + z, (d * tp + o // seq) * seq + o % seq))
    return lax.ppermute(value, ("rep", "seq"), pairs)


def to_owners(plan, chunk, axis):
    if plan.dp == 1:
        return chunk
    part = lax.psum_scatter(
        chunk, "rep", scatter_dimension=axis, tiled=True, axis_index_groups=plan.dp_groups
    )
    tp, seq, dp = plan.tp, plan.seq, plan.dp
    pairs = [
        ((d * tp + t) * seq + z, (t * seq + z) * dp + d)
        for d in range(dp)
        for t in range(tp)
        for z in range(seq)
    ]
    return lax.ppermute(part, ("rep", "seq"), pairs)


def shifted(plan, value, step):
    pairs = [(z, z + step) for z in range(plan.seq) if 0 <= z + step < plan.seq]
    return lax.ppermute(value, "seq", pairs)


def scan_body(reverse, rows, slots, a_ref, b_ref, h_ref, q_ref):
    width = a_ref.shape[1]

    def step(i, carry):
        state, decay = carry
        p = rows - 1 - i if reverse else i
        at = pl.ds(p, slots, stride=rows)
        a = a_ref[at, :]
        state = a * state + b_ref[at, :]
        decay = a * decay
        h_ref[at, :] = state
        q_ref[at, :] = decay
        return state, decay

    lax.fori_loop(
        0,
        rows,
        step,
        (jnp.zeros((slots, width), F32), jnp.ones((slots, width), F32)),
        unroll=8,
    )


def local_scan(a, b, slots, reverse):
    rows = a.shape[0] // slots
    width = 128
    spec = pl.BlockSpec((a.shape[0], width), lambda i: (0, i))
    shape = jax.ShapeDtypeStruct(a.shape, F32)
    return pl.pallas_call(
        partial(scan_body, reverse, rows, slots),
        grid=(a.shape[1] // width,),
        in_specs=[spec, spec],
        out_specs=[spec, spec],
        out_shape=[shape, shape],
        compiler_params=pltpu.CompilerParams(vmem_limit_bytes=40 << 20),
        cost_estimate=pl.CostEstimate(flops=0, bytes_accessed=16 * a.size, transcendentals=0),
    )(a, b)


def carried(plan, decay, state, reverse):
    ends = lax.all_gather(jnp.stack([decay, state]), "seq")
    place = lax.axis_index("seq")
    carry = jnp.zeros_like(state)
    order = range(plan.seq)
    for z in reversed(order) if reverse else order:
        ahead = z > place if reverse else z < place
        carry = jnp.where(ahead, ends[z, 0] * carry + ends[z, 1], carry)
    return carry


def masks_of(plan, lengths, offsets, rows):
    start = lax.axis_index("seq") * rows
    extra = CONV - 1
    positions = start + jnp.arange(rows + 2 * extra, dtype=jnp.int32) - extra
    inside = (positions >= offsets[:, None]) & (positions < (offsets + lengths)[:, None])
    core = inside[:, extra : extra + rows]
    restart = (positions[extra : extra + rows] == 0)[None] | (core != inside[:, extra - 1 : extra - 1 + rows])
    fwd = [
        (core == inside[:, extra - j : extra - j + rows]).astype(F32)[..., None]
        for j in range(1, CONV)
    ]
    back = [
        (core == inside[:, extra + j : extra + j + rows]).astype(F32)[..., None]
        for j in range(1, CONV)
    ]
    return restart.reshape(-1, 1), fwd, back


def layer_forward(plan, residual, w, masks):
    restart, same_fwd, _ = masks
    slots, rows = plan.tp, residual.shape[0]
    head = w["rate"].shape[0]
    normed = rms_scale(residual, w["gain"][0]).astype(BF)
    x = gather_plane(plan, normed)
    both = dot(x, w["col_rec"])
    branch, stream = both[:, :head], both[:, head:]
    stream3 = stream.reshape(slots, rows, head)
    before = shifted(plan, stream3[:, rows - (CONV - 1) :], 1)
    widened = jnp.concatenate([before, stream3], 1)
    taps = w["conv"]
    mixed = w["bias"] + taps[0] * stream3
    for j in range(1, CONV):
        low = CONV - 1 - j
        mixed = mixed + taps[j] * widened[:, low : low + rows] * same_fwd[j - 1]
    conv_low = mixed.astype(BF).reshape(slots * rows, head)
    pre_rate = dot(conv_low, w["rate"])
    pre_admit = dot(conv_low, w["admit"])
    retain, inflow = gate_terms(
        pre_rate, pre_admit, conv_low.astype(F32), w["decay"], w["gbias"], restart
    )
    states, running = local_scan(retain, inflow, slots, False)
    carry = carried(
        plan,
        running.reshape(slots, rows, head)[:, -1],
        states.reshape(slots, rows, head)[:, -1],
        False,
    )
    states = (
        states.reshape(slots, rows, head) + running.reshape(slots, rows, head) * carry[:, None]
    ).reshape(slots * rows, head)
    joined = glu_product(branch, states).astype(BF)
    middle = residual + scatter_plane(plan, dot(joined, w["out"]).astype(BF)).astype(F32)
    normed_two = rms_scale(middle, w["gain"][1]).astype(BF)
    x_two = gather_plane(plan, normed_two)
    up = dot(x_two, w["col_mlp"])
    half = up.shape[1] // 2
    hidden = glu_product(up[:, :half], up[:, half:]).astype(BF)
    output = middle + scatter_plane(plan, dot(hidden, w["down"]).astype(BF)).astype(F32)
    saved = (
        residual, x, branch, widened, conv_low, pre_rate, pre_admit, retain, states, carry,
        joined, middle, x_two, up, hidden,
    )
    return output, saved


def layer_backward(plan, upstream, w, saved, masks):
    (
        residual, x, branch, widened, conv_low, pre_rate, pre_admit, retain, states, carry,
        joined, middle, x_two, up, hidden,
    ) = saved
    restart, same_fwd, same_back = masks
    slots, rows = plan.tp, residual.shape[0]
    seq = plan.seq
    head = w["rate"].shape[0]
    half = up.shape[1] // 2
    down_low = gather_plane(plan, upstream.astype(BF))
    grad_hidden = dot_nt(down_low, w["down"])
    _, glu_pull = jax.vjp(glu_product, up[:, :half], up[:, half:])
    grad_up = jnp.concatenate([p.astype(BF) for p in glu_pull(grad_hidden)], 1)
    grad_two = scatter_plane(plan, dot_nt(grad_up, w["col_mlp"]).astype(BF)).astype(F32)
    g_down = dot_tn(hidden, down_low)
    g_col_mlp = dot_tn(x_two, grad_up)
    _, pull_two = jax.vjp(rms_scale, middle, w["gain"][1])
    part, grad_gain_two = pull_two(grad_two)
    grad_middle = upstream + part
    mid_low = gather_plane(plan, grad_middle.astype(BF))
    g_out = dot_tn(joined, mid_low)
    grad_joined = dot_nt(mid_low, w["out"])
    _, mix_pull = jax.vjp(glu_product, branch, states)
    branch_part, grad_direct = mix_pull(grad_joined)
    retain3 = retain.reshape(slots, rows, head)
    retain_next = jnp.concatenate([retain3[:, 1:], jnp.ones_like(retain3[:, :1])], 1)
    local, suffix = local_scan(retain_next.reshape(-1, head), grad_direct, slots, True)
    local3, suffix3 = local.reshape(retain3.shape), suffix.reshape(retain3.shape)
    first = retain3[:, 0]
    incoming = carried(plan, first * suffix3[:, 0], first * local3[:, 0], True)
    grad_states3 = local3 + suffix3 * incoming[:, None]
    grad_states = grad_states3.reshape(-1, head)
    states3 = states.reshape(retain3.shape)
    previous = jnp.concatenate([carry[:, None], states3[:, :-1]], 1).reshape(-1, head)
    _, gate_pull = jax.vjp(
        partial(gate_terms, restart=restart),
        pre_rate, pre_admit, conv_low.astype(F32), w["decay"], w["gbias"],
    )
    rate_part, admit_part, grad_conv, grad_decay, grad_gbias = gate_pull(
        (grad_states * previous, grad_states)
    )
    grad_pre = jnp.concatenate([rate_part.astype(BF), admit_part.astype(BF)], 1)
    g_gates = dot_tn(conv_low, grad_pre)
    grad_mixed = (
        grad_conv + dot_nt(grad_pre[:, :head], w["rate"]) + dot_nt(grad_pre[:, head:], w["admit"])
    ).reshape(slots, rows, head)
    after = shifted(plan, grad_mixed[:, : CONV - 1], -1)
    wide_grad = jnp.concatenate([grad_mixed, after], 1)
    taps = w["conv"]
    tap_rows = [jnp.sum(grad_mixed * widened[:, CONV - 1 :], axis=(0, 1))]
    grad_stream = taps[0] * grad_mixed
    for j in range(1, CONV):
        low = CONV - 1 - j
        tap_rows.append(
            jnp.sum(grad_mixed * widened[:, low : low + rows] * same_fwd[j - 1], axis=(0, 1))
        )
        grad_stream = grad_stream + taps[j] * wide_grad[:, j : j + rows] * same_back[j - 1]
    grad_bias = jnp.sum(grad_mixed, axis=(0, 1))
    grad_both = jnp.concatenate(
        [branch_part.astype(BF), grad_stream.astype(BF).reshape(-1, head)], 1
    )
    grad_normed = scatter_plane(plan, dot_nt(grad_both, w["col_rec"]).astype(BF)).astype(F32)
    g_col_rec = dot_tn(x, grad_both)
    _, pull_one = jax.vjp(rms_scale, residual, w["gain"][0])
    part, grad_gain_one = pull_one(grad_normed)
    channel = jnp.stack(tap_rows + [grad_bias, grad_gbias[0], grad_gbias[1], grad_decay], 0)
    gains = jnp.stack([grad_gain_one, grad_gain_two], 0)
    return grad_middle + part, (g_col_rec, g_gates, g_out, g_col_mlp, g_down), channel, gains


def local(plan, *args):
    (
        block_input, cotangent, lengths, offsets, norm_gains, branch_proj, stream_proj, conv_kernel,
        conv_bias, rate_proj, admit_proj, gate_bias, decay_logit, out_proj, mlp_gate, mlp_up,
        mlp_down,
    ) = args
    tp, dp, seq = plan.tp, plan.dp, plan.seq
    t = lax.axis_index("rep") % tp
    z = lax.axis_index("seq")
    rows = block_input.shape[0]
    head = branch_proj.shape[2] // tp
    units = mlp_gate.shape[2] // tp

    channels = conv_kernel.shape[2]
    small = jnp.concatenate(
        [
            conv_kernel,
            conv_bias[:, None],
            gate_bias,
            decay_logit[:, None],
        ],
        1,
    )
    packed = jnp.concatenate([small.reshape(-1), norm_gains.reshape(-1)])
    packed = lax.all_gather(packed, "seq")
    small = packed[:, : small.size].reshape(seq, LAYERS, 8, channels)
    small = jnp.moveaxis(small, 0, 2).reshape(LAYERS, 8, seq * channels)
    small = lax.dynamic_slice_in_dim(small, t * head, head, 2).astype(F32)
    gains = packed[:, LAYERS * 8 * channels :].reshape(seq, LAYERS, 2, -1)
    gains = jnp.moveaxis(gains, 0, 2).reshape(LAYERS, 2, -1).astype(F32)
    layout = gather_plane(plan, jnp.stack([lengths, offsets], 1))
    masks = masks_of(plan, layout[:, 0], layout[:, 1], rows)

    def col(weight, layer, width):
        return lax.dynamic_slice_in_dim(weight[layer], t * width, width, 1)

    def chunk(weight, layer):
        size = weight.shape[1] // tp
        return lax.dynamic_slice_in_dim(weight[layer], t * size, size, 0)

    weights = []
    for l in range(LAYERS):
        col_rec = jnp.concatenate([col(branch_proj, l, head), col(stream_proj, l, head)], 1)
        col_mlp = jnp.concatenate([col(mlp_gate, l, units), col(mlp_up, l, units)], 1)
        wide = owner_chunks(plan, jnp.concatenate([chunk(out_proj, l), chunk(mlp_down, l)], 0))
        out_rows = out_proj.shape[1] // tp
        gates = owner_chunks(plan, jnp.concatenate([chunk(rate_proj, l), chunk(admit_proj, l)], 1))
        gates = lax.all_gather(gates, "seq", axis=0, tiled=True)
        weights.append(
            dict(
                gain=gains[l],
                conv=small[l, :CONV],
                bias=small[l, CONV],
                gbias=small[l, CONV + 1 : CONV + 3],
                decay=small[l, CONV + 3],
                col_rec=lax.all_gather(col_rec, "seq", axis=0, tiled=True),
                rate=gates[:, :head],
                admit=gates[:, head:],
                out=lax.all_gather(wide[:out_rows], "seq", axis=0, tiled=True),
                col_mlp=lax.all_gather(col_mlp, "seq", axis=0, tiled=True),
                down=lax.all_gather(wide[out_rows:], "seq", axis=0, tiled=True),
            )
        )

    residual = block_input.astype(F32)
    saved_all = []
    for l in range(LAYERS):
        residual, saved = layer_forward(plan, residual, weights[l], masks)
        saved_all.append(saved)
    positions = z * rows + jnp.arange(rows, dtype=jnp.int32)
    inside = (positions >= offsets[0]) & (positions < offsets[0] + lengths[0])
    gradient = cotangent.astype(F32) * inside.astype(F32)[:, None]

    outs = [None] * LAYERS
    channel_all, gain_all = [None] * LAYERS, [None] * LAYERS

    def over_seq(value):
        return lax.psum_scatter(value, "seq", scatter_dimension=0, tiled=False)

    def exchange(share):
        return lax.all_to_all(
            share, "rep", split_axis=0, concat_axis=0, axis_index_groups=plan.tp_groups
        )

    for l in reversed(range(LAYERS)):
        gradient, big, channel_all[l], gain_all[l] = layer_backward(
            plan, gradient, weights[l], saved_all[l], masks
        )
        g_col_rec, g_gates, g_out, g_col_mlp, g_down = (g.astype(BF) for g in big)

        def by_owner(g):
            return g.reshape(tp, seq, -1, g.shape[1]).swapaxes(0, 1).reshape(seq, -1, g.shape[1])

        def shares(g):
            return over_seq(by_owner(g)).reshape(tp, -1, g.shape[1])

        rec = exchange(shares(g_col_rec))
        mlp = exchange(shares(g_col_mlp))

        def columns(parts, at, width):
            return jnp.moveaxis(parts[:, :, at : at + width], 0, 1).reshape(parts.shape[1], -1)

        gates = over_seq(g_gates.reshape(seq, -1, 2 * head))
        outs[l] = [
            columns(rec, 0, head),
            columns(rec, head, head),
            gates[:, :head],
            gates[:, head:],
            over_seq(g_out.reshape(seq, -1, g_out.shape[1])),
            columns(mlp, 0, units),
            columns(mlp, units, units),
            over_seq(g_down.reshape(seq, -1, g_down.shape[1])),
        ]
        outs[l] = [to_owners(plan, g.astype(F32), 0) for g in outs[l]]
    big = [jnp.stack([outs[l][i] for l in range(LAYERS)]) for i in range(8)]

    channel = jnp.stack(channel_all).reshape(LAYERS * 8, seq, head // seq)
    channel = lax.psum_scatter(channel, "seq", scatter_dimension=1, tiled=False)
    channel = to_owners(plan, channel, 1).reshape(LAYERS, 8, -1)
    gains = lax.psum(jnp.stack(gain_all), ("rep", "seq"))
    width = gains.shape[2] // (plan.rep * seq)
    owner = lax.axis_index(("rep", "seq"))
    gains = lax.dynamic_slice_in_dim(gains, owner * width, width, 2)
    return (
        residual.astype(BF),
        gradient,
        gains,
        big[0],
        big[1],
        channel[:, :CONV],
        channel[:, CONV],
        big[2],
        big[3],
        channel[:, CONV + 1 : CONV + 3],
        channel[:, CONV + 3],
        big[4],
        big[5],
        big[6],
        big[7],
    )


def solution(mesh):
    tokens = P(("rep", "seq"), None)
    rows = P(None, "seq", None)
    last3 = P(None, None, "seq")
    last2 = P(None, "seq")
    own_rows = P(None, ("rep", "seq"), None)
    own3 = P(None, None, ("rep", "seq"))
    own2 = P(None, ("rep", "seq"))

    def whole(*args):
        heads = args[9].shape[1] // args[9].shape[2]
        plan = Plan(mesh, heads)
        return jax.shard_map(
            partial(local, plan),
            mesh=mesh,
            in_specs=(
                tokens, tokens, P("rep"), P("rep"), last3, rows, rows, last3, last2, rows, rows,
                last3, last2, rows, rows, rows, rows,
            ),
            out_specs=(
                tokens, tokens, own3, own_rows, own_rows, own3, own2, own_rows, own_rows, own3,
                own2, own_rows, own_rows, own_rows, own_rows,
            ),
            check_vma=False,
        )(*args)

    return whole
```

```python
from functools import partial

import jax
import jax.numpy as jnp
from jax import lax
from jax.experimental import pallas as pl
from jax.experimental.pallas import tpu as pltpu
from jax.sharding import PartitionSpec as P

CONV = 4
LAYERS = 2
EPSILON = 1e-06
BF = jnp.bfloat16
F32 = jnp.float32


def dot(a, b):
    return jnp.dot(a, b, preferred_element_type=F32)


def dot_tn(a, b):
    return lax.dot_general(a, b, (((0,), (0,)), ((), ())), preferred_element_type=F32)


def dot_nt(a, b):
    return lax.dot_general(a, b, (((1,), (1,)), ((), ())), preferred_element_type=F32)


def rms_scale(values, scale_vec):
    return (
        values * lax.rsqrt(jnp.mean(values * values, axis=-1, keepdims=True) + EPSILON) * scale_vec
    )


def gate_terms(pre_rate, pre_admit, conv_value, decay_logit, gate_bias, restart):
    rate_gate = jax.nn.sigmoid(pre_rate + gate_bias[0])
    admit_gate = jax.nn.sigmoid(pre_admit + gate_bias[1])
    log_retain = -8.0 * rate_gate * jax.nn.softplus(-decay_logit)
    retain = jnp.where(restart, 0.0, jnp.exp(log_retain))
    input_scale = jnp.where(restart, 1.0, jnp.sqrt(-jnp.expm1(2.0 * log_retain)))
    return (retain, input_scale * admit_gate * conv_value)


def glu_product(gate_in, value_in):
    return jax.nn.gelu(gate_in, approximate=True) * value_in


class Plan:
    def __init__(self, mesh, heads):
        self.rep = mesh.shape["rep"]
        self.seq = mesh.shape["seq"]
        self.tp = min(heads, self.rep)
        self.dp = self.rep // self.tp
        tp, dp = self.tp, self.dp
        self.tp_groups = None if dp == 1 else [[d * tp + t for t in range(tp)] for d in range(dp)]
        self.dp_groups = [[d * tp + t for d in range(dp)] for t in range(tp)]


def gather_plane(plan, value):
    return lax.all_gather(value, "rep", axis=0, tiled=True, axis_index_groups=plan.tp_groups)


def scatter_plane(plan, value):
    return lax.psum_scatter(
        value, "rep", scatter_dimension=0, tiled=True, axis_index_groups=plan.tp_groups
    )


def owner_chunks(plan, value):
    tp, seq = plan.tp, plan.seq
    pairs = []
    for d in range(plan.dp):
        for j in range(tp):
            for z in range(seq):
                o = tp * z + j
                pairs.append(((d * tp + j) * seq + z, (d * tp + o // seq) * seq + o % seq))
    return lax.ppermute(value, ("rep", "seq"), pairs)


def to_owners(plan, chunk, axis):
    if plan.dp == 1:
        return chunk
    part = lax.psum_scatter(
        chunk, "rep", scatter_dimension=axis, tiled=True, axis_index_groups=plan.dp_groups
    )
    tp, seq, dp = plan.tp, plan.seq, plan.dp
    pairs = [
        ((d * tp + t) * seq + z, (t * seq + z) * dp + d)
        for d in range(dp)
        for t in range(tp)
        for z in range(seq)
    ]
    return lax.ppermute(part, ("rep", "seq"), pairs)


def shifted(plan, value, step):
    pairs = [(z, z + step) for z in range(plan.seq) if 0 <= z + step < plan.seq]
    return lax.ppermute(value, "seq", pairs)


MESH = pl.DeviceIdType.MESH
ANY = pl.BlockSpec(memory_space=pl.ANY)
VM = pl.BlockSpec(memory_space=pltpu.VMEM)
TP = 8


class Net:
    def __init__(self):
        rep = lax.axis_index("rep")
        self.z = lax.axis_index("seq")
        self.t = lax.rem(rep, TP)
        self.base = rep - self.t
        chip = self.t // 2
        self.k = lax.rem(self.t, 2)
        self.b0 = lax.rem(chip, 2)
        self.b1 = chip // 2

    def slot(self, m, s):
        b0 = lax.rem(self.b0 + m % 2, 2)
        b1 = lax.rem(self.b1 + m // 2, 2)
        return (b1 * 2 + b0) * 2 + lax.rem(self.k + s, 2)

    def device(self, m, s):
        return (self.base + self.slot(m, s), self.z)

    def enter(self, extra=()):
        barrier = pltpu.get_barrier_semaphore()
        devices = [self.device(1, 0), self.device(2, 0), self.device(0, 1)] + list(extra)
        for device in devices:
            pl.semaphore_signal(barrier, inc=1, device_id=device, device_id_type=MESH)
        pl.semaphore_wait(barrier, len(devices))


def remote(src, dst, send, recv, device):
    return pltpu.make_async_remote_copy(
        src_ref=src, dst_ref=dst, send_sem=send, recv_sem=recv, device_id=device,
        device_id_type=MESH,
    )


class Gather:
    def __init__(self, net, full, send, recv):
        self.net, self.full, self.send, self.recv = net, full, send, recv
        half = full.shape[1] // 2
        a, b, whole = pl.ds(0, half), pl.ds(half, half), pl.ds(0, 2 * half)
        x, y, sib = net.device(1, 0), net.device(2, 0), net.device(0, 1)
        self.plan = [
            (0, a, x, 1), (0, b, y, 2), (0, b, x, 1), (0, a, y, 2), (2, b, x, 3), (1, a, y, 3),
            (0, whole, sib, 0), (1, whole, sib, 1), (2, whole, sib, 2), (3, whole, sib, 3),
        ]

    def copy(self, i):
        m, rows, to, _ = self.plan[i]
        at = self.full.at[self.net.slot(m, 0), rows]
        return remote(at, at, self.send.at[i], self.recv.at[i], to)

    def arrived(self, i):
        _, rows, to, m = self.plan[i]
        at = self.full.at[self.net.slot(m, 0 if i < 6 else 1), rows]
        remote(at, at, self.send.at[i], self.recv.at[i], to).wait_recv()

    def begin(self):
        for i in (0, 1, 2, 3, 6):
            self.copy(i).start()

    def before(self, n):
        if n == 1:
            self.arrived(6)
        if n == 2:
            self.arrived(0)
            self.copy(5).start()
            self.arrived(1)
            self.copy(4).start()
            self.arrived(2)
            self.copy(7).start()
        if n == 3:
            self.arrived(7)
        if n == 4:
            self.arrived(3)
            self.copy(8).start()
        if n == 5:
            self.arrived(8)
        if n == 6:
            self.arrived(4)
            self.arrived(5)
            self.copy(9).start()
        if n == 7:
            self.arrived(9)

    def finish(self):
        for i in range(10):
            self.copy(i).wait_send()


class Scatter:
    def __init__(self, net, part, near, wide, far, send, recv):
        self.net, self.part, self.near = net, part, near
        self.wide, self.far, self.send, self.recv = wide, far, send, recv
        self.rows = part.shape[2]
        half = self.rows // 2
        a, b, whole = pl.ds(0, half), pl.ds(half, half), pl.ds(0, 2 * half)
        self.a, self.b = a, b
        x, y, sib = net.device(1, 0), net.device(2, 0), net.device(0, 1)
        self.plan = [
            (part.at[1, m], near.at[m], sib) for m in range(4)
        ] + [
            (part.at[0, 3, a], wide.at[0], x),
            (part.at[0, 3, b], wide.at[1], y),
            (part.at[0, 1, a], far.at[0, a], x),
            (part.at[0, 2, b], far.at[1, b], y),
            (part.at[0, 1, b], far.at[0, b], x),
            (part.at[0, 2, a], far.at[1, a], y),
        ]

    def copy(self, i):
        src, dst, to = self.plan[i]
        return remote(src, dst, self.send.at[i], self.recv.at[i], to)

    def add(self, m, start, count, other):
        def some(i, carry):
            at = pl.ds(pl.multiple_of(start + i * 64, 64), 64)
            from_at = pl.ds(pl.multiple_of(i * 64, 64), 64)
            total = self.part[0, m, at].astype(F32) + other[from_at].astype(F32)
            self.part[0, m, at] = total.astype(BF)
            return carry

        lax.fori_loop(0, count // 64, some, 0)

    def after(self, n):
        if n == 1:
            self.copy(0).start()
        if n == 3:
            self.copy(1).start()
        if n == 4:
            self.copy(1).wait_recv()
            self.add(1, 0, self.rows, self.near.at[1])
            self.copy(6).start()
        if n == 5:
            self.copy(2).start()
        if n == 6:
            self.copy(2).wait_recv()
            self.add(2, 0, self.rows, self.near.at[2])
            self.copy(7).start()
        if n == 7:
            self.copy(3).start()

    def corner(self):
        self.copy(3).wait_recv()
        self.add(3, 0, self.rows, self.near.at[3])
        self.copy(4).start()
        self.copy(5).start()

    def edges(self):
        half = self.rows // 2
        self.copy(4).wait_recv()
        self.add(2, 0, half, self.wide.at[0])
        self.copy(9).start()
        self.copy(5).wait_recv()
        self.add(1, half, half, self.wide.at[1])
        self.copy(8).start()
        self.copy(0).wait_recv()

    def finish(self):
        for i in (6, 7, 8, 9):
            self.copy(i).wait_recv()
        for i in range(10):
            self.copy(i).wait_send()

    def total(self, at):
        own = self.part[0, 0, at].astype(F32) + self.near[0, at].astype(F32)
        return own + self.far[0, at].astype(F32) + self.far[1, at].astype(F32)


def plane_scratch(rows, width):
    dma = pltpu.SemaphoreType.DMA
    return [
        pltpu.VMEM((TP, rows, width), BF),
        pltpu.VMEM((2, 4, rows, width), BF),
        pltpu.VMEM((4, rows, width), BF),
        pltpu.VMEM((2, rows // 2, width), BF),
        pltpu.VMEM((2, rows, width), BF),
        dma((10,)), dma((10,)), dma((10,)), dma((10,)),
    ]


def steps(gather, scatter, compute):
    def one(i, carry):
        for n in range(1, 2 * 4):
            @pl.when(i == n)
            def _():
                if gather is not None:
                    gather.before(n)

        compute(i // 2, lax.rem(i, 2))
        for n in range(2 * 4):
            @pl.when(i == n)
            def _():
                if scatter is not None:
                    scatter.after(n)

        return carry

    lax.fori_loop(0, 2 * 4, one, 0)


def end_forward(scatter, residual, gain, out, normed):
    rows, chunk = out.shape[0], 32

    def some(i, carry):
        at = pl.ds(pl.multiple_of(i * chunk, chunk), chunk)
        value = residual[at] + scatter.total(at)
        out[at] = value
        scale = lax.rsqrt(jnp.mean(value * value, axis=-1, keepdims=True) + EPSILON)
        normed[at] = (value * scale * gain[...]).astype(BF)
        return carry

    lax.fori_loop(0, rows // chunk, some, 0)


def end_backward(scatter, upstream, values, gain, grad, grad_low, grad_gain):
    rows, chunk = grad.shape[0], 32
    grad_gain[...] = jnp.zeros_like(grad_gain)

    def some(i, carry):
        at = pl.ds(pl.multiple_of(i * chunk, chunk), chunk)
        value, given = values[at], scatter.total(at)
        scale = lax.rsqrt(jnp.mean(value * value, axis=-1, keepdims=True) + EPSILON)
        scaled = given * gain[...]
        mean = jnp.mean(value * scaled, axis=-1, keepdims=True)
        result = upstream[at] + scale * scaled - value * (scale * scale * scale * mean)
        grad[at] = result
        grad_low[at] = result.astype(BF)
        grad_gain[...] += jnp.sum(given * value * scale, axis=0, keepdims=True)
        return carry

    lax.fori_loop(0, rows // chunk, some, 0)


GELU_A = 0.7978845608028654
GELU_B = 0.044715


def gelu_parts(v):
    square = v * v
    tanh = jnp.tanh(GELU_A * (v + GELU_B * v * square))
    half = 0.5 * (1.0 + tanh)
    slope = half + 0.5 * v * (1.0 - tanh * tanh) * (GELU_A * (1.0 + 3.0 * GELU_B * square))
    return v * half, slope


def mlp_weight_copies(col_ref, down_ref, wg, wu, wd, sem):
    seq, _, rows, _ = col_ref.shape
    copies = []
    for i, w in enumerate((wg, wu)):
        for z in range(seq):
            copies.append(
                pltpu.make_async_copy(
                    col_ref.at[z, i], w.at[pl.ds(z * rows, rows)], sem.at[i * seq + z]
                )
            )
    copies.append(pltpu.make_async_copy(down_ref, wd, sem.at[2 * seq]))
    return copies


def mlp_forward_kernel(
    x_ref, residual_ref, gain_ref, col_ref, down_ref,
    out_ref, normed_ref, full_out, gate_out, value_out,
    full, part, near, wide, far, gs, gr, ss, sr, wg, wu, wd, gate, value, sem,
):
    net = Net()
    gather = Gather(net, full, gs, gr)
    scatter = Scatter(net, part, near, wide, far, ss, sr)
    n = 2 * col_ref.shape[0] + 1
    own = pltpu.make_async_copy(x_ref, full.at[net.t], sem.at[n])
    own.start()
    weights = mlp_weight_copies(col_ref, down_ref, wg, wu, wd, sem)
    for copy in weights:
        copy.start()
    net.enter()
    own.wait()
    gather.begin()
    for copy in weights:
        copy.wait()

    def compute(m, s):
        slot = net.slot(m, s)
        x = full[slot]
        up_gate, up_value = dot(x, wg[...]), dot(x, wu[...])
        gate[slot] = up_gate.astype(BF)
        value[slot] = up_value.astype(BF)
        hidden = glu_product(up_gate, up_value).astype(BF)
        part[s, m] = dot(hidden, wd[...]).astype(BF)

    steps(gather, scatter, compute)
    saves = [
        pltpu.make_async_copy(full, full_out, sem.at[n + 1]),
        pltpu.make_async_copy(gate, gate_out, sem.at[n + 2]),
        pltpu.make_async_copy(value, value_out, sem.at[n + 3]),
    ]
    for copy in saves:
        copy.start()
    scatter.corner()
    scatter.edges()
    scatter.finish()
    end_forward(scatter, residual_ref, gain_ref, out_ref, normed_ref)
    gather.finish()
    for copy in saves:
        copy.wait()


def mlp_forward(x, residual, gain, col, down):
    rows, width = x.shape
    seq, _, part_rows, units = col.shape
    shape = jax.ShapeDtypeStruct
    return pl.pallas_call(
        mlp_forward_kernel,
        in_specs=[ANY, VM, VM, ANY, ANY],
        out_specs=[VM, VM, ANY, ANY, ANY],
        out_shape=[
            shape((rows, width), F32),
            shape((rows, width), BF),
            shape((TP, rows, width), BF),
            shape((TP, rows, units), BF),
            shape((TP, rows, units), BF),
        ],
        scratch_shapes=plane_scratch(rows, width)
        + [
            pltpu.VMEM((width, units), BF),
            pltpu.VMEM((width, units), BF),
            pltpu.VMEM((units, width), BF),
            pltpu.VMEM((TP, rows, units), BF),
            pltpu.VMEM((TP, rows, units), BF),
            pltpu.SemaphoreType.DMA((2 * seq + 5,)),
        ],
        compiler_params=pltpu.CompilerParams(
            collective_id=1, has_side_effects=True, vmem_limit_bytes=58 << 20
        ),
        cost_estimate=pl.CostEstimate(
            flops=60 * 10**9, bytes_accessed=30 << 20, transcendentals=0
        ),
        name="mlp_forward",
    )(x, residual, gain.reshape(1, -1), col, down)


def mlp_backward_kernel(
    g_ref, upstream_ref, values_ref, gain_ref, col_ref, down_ref, x_ref, gate_ref, value_ref,
    grad_ref, low_ref, gain_out, gcol_ref, gdown_ref,
    full, part, near, wide, far, gs, gr, ss, sr, wg, wu, wd, xs, gate, value, hid, sem,
):
    net = Net()
    gather = Gather(net, full, gs, gr)
    scatter = Scatter(net, part, near, wide, far, ss, sr)
    seq = col_ref.shape[0]
    n = 2 * seq + 1
    own = pltpu.make_async_copy(g_ref, full.at[net.t], sem.at[n])
    own.start()
    loads = mlp_weight_copies(col_ref, down_ref, wg, wu, wd, sem) + [
        pltpu.make_async_copy(gate_ref, gate, sem.at[n + 1]),
        pltpu.make_async_copy(value_ref, value, sem.at[n + 2]),
    ]
    late = pltpu.make_async_copy(x_ref, xs, sem.at[n + 3])
    for copy in loads + [late]:
        copy.start()
    net.enter()
    own.wait()
    gather.begin()
    for copy in loads:
        copy.wait()
    rows = full.shape[1]

    def compute(m, s):
        slot = net.slot(m, s)
        at = pl.ds(pl.multiple_of(slot * rows, rows), rows)
        grad_hidden = dot_nt(full[slot], wd[...])
        act, slope = gelu_parts(gate[at].astype(F32))
        up_value = value[at].astype(F32)
        hid[at] = (act * up_value).astype(BF)
        grad_gate = (grad_hidden * up_value * slope).astype(BF)
        grad_value = (grad_hidden * act).astype(BF)
        gate[at] = grad_gate
        value[at] = grad_value
        part[s, m] = (dot_nt(grad_gate, wg[...]) + dot_nt(grad_value, wu[...])).astype(BF)

    steps(gather, scatter, compute)
    late.wait()
    scatter.corner()
    width = full.shape[2]
    own_rows = width // (TP * seq)
    tile = 2 * seq * own_rows

    def columns(j, carry):
        x = xs[:, pl.ds(pl.multiple_of(j * tile, 128), tile)]
        for i, grads in enumerate((gate, value)):
            product = dot_tn(x, grads[...]).astype(BF)
            for r in range(2):
                for z in range(seq):
                    low = (r * seq + z) * own_rows
                    at = pl.ds(pl.multiple_of((2 * j + r) * own_rows, own_rows), own_rows)
                    gcol_ref[z, i, at] = product[low : low + own_rows]
        return carry

    lax.fori_loop(0, TP // 2, columns, 0)
    scatter.edges()

    tokens = full.shape[0] * rows
    third = width // 3

    for j in range(3):
        at = pl.ds(j * third, third)
        gdown_ref[:, at] = dot_tn(hid[...], full[:, :, at].reshape(tokens, third)).astype(BF)
    scatter.finish()
    end_backward(scatter, upstream_ref, values_ref, gain_ref, grad_ref, low_ref, gain_out)
    gather.finish()


def mlp_backward(g, upstream, values, gain, col, down, x, gate, value):
    rows, width = g.shape
    seq, _, part_rows, units = col.shape
    tokens = TP * rows
    shape = jax.ShapeDtypeStruct
    return pl.pallas_call(
        mlp_backward_kernel,
        in_specs=[ANY, VM, VM, VM, ANY, ANY, ANY, ANY, ANY],
        out_specs=[VM, VM, VM, VM, VM],
        out_shape=[
            shape((rows, width), F32),
            shape((rows, width), BF),
            shape((1, width), F32),
            shape((seq, 2, part_rows, units), BF),
            shape((units, width), BF),
        ],
        scratch_shapes=plane_scratch(rows, width)
        + [
            pltpu.VMEM((width, units), BF),
            pltpu.VMEM((width, units), BF),
            pltpu.VMEM((units, width), BF),
            pltpu.VMEM((tokens, width), BF),
            pltpu.VMEM((tokens, units), BF),
            pltpu.VMEM((tokens, units), BF),
            pltpu.VMEM((tokens, units), BF),
            pltpu.SemaphoreType.DMA((2 * seq + 5,)),
        ],
        compiler_params=pltpu.CompilerParams(
            collective_id=2, has_side_effects=True, vmem_limit_bytes=60 << 20
        ),
        cost_estimate=pl.CostEstimate(
            flops=70 * 10**9, bytes_accessed=30 << 20, transcendentals=0
        ),
        name="mlp_backward",
    )(
        g, upstream, values, gain.reshape(1, -1), col, down, x.reshape(tokens, width),
        gate.reshape(tokens, units), value.reshape(tokens, units),
    )


def scan_body(reverse, rows, slots, a_ref, b_ref, h_ref, q_ref):
    width = a_ref.shape[1]

    def step(i, carry):
        state, decay = carry
        p = rows - 1 - i if reverse else i
        at = pl.ds(p, slots, stride=rows)
        a = a_ref[at, :]
        state = a * state + b_ref[at, :]
        decay = a * decay
        h_ref[at, :] = state
        q_ref[at, :] = decay
        return state, decay

    lax.fori_loop(
        0,
        rows,
        step,
        (jnp.zeros((slots, width), F32), jnp.ones((slots, width), F32)),
        unroll=8,
    )


def local_scan(a, b, slots, reverse):
    rows = a.shape[0] // slots
    width = 128
    spec = pl.BlockSpec((a.shape[0], width), lambda i: (0, i))
    shape = jax.ShapeDtypeStruct(a.shape, F32)
    return pl.pallas_call(
        partial(scan_body, reverse, rows, slots),
        grid=(a.shape[1] // width,),
        in_specs=[spec, spec],
        out_specs=[spec, spec],
        out_shape=[shape, shape],
        compiler_params=pltpu.CompilerParams(vmem_limit_bytes=40 << 20),
        cost_estimate=pl.CostEstimate(flops=0, bytes_accessed=16 * a.size, transcendentals=0),
    )(a, b)


def carried(plan, decay, state, reverse):
    ends = lax.all_gather(jnp.stack([decay, state]), "seq")
    place = lax.axis_index("seq")
    carry = jnp.zeros_like(state)
    order = range(plan.seq)
    for z in reversed(order) if reverse else order:
        ahead = z > place if reverse else z < place
        carry = jnp.where(ahead, ends[z, 0] * carry + ends[z, 1], carry)
    return carry


def masks_of(plan, lengths, offsets, rows):
    start = lax.axis_index("seq") * rows
    extra = CONV - 1
    positions = start + jnp.arange(rows + 2 * extra, dtype=jnp.int32) - extra
    inside = (positions >= offsets[:, None]) & (positions < (offsets + lengths)[:, None])
    core = inside[:, extra : extra + rows]
    restart = (positions[extra : extra + rows] == 0)[None] | (core != inside[:, extra - 1 : extra - 1 + rows])
    fwd = [
        (core == inside[:, extra - j : extra - j + rows]).astype(F32)[..., None]
        for j in range(1, CONV)
    ]
    back = [
        (core == inside[:, extra + j : extra + j + rows]).astype(F32)[..., None]
        for j in range(1, CONV)
    ]
    return restart.reshape(-1, 1), fwd, back


def layer_forward(plan, residual, normed, w, next_gain, masks):
    restart, same_fwd, _ = masks
    slots, rows = plan.tp, residual.shape[0]
    head = w["rate"].shape[0]
    x = gather_plane(plan, normed)
    both = dot(x, w["col_rec"])
    branch, stream = both[:, :head], both[:, head:]
    stream3 = stream.reshape(slots, rows, head)
    before = shifted(plan, stream3[:, rows - (CONV - 1) :], 1)
    widened = jnp.concatenate([before, stream3], 1)
    taps = w["conv"]
    mixed = w["bias"] + taps[0] * stream3
    for j in range(1, CONV):
        low = CONV - 1 - j
        mixed = mixed + taps[j] * widened[:, low : low + rows] * same_fwd[j - 1]
    conv_low = mixed.astype(BF).reshape(slots * rows, head)
    pre_rate = dot(conv_low, w["rate"])
    pre_admit = dot(conv_low, w["admit"])
    retain, inflow = gate_terms(
        pre_rate, pre_admit, conv_low.astype(F32), w["decay"], w["gbias"], restart
    )
    states, running = local_scan(retain, inflow, slots, False)
    carry = carried(
        plan,
        running.reshape(slots, rows, head)[:, -1],
        states.reshape(slots, rows, head)[:, -1],
        False,
    )
    states = (
        states.reshape(slots, rows, head) + running.reshape(slots, rows, head) * carry[:, None]
    ).reshape(slots * rows, head)
    joined = glu_product(branch, states).astype(BF)
    middle = residual + scatter_plane(plan, dot(joined, w["out"]).astype(BF)).astype(F32)
    normed_two = rms_scale(middle, w["gain"][1]).astype(BF)
    output, next_normed, x_two, gate, value = mlp_forward(
        normed_two, middle, next_gain, w["col_mlp"], w["down"]
    )
    saved = (
        residual, x, branch, widened, conv_low, pre_rate, pre_admit, retain, states, carry,
        joined, middle, x_two, gate, value,
    )
    return output, next_normed, saved


def layer_backward(plan, upstream, upstream_low, w, saved, masks):
    (
        residual, x, branch, widened, conv_low, pre_rate, pre_admit, retain, states, carry,
        joined, middle, x_two, gate, value,
    ) = saved
    restart, same_fwd, same_back = masks
    slots, rows = plan.tp, residual.shape[0]
    seq = plan.seq
    head = w["rate"].shape[0]
    grad_middle, mid_low, grad_gain_two, g_col_mlp, g_down = mlp_backward(
        upstream_low, upstream, middle, w["gain"][1], w["col_mlp"], w["down"], x_two, gate, value
    )
    mid_low = gather_plane(plan, mid_low)
    g_out = dot_tn(joined, mid_low)
    grad_joined = dot_nt(mid_low, w["out"])
    _, mix_pull = jax.vjp(glu_product, branch, states)
    branch_part, grad_direct = mix_pull(grad_joined)
    retain3 = retain.reshape(slots, rows, head)
    retain_next = jnp.concatenate([retain3[:, 1:], jnp.ones_like(retain3[:, :1])], 1)
    local, suffix = local_scan(retain_next.reshape(-1, head), grad_direct, slots, True)
    local3, suffix3 = local.reshape(retain3.shape), suffix.reshape(retain3.shape)
    first = retain3[:, 0]
    incoming = carried(plan, first * suffix3[:, 0], first * local3[:, 0], True)
    grad_states3 = local3 + suffix3 * incoming[:, None]
    grad_states = grad_states3.reshape(-1, head)
    states3 = states.reshape(retain3.shape)
    previous = jnp.concatenate([carry[:, None], states3[:, :-1]], 1).reshape(-1, head)
    _, gate_pull = jax.vjp(
        partial(gate_terms, restart=restart),
        pre_rate, pre_admit, conv_low.astype(F32), w["decay"], w["gbias"],
    )
    rate_part, admit_part, grad_conv, grad_decay, grad_gbias = gate_pull(
        (grad_states * previous, grad_states)
    )
    grad_pre = jnp.concatenate([rate_part.astype(BF), admit_part.astype(BF)], 1)
    g_gates = dot_tn(conv_low, grad_pre)
    grad_mixed = (
        grad_conv + dot_nt(grad_pre[:, :head], w["rate"]) + dot_nt(grad_pre[:, head:], w["admit"])
    ).reshape(slots, rows, head)
    after = shifted(plan, grad_mixed[:, : CONV - 1], -1)
    wide_grad = jnp.concatenate([grad_mixed, after], 1)
    taps = w["conv"]
    tap_rows = [jnp.sum(grad_mixed * widened[:, CONV - 1 :], axis=(0, 1))]
    grad_stream = taps[0] * grad_mixed
    for j in range(1, CONV):
        low = CONV - 1 - j
        tap_rows.append(
            jnp.sum(grad_mixed * widened[:, low : low + rows] * same_fwd[j - 1], axis=(0, 1))
        )
        grad_stream = grad_stream + taps[j] * wide_grad[:, j : j + rows] * same_back[j - 1]
    grad_bias = jnp.sum(grad_mixed, axis=(0, 1))
    grad_both = jnp.concatenate(
        [branch_part.astype(BF), grad_stream.astype(BF).reshape(-1, head)], 1
    )
    grad_normed = scatter_plane(plan, dot_nt(grad_both, w["col_rec"]).astype(BF)).astype(F32)
    g_col_rec = dot_tn(x, grad_both)
    _, pull_one = jax.vjp(rms_scale, residual, w["gain"][0])
    part, grad_gain_one = pull_one(grad_normed)
    channel = jnp.stack(tap_rows + [grad_bias, grad_gbias[0], grad_gbias[1], grad_decay], 0)
    gains = jnp.stack([grad_gain_one, grad_gain_two[0]], 0)
    return grad_middle + part, (g_col_rec, g_gates, g_out, g_col_mlp, g_down), channel, gains


def local(plan, *args):
    (
        block_input, cotangent, lengths, offsets, norm_gains, branch_proj, stream_proj, conv_kernel,
        conv_bias, rate_proj, admit_proj, gate_bias, decay_logit, out_proj, mlp_gate, mlp_up,
        mlp_down,
    ) = args
    tp, dp, seq = plan.tp, plan.dp, plan.seq
    t = lax.axis_index("rep") % tp
    z = lax.axis_index("seq")
    rows = block_input.shape[0]
    head = branch_proj.shape[2] // tp
    units = mlp_gate.shape[2] // tp

    channels = conv_kernel.shape[2]
    small = jnp.concatenate(
        [
            conv_kernel,
            conv_bias[:, None],
            gate_bias,
            decay_logit[:, None],
        ],
        1,
    )
    packed = jnp.concatenate([small.reshape(-1), norm_gains.reshape(-1)])
    packed = lax.all_gather(packed, "seq")
    small = packed[:, : small.size].reshape(seq, LAYERS, 8, channels)
    small = jnp.moveaxis(small, 0, 2).reshape(LAYERS, 8, seq * channels)
    small = lax.dynamic_slice_in_dim(small, t * head, head, 2).astype(F32)
    gains = packed[:, LAYERS * 8 * channels :].reshape(seq, LAYERS, 2, -1)
    gains = jnp.moveaxis(gains, 0, 2).reshape(LAYERS, 2, -1).astype(F32)
    layout = gather_plane(plan, jnp.stack([lengths, offsets], 1))
    masks = masks_of(plan, layout[:, 0], layout[:, 1], rows)

    def col(weight, layer, width):
        return lax.dynamic_slice_in_dim(weight[layer], t * width, width, 1)

    def chunk(weight, layer):
        size = weight.shape[1] // tp
        return lax.dynamic_slice_in_dim(weight[layer], t * size, size, 0)

    weights = []
    for l in range(LAYERS):
        col_rec = jnp.concatenate([col(branch_proj, l, head), col(stream_proj, l, head)], 1)
        col_mlp = jnp.stack([col(mlp_gate, l, units), col(mlp_up, l, units)], 0)
        wide = owner_chunks(plan, jnp.concatenate([chunk(out_proj, l), chunk(mlp_down, l)], 0))
        out_rows = out_proj.shape[1] // tp
        gates = owner_chunks(plan, jnp.concatenate([chunk(rate_proj, l), chunk(admit_proj, l)], 1))
        gates = lax.all_gather(gates, "seq", axis=0, tiled=True)
        weights.append(
            dict(
                gain=gains[l],
                conv=small[l, :CONV],
                bias=small[l, CONV],
                gbias=small[l, CONV + 1 : CONV + 3],
                decay=small[l, CONV + 3],
                col_rec=lax.all_gather(col_rec, "seq", axis=0, tiled=True),
                rate=gates[:, :head],
                admit=gates[:, head:],
                out=lax.all_gather(wide[:out_rows], "seq", axis=0, tiled=True),
                col_mlp=lax.all_gather(col_mlp, "seq"),
                down=lax.all_gather(wide[out_rows:], "seq", axis=0, tiled=True),
            )
        )

    residual = block_input.astype(F32)
    normed = rms_scale(residual, gains[0, 0]).astype(BF)
    saved_all = []
    for l in range(LAYERS):
        next_gain = gains[(l + 1) % LAYERS, 0]
        residual, normed, saved = layer_forward(
            plan, residual, normed, weights[l], next_gain, masks
        )
        saved_all.append(saved)
    positions = z * rows + jnp.arange(rows, dtype=jnp.int32)
    inside = (positions >= offsets[0]) & (positions < offsets[0] + lengths[0])
    gradient = cotangent.astype(F32) * inside.astype(F32)[:, None]

    outs = [None] * LAYERS
    channel_all, gain_all = [None] * LAYERS, [None] * LAYERS

    def over_seq(value):
        return lax.psum_scatter(value, "seq", scatter_dimension=0, tiled=False)

    def exchange(share):
        return lax.all_to_all(
            share, "rep", split_axis=0, concat_axis=0, axis_index_groups=plan.tp_groups
        )

    for l in reversed(range(LAYERS)):
        gradient, big, channel_all[l], gain_all[l] = layer_backward(
            plan, gradient, gradient.astype(BF), weights[l], saved_all[l], masks
        )
        g_col_rec, g_gates, g_out, g_col_mlp, g_down = (g.astype(BF) for g in big)

        def by_owner(g):
            return g.reshape(tp, seq, -1, g.shape[1]).swapaxes(0, 1).reshape(seq, -1, g.shape[1])

        rec = exchange(over_seq(by_owner(g_col_rec)).reshape(tp, -1, 2 * head))
        mlp = over_seq(g_col_mlp.reshape(seq, -1, units)).reshape(2, tp, -1, units)
        mlp = exchange(mlp.swapaxes(0, 1).reshape(tp, -1, units)).reshape(tp, 2, -1, units)

        def columns(parts):
            return jnp.moveaxis(parts, 0, 1).reshape(parts.shape[1], -1)

        gates = over_seq(g_gates.reshape(seq, -1, 2 * head))
        outs[l] = [
            columns(rec[:, :, :head]),
            columns(rec[:, :, head:]),
            gates[:, :head],
            gates[:, head:],
            over_seq(g_out.reshape(seq, -1, g_out.shape[1])),
            columns(mlp[:, 0]),
            columns(mlp[:, 1]),
            over_seq(g_down.reshape(seq, -1, g_down.shape[1])),
        ]
        outs[l] = [to_owners(plan, g.astype(F32), 0) for g in outs[l]]
    big = [jnp.stack([outs[l][i] for l in range(LAYERS)]) for i in range(8)]

    channel = jnp.stack(channel_all).reshape(LAYERS * 8, seq, head // seq)
    channel = lax.psum_scatter(channel, "seq", scatter_dimension=1, tiled=False)
    channel = to_owners(plan, channel, 1).reshape(LAYERS, 8, -1)
    gains = lax.psum(jnp.stack(gain_all), ("rep", "seq"))
    width = gains.shape[2] // (plan.rep * seq)
    owner = lax.axis_index(("rep", "seq"))
    gains = lax.dynamic_slice_in_dim(gains, owner * width, width, 2)
    return (
        residual.astype(BF),
        gradient,
        gains,
        big[0],
        big[1],
        channel[:, :CONV],
        channel[:, CONV],
        big[2],
        big[3],
        channel[:, CONV + 1 : CONV + 3],
        channel[:, CONV + 3],
        big[4],
        big[5],
        big[6],
        big[7],
    )


def solution(mesh):
    tokens = P(("rep", "seq"), None)
    rows = P(None, "seq", None)
    last3 = P(None, None, "seq")
    last2 = P(None, "seq")
    own_rows = P(None, ("rep", "seq"), None)
    own3 = P(None, None, ("rep", "seq"))
    own2 = P(None, ("rep", "seq"))

    def whole(*args):
        heads = args[9].shape[1] // args[9].shape[2]
        plan = Plan(mesh, heads)
        return jax.shard_map(
            partial(local, plan),
            mesh=mesh,
            in_specs=(
                tokens, tokens, P("rep"), P("rep"), last3, rows, rows, last3, last2, rows, rows,
                last3, last2, rows, rows, rows, rows,
            ),
            out_specs=(
                tokens, tokens, own3, own_rows, own_rows, own3, own2, own_rows, own_rows, own3,
                own2, own_rows, own_rows, own_rows, own_rows,
            ),
            check_vma=False,
        )(*args)

    return whole
```

```python
from functools import partial

import jax
import jax.numpy as jnp
from jax import lax
from jax.experimental import pallas as pl
from jax.experimental.pallas import tpu as pltpu
from jax.sharding import PartitionSpec as P

CONV = 4
LAYERS = 2
EPSILON = 1e-06
BF = jnp.bfloat16
F32 = jnp.float32


def dot(a, b):
    return jnp.dot(a, b, preferred_element_type=F32)


def dot_tn(a, b):
    return lax.dot_general(a, b, (((0,), (0,)), ((), ())), preferred_element_type=F32)


def dot_nt(a, b):
    return lax.dot_general(a, b, (((1,), (1,)), ((), ())), preferred_element_type=F32)


def glu_product(gate_in, value_in):
    return jax.nn.gelu(gate_in, approximate=True) * value_in


class Plan:
    def __init__(self, mesh, heads):
        self.rep = mesh.shape["rep"]
        self.seq = mesh.shape["seq"]
        self.tp = min(heads, self.rep)
        self.dp = self.rep // self.tp
        tp, dp = self.tp, self.dp
        self.tp_groups = None if dp == 1 else [[d * tp + t for t in range(tp)] for d in range(dp)]
        self.dp_groups = [[d * tp + t for d in range(dp)] for t in range(tp)]


def owner_chunks(plan, value):
    tp, seq = plan.tp, plan.seq
    pairs = []
    for d in range(plan.dp):
        for j in range(tp):
            for z in range(seq):
                o = tp * z + j
                pairs.append(((d * tp + j) * seq + z, (d * tp + o // seq) * seq + o % seq))
    return lax.ppermute(value, ("rep", "seq"), pairs)


def to_owners(plan, chunk, axis):
    if plan.dp == 1:
        return chunk
    part = lax.psum_scatter(
        chunk, "rep", scatter_dimension=axis, tiled=True, axis_index_groups=plan.dp_groups
    )
    tp, seq, dp = plan.tp, plan.seq, plan.dp
    pairs = [
        ((d * tp + t) * seq + z, (t * seq + z) * dp + d)
        for d in range(dp)
        for t in range(tp)
        for z in range(seq)
    ]
    return lax.ppermute(part, ("rep", "seq"), pairs)


MESH = pl.DeviceIdType.MESH
ANY = pl.BlockSpec(memory_space=pl.ANY)
VM = pl.BlockSpec(memory_space=pltpu.VMEM)
TP = 8
LATER = 3


class Net:
    def __init__(self):
        rep = lax.axis_index("rep")
        self.z = lax.axis_index("seq")
        self.t = lax.rem(rep, TP)
        self.base = rep - self.t
        chip = self.t // 2
        self.k = lax.rem(self.t, 2)
        self.b0 = lax.rem(chip, 2)
        self.b1 = chip // 2

    def slot(self, m, s):
        b0 = lax.rem(self.b0 + m % 2, 2)
        b1 = lax.rem(self.b1 + m // 2, 2)
        return (b1 * 2 + b0) * 2 + lax.rem(self.k + s, 2)

    def device(self, m, s):
        return (self.base + self.slot(m, s), self.z)

    def enter(self, extra=()):
        barrier = pltpu.get_barrier_semaphore()
        devices = [self.device(1, 0), self.device(2, 0), self.device(0, 1)] + list(extra)
        for device in devices:
            pl.semaphore_signal(barrier, inc=1, device_id=device, device_id_type=MESH)
        pl.semaphore_wait(barrier, len(devices))


def remote(src, dst, send, recv, device):
    return pltpu.make_async_remote_copy(
        src_ref=src, dst_ref=dst, send_sem=send, recv_sem=recv, device_id=device,
        device_id_type=MESH,
    )


class Gather:
    def __init__(self, net, full, send, recv):
        self.net, self.full, self.send, self.recv = net, full, send, recv
        half = full.shape[1] // 2
        a, b, whole = pl.ds(0, half), pl.ds(half, half), pl.ds(0, 2 * half)
        x, y, sib = net.device(1, 0), net.device(2, 0), net.device(0, 1)
        self.plan = [
            (0, a, x, 1), (0, b, y, 2), (0, b, x, 1), (0, a, y, 2), (2, b, x, 3), (1, a, y, 3),
            (0, whole, sib, 0), (1, whole, sib, 1), (2, whole, sib, 2), (3, whole, sib, 3),
        ]

    def copy(self, i):
        m, rows, to, _ = self.plan[i]
        at = self.full.at[self.net.slot(m, 0), rows]
        return remote(at, at, self.send.at[i], self.recv.at[i], to)

    def arrived(self, i):
        _, rows, to, m = self.plan[i]
        at = self.full.at[self.net.slot(m, 0 if i < 6 else 1), rows]
        remote(at, at, self.send.at[i], self.recv.at[i], to).wait_recv()

    def begin(self):
        for i in (0, 1, 2, 3, 6):
            self.copy(i).start()

    def before(self, n):
        if n == 1:
            self.arrived(6)
        if n == 2:
            self.arrived(0)
            self.copy(5).start()
            self.arrived(1)
            self.copy(4).start()
            self.arrived(2)
            self.copy(7).start()
        if n == 3:
            self.arrived(7)
        if n == 4:
            self.arrived(3)
            self.copy(8).start()
        if n == 5:
            self.arrived(8)
        if n == 6:
            self.arrived(4)
            self.arrived(5)
            self.copy(9).start()
        if n == 7:
            self.arrived(9)

    def finish(self):
        for i in range(10):
            self.copy(i).wait_send()


class Scatter:
    def __init__(self, net, part, near, wide, far, send, recv):
        self.net, self.part, self.near = net, part, near
        self.wide, self.far, self.send, self.recv = wide, far, send, recv
        self.rows = part.shape[2]
        half = self.rows // 2
        a, b, whole = pl.ds(0, half), pl.ds(half, half), pl.ds(0, 2 * half)
        self.a, self.b = a, b
        x, y, sib = net.device(1, 0), net.device(2, 0), net.device(0, 1)
        self.plan = [
            (part.at[1, m], near.at[m], sib) for m in range(4)
        ] + [
            (part.at[0, 3, a], wide.at[0], x),
            (part.at[0, 3, b], wide.at[1], y),
            (part.at[0, 1, a], far.at[0, a], x),
            (part.at[0, 2, b], far.at[1, b], y),
            (part.at[0, 1, b], far.at[0, b], x),
            (part.at[0, 2, a], far.at[1, a], y),
        ]

    def copy(self, i):
        src, dst, to = self.plan[i]
        return remote(src, dst, self.send.at[i], self.recv.at[i], to)

    def add(self, m, start, count, other):
        def some(i, carry):
            at = pl.ds(pl.multiple_of(start + i * 64, 64), 64)
            from_at = pl.ds(pl.multiple_of(i * 64, 64), 64)
            total = self.part[0, m, at].astype(F32) + other[from_at].astype(F32)
            self.part[0, m, at] = total.astype(BF)
            return carry

        lax.fori_loop(0, count // 64, some, 0)

    def after(self, n):
        if n == 1:
            self.copy(0).start()
        if n == 3:
            self.copy(1).start()
        if n == 4:
            self.copy(1).wait_recv()
            self.add(1, 0, self.rows, self.near.at[1])
            self.copy(6).start()
        if n == 5:
            self.copy(2).start()
        if n == 6:
            self.copy(2).wait_recv()
            self.add(2, 0, self.rows, self.near.at[2])
            self.copy(7).start()
        if n == 7:
            self.copy(3).start()

    def corner(self):
        self.copy(3).wait_recv()
        self.add(3, 0, self.rows, self.near.at[3])
        self.copy(4).start()
        self.copy(5).start()

    def edges(self):
        half = self.rows // 2
        self.copy(4).wait_recv()
        self.add(2, 0, half, self.wide.at[0])
        self.copy(9).start()
        self.copy(5).wait_recv()
        self.add(1, half, half, self.wide.at[1])
        self.copy(8).start()
        self.copy(0).wait_recv()

    def finish(self):
        for i in (6, 7, 8, 9):
            self.copy(i).wait_recv()
        for i in range(10):
            self.copy(i).wait_send()

    def total(self, at):
        own = self.part[0, 0, at].astype(F32) + self.near[0, at].astype(F32)
        return own + self.far[0, at].astype(F32) + self.far[1, at].astype(F32)


def plane_scratch(rows, width):
    dma = pltpu.SemaphoreType.DMA
    return [
        pltpu.VMEM((TP, rows, width), BF),
        pltpu.VMEM((2, 4, rows, width), BF),
        pltpu.VMEM((4, rows, width), BF),
        pltpu.VMEM((2, rows // 2, width), BF),
        pltpu.VMEM((2, rows, width), BF),
        dma((10,)), dma((10,)), dma((10,)), dma((10,)),
    ]


def steps(gather, scatter, compute):
    def one(i, carry):
        for n in range(1, 2 * 4):
            @pl.when(i == n)
            def _():
                if gather is not None:
                    gather.before(n)

        compute(i // 2, lax.rem(i, 2))
        for n in range(2 * 4):
            @pl.when(i == n)
            def _():
                if scatter is not None:
                    scatter.after(n)

        return carry

    lax.fori_loop(0, 2 * 4, one, 0)


def end_forward(scatter, residual, gain, out, normed):
    rows, chunk = out.shape[0], 32

    def some(i, carry):
        at = pl.ds(pl.multiple_of(i * chunk, chunk), chunk)
        value = residual[at] + scatter.total(at)
        out[at] = value
        scale = lax.rsqrt(jnp.mean(value * value, axis=-1, keepdims=True) + EPSILON)
        normed[at] = (value * scale * gain[...]).astype(BF)
        return carry

    lax.fori_loop(0, rows // chunk, some, 0)


def end_backward(scatter, upstream, values, gain, grad, grad_low, grad_gain):
    rows, chunk = grad.shape[0], 32
    grad_gain[...] = jnp.zeros_like(grad_gain)

    def some(i, carry):
        at = pl.ds(pl.multiple_of(i * chunk, chunk), chunk)
        value, given = values[at], scatter.total(at)
        scale = lax.rsqrt(jnp.mean(value * value, axis=-1, keepdims=True) + EPSILON)
        scaled = given * gain[...]
        mean = jnp.mean(value * scaled, axis=-1, keepdims=True)
        result = upstream[at] + scale * scaled - value * (scale * scale * scale * mean)
        grad[at] = result
        grad_low[at] = result.astype(BF)
        grad_gain[...] += jnp.sum(given * value * scale, axis=0, keepdims=True)
        return carry

    lax.fori_loop(0, rows // chunk, some, 0)


GELU_A = 0.7978845608028654
GELU_B = 0.044715


def gelu_parts(v):
    square = v * v
    tanh = jnp.tanh(GELU_A * (v + GELU_B * v * square))
    half = 0.5 * (1.0 + tanh)
    slope = half + 0.5 * v * (1.0 - tanh * tanh) * (GELU_A * (1.0 + 3.0 * GELU_B * square))
    return v * half, slope


def copy_list(pairs, sem, first):
    return [
        pltpu.make_async_copy(src, dst, sem.at[first + n]) for n, (src, dst) in enumerate(pairs)
    ]


def unpack_rec(pack, col, wout, gates, sem, first):
    seq, both = pack.shape[0], pack.shape[2]
    rows, part = col.shape[0] // seq, gates.shape[0] // seq
    pairs = []
    for z in range(seq):
        pairs.append((pack.at[z, pl.ds(0, rows)], col.at[pl.ds(z * rows, rows)]))
        own = pl.ds(z * part, part)
        for j in range(3):
            pairs.append(
                (pack.at[z, pl.ds(rows + j * part, part)], wout.at[own, pl.ds(j * both, both)])
            )
        pairs.append((pack.at[z, pl.ds(rows + 3 * part, part)], gates.at[own]))
    return copy_list(pairs, sem, first)


def mlp_split(width, twice):
    rest = width - twice
    return rest, twice // rest


def unpack_mlp(pack, col, down, sem, first):
    seq, twice = pack.shape[0], pack.shape[2]
    rows, part = col.shape[0] // seq, down.shape[0] // seq
    rest, blocks = mlp_split(down.shape[1], twice)
    low = part // blocks
    pairs = []
    for z in range(seq):
        pairs.append((pack.at[z, pl.ds(0, rows)], col.at[pl.ds(z * rows, rows)]))
        pairs.append(
            (pack.at[z, pl.ds(rows, part)], down.at[pl.ds(z * part, part), pl.ds(0, twice)])
        )
        for n in range(blocks):
            pairs.append(
                (
                    pack.at[z, pl.ds(rows + part, low), pl.ds(n * rest, rest)],
                    down.at[pl.ds(z * part + n * low, low), pl.ds(twice, rest)],
                )
            )
    return copy_list(pairs, sem, first)


def mlp_forward_kernel(
    x_ref, residual_ref, gain_ref, pack_ref,
    out_ref, normed_ref, full_out, up_out,
    full, part, near, wide, far, gs, gr, ss, sr, col, wd, ups, sem,
):
    net = Net()
    gather = Gather(net, full, gs, gr)
    scatter = Scatter(net, part, near, wide, far, ss, sr)
    n = 5 * pack_ref.shape[0]
    own = pltpu.make_async_copy(x_ref, full.at[net.t], sem.at[n])
    own.start()
    weights = unpack_mlp(pack_ref, col, wd, sem, 0)
    for copy in weights:
        copy.start()
    net.enter()
    own.wait()
    gather.begin()
    for copy in weights:
        copy.wait()

    units = wd.shape[0]

    def compute(m, s):
        slot = net.slot(m, s)
        x = full[slot]
        up = dot(x, col[...])
        ups[slot] = up.astype(BF)
        hidden = glu_product(up[:, :units], up[:, units:]).astype(BF)
        part[s, m] = dot(hidden, wd[...]).astype(BF)

    steps(gather, scatter, compute)
    saves = [
        pltpu.make_async_copy(full, full_out, sem.at[n + 1]),
        pltpu.make_async_copy(ups, up_out, sem.at[n + 2]),
    ]
    for copy in saves:
        copy.start()
    scatter.corner()
    scatter.edges()
    scatter.finish()
    end_forward(scatter, residual_ref, gain_ref, out_ref, normed_ref)
    gather.finish()
    for copy in saves:
        copy.wait()


def mlp_forward(x, residual, gain, pack):
    rows, width = x.shape
    seq, _, twice = pack.shape
    shape = jax.ShapeDtypeStruct
    return pl.pallas_call(
        mlp_forward_kernel,
        in_specs=[ANY, VM, VM, ANY],
        out_specs=[VM, VM, ANY, ANY],
        out_shape=[
            shape((rows, width), F32),
            shape((rows, width), BF),
            shape((TP, rows, width), BF),
            shape((TP, rows, twice), BF),
        ],
        scratch_shapes=plane_scratch(rows, width)
        + [
            pltpu.VMEM((width, twice), BF),
            pltpu.VMEM((twice // 2, width), BF),
            pltpu.VMEM((TP, rows, twice), BF),
            pltpu.SemaphoreType.DMA((5 * seq + 4,)),
        ],
        compiler_params=pltpu.CompilerParams(
            collective_id=1, has_side_effects=True, vmem_limit_bytes=58 << 20
        ),
        cost_estimate=pl.CostEstimate(
            flops=60 * 10**9, bytes_accessed=30 << 20, transcendentals=0
        ),
        name="mlp_forward",
    )(x, residual, gain.reshape(1, -1), pack)


def mlp_backward_kernel(
    g_ref, upstream_ref, values_ref, gain_ref, pack_ref, x_ref, up_ref,
    grad_ref, low_ref, gain_out, gcol_ref,
    full, part, near, wide, far, gs, gr, ss, sr, col, wd, xs, ups, hid, sem,
):
    net = Net()
    gather = Gather(net, full, gs, gr)
    scatter = Scatter(net, part, near, wide, far, ss, sr)
    seq = pack_ref.shape[0]
    n = 5 * seq
    own = pltpu.make_async_copy(g_ref, full.at[net.t], sem.at[n])
    own.start()
    loads = unpack_mlp(pack_ref, col, wd, sem, 0) + [
        pltpu.make_async_copy(up_ref, ups, sem.at[n + 1]),
    ]
    late = pltpu.make_async_copy(x_ref, xs, sem.at[n + 3])
    for copy in loads + [late]:
        copy.start()
    net.enter()
    own.wait()
    gather.begin()
    for copy in loads:
        copy.wait()
    rows, units = full.shape[1], wd.shape[0]

    def compute(m, s):
        slot = net.slot(m, s)
        at = pl.ds(pl.multiple_of(slot * rows, rows), rows)
        grad_hidden = dot_nt(full[slot], wd[...])
        up = ups[at].astype(F32)
        act, slope = gelu_parts(up[:, :units])
        up_value = up[:, units:]
        hid[at] = (act * up_value).astype(BF)
        grads = jnp.concatenate([grad_hidden * up_value * slope, grad_hidden * act], 1).astype(BF)
        ups[at] = grads
        part[s, m] = dot_nt(grads, col[...]).astype(BF)

    steps(gather, scatter, compute)
    late.wait()
    scatter.corner()
    width = full.shape[2]
    own_rows = width // (TP * seq)
    tile = 2 * seq * own_rows
    base = width // seq

    def columns(j, carry):
        x = xs[:, pl.ds(pl.multiple_of(j * tile, 128), tile)]
        product = dot_tn(x, ups[...]).astype(BF)
        for r in range(2):
            for z in range(seq):
                low = (r * seq + z) * own_rows
                at = pl.ds(pl.multiple_of((2 * j + r) * own_rows, own_rows), own_rows)
                gcol_ref[z, at] = product[low : low + own_rows]
        return carry

    lax.fori_loop(0, TP // 2, columns, 0)
    scatter.edges()

    tokens = full.shape[0] * rows
    part_units = units // seq
    rest, blocks = mlp_split(width, 2 * units)
    low = part_units // blocks
    hidden = hid[...]
    for first in range(0, width, width // 2):
        at = pl.ds(first, width // 2)
        product = dot_tn(hidden, full[:, :, at].reshape(tokens, width // 2)).astype(BF)
        beside = min(2 * units - first, width // 2)
        for z in range(seq):
            own = product[z * part_units : (z + 1) * part_units]
            gcol_ref[z, base : base + part_units, first : first + beside] = own[:, :beside]
            if beside < width // 2:
                for n in range(blocks):
                    gcol_ref[z, base + part_units :, n * rest : (n + 1) * rest] = own[
                        n * low : (n + 1) * low, beside:
                    ]
    scatter.finish()
    end_backward(scatter, upstream_ref, values_ref, gain_ref, grad_ref, low_ref, gain_out)
    gather.finish()


def mlp_backward(g, upstream, values, gain, pack, x, up):
    rows, width = g.shape
    seq, _, twice = pack.shape
    tokens = TP * rows
    shape = jax.ShapeDtypeStruct
    return pl.pallas_call(
        mlp_backward_kernel,
        in_specs=[ANY, VM, VM, VM, ANY, ANY, ANY],
        out_specs=[VM, VM, VM, VM],
        out_shape=[
            shape((rows, width), F32),
            shape((rows, width), BF),
            shape((1, width), F32),
            shape(pack.shape, BF),
        ],
        scratch_shapes=plane_scratch(rows, width)
        + [
            pltpu.VMEM((width, twice), BF),
            pltpu.VMEM((twice // 2, width), BF),
            pltpu.VMEM((tokens, width), BF),
            pltpu.VMEM((tokens, twice), BF),
            pltpu.VMEM((tokens, twice // 2), BF),
            pltpu.SemaphoreType.DMA((5 * seq + 4,)),
        ],
        compiler_params=pltpu.CompilerParams(
            collective_id=2, has_side_effects=True, vmem_limit_bytes=60 << 20
        ),
        cost_estimate=pl.CostEstimate(
            flops=70 * 10**9, bytes_accessed=30 << 20, transcendentals=0
        ),
        name="mlp_backward",
    )(
        g, upstream, values, gain.reshape(1, -1), pack, x.reshape(tokens, width),
        up.reshape(tokens, twice),
    )


def after_corner_first(scatter, n):
    if n % 2 == 0:
        scatter.copy(3 - n // 2).start()
    if n == 3:
        scatter.corner()
    if n == 5:
        scatter.copy(2).wait_recv()
        scatter.add(2, 0, scatter.rows, scatter.near.at[2])
        scatter.copy(7).start()
    if n == 7:
        scatter.copy(1).wait_recv()
        scatter.add(1, 0, scatter.rows, scatter.near.at[1])
        scatter.copy(6).start()


class Line:
    def __init__(self, net, count):
        self.net, self.count = net, count
        self.others = [(net.base + net.t, lax.rem(net.z + d, count)) for d in range(1, count)]
        self.next = (net.base + net.t, net.z + 1)
        self.before = (net.base + net.t, net.z - 1)

    def to_all(self, ends, send, recv):
        at = ends.at[self.net.z]
        copies = [
            remote(at, at, send.at[d], recv.at[d], to) for d, to in enumerate(self.others)
        ]
        for copy in copies:
            copy.start()
        for d, copy in enumerate(copies):
            source = lax.rem(self.net.z + self.count - 1 - d, self.count)
            from_at = ends.at[source]
            remote(from_at, from_at, send.at[d], recv.at[d], self.others[d]).wait_recv()
        for copy in copies:
            copy.wait_send()


def inside_of(positions, offset, length):
    return jnp.where((positions >= offset) & (positions < offset + length), 1.0, 0.0)


def read_halves(ref, at):
    return jnp.concatenate([ref[n, at] for n in range(ref.shape[0])], 1)


def write_halves(ref, at, value):
    for n in range(ref.shape[0]):
        ref[n, at] = value[:, n * 128 : (n + 1) * 128]


def one_minus_exp(v):
    series = 1.0 + v * (1.0 / 7.0)
    for n in (6.0, 5.0, 4.0, 3.0, 2.0):
        series = 1.0 + v * (1.0 / n) * series
    return jnp.where(v > -0.35, -v * series, 1.0 - jnp.exp(v))


def sigmoid(v):
    return 1.0 / (1.0 + jnp.exp(-v))


def rec_forward_kernel(
    gathered,
    x_ref, residual_ref, gain_ref, pack_ref, small_ref, slots_ref,
    out_ref, normed_ref, full_out, branch_out, stream_out, conv_out, state_out,
    full, part, near, wide, far, gs, gr, ss, sr,
    col, gates, wout, branch, stream, conv, state, retain, inflow, ends, carry, hs, hr, es, er, sem,
):
    net = Net()
    seq = ends.shape[0]
    line = Line(net, seq)
    gather = Gather(net, full, gs, gr)
    scatter = Scatter(net, part, near, wide, far, ss, sr)
    rows = full.shape[1]
    head = gates.shape[0]
    own = pltpu.make_async_copy(x_ref, full if gathered else full.at[net.t], sem.at[0])
    loads = unpack_rec(pack_ref, col, wout, gates, sem, 9)
    for load in [own] + loads:
        load.start()
    net.enter(line.others)
    own.wait()
    if not gathered:
        gather.begin()

    @pl.when(net.z == 0)
    def _():
        stream[:, pl.ds(0, 8), :] = jnp.zeros((TP, 8, head), F32)

    for load in loads:
        load.wait()

    def halo(i):
        slot = net.slot(i // 2, lax.rem(i, 2))
        return remote(
            stream.at[slot, pl.ds(rows, 8)], stream.at[slot, pl.ds(0, 8)],
            hs.at[i], hr.at[i], line.next,
        )

    def project(i):
        slot = net.slot(i // 2, lax.rem(i, 2))
        both = dot(full[slot], col[...])
        branch[slot] = both[:, :head]
        stream[slot, pl.ds(8, rows)] = both[:, head:]

        @pl.when(net.z < seq - 1)
        def _():
            halo(i).start()

    def gate(i):
        slot = net.slot(i // 2, lax.rem(i, 2))

        @pl.when(net.z > 0)
        def _():
            halo(i).wait_recv()

        length, offset = slots_ref[slot, 0], slots_ref[slot, 1]
        positions = net.z * rows + lax.broadcasted_iota(jnp.int32, (rows, head), 0)
        inside = inside_of(positions, offset, length)
        mixed = small_ref[pl.ds(CONV, 1), :] + small_ref[pl.ds(0, 1), :] * stream[slot, pl.ds(8, rows)]
        restart = positions == 0
        for j in range(1, CONV):
            same = jnp.where(inside == inside_of(positions - j, offset, length), 1.0, 0.0)
            if j == 1:
                restart = restart | (same == 0.0)
            mixed += small_ref[pl.ds(j, 1), :] * stream[slot, pl.ds(8 - j, rows)] * same
        low = mixed.astype(BF)
        conv[slot] = low
        pre = dot(low, gates[...])
        rate = sigmoid(pre[:, :head] + small_ref[pl.ds(CONV + 1, 1), :])
        admit = sigmoid(pre[:, head:] + small_ref[pl.ds(CONV + 2, 1), :])
        log_retain = rate * small_ref[pl.ds(CONV + 3, 1), :]
        at = pl.ds(pl.multiple_of(slot * rows, rows), rows)
        write_halves(retain, at, jnp.where(restart, 0.0, jnp.exp(log_retain)))
        scale = jnp.where(restart, 1.0, jnp.sqrt(one_minus_exp(2.0 * log_retain)))
        write_halves(inflow, at, scale * admit * low.astype(F32))

    def one(i, _):
        for n in range(1, TP):
            @pl.when(i == n)
            def _():
                if not gathered:
                    gather.before(n)

        @pl.when(i < TP)
        def _():
            project(i)

        @pl.when(i >= LATER)
        def _():
            gate(i - LATER)

        return 0

    lax.fori_loop(0, TP + LATER, one, 0)
    saves = [
        pltpu.make_async_copy(branch, branch_out, sem.at[5]),
        pltpu.make_async_copy(stream, stream_out, sem.at[6]),
        pltpu.make_async_copy(conv, conv_out, sem.at[7]),
    ]
    if not gathered:
        saves.append(pltpu.make_async_copy(full, full_out, sem.at[4]))
    for save in saves:
        save.start()

    lanes = [pl.ds(i, 128) for i in range(0, head, 128)]

    def step(p, carried):
        at = pl.ds(p, TP, stride=rows)
        result = []
        for n, (value, decay) in enumerate(carried):
            a = retain[n, at]
            value = a * value + inflow[n, at]
            decay = a * decay
            inflow[n, at] = value
            retain[n, at] = decay
            result.append((value, decay))
        return tuple(result)

    start = tuple((jnp.zeros((TP, 128), F32), jnp.ones((TP, 128), F32)) for _ in lanes)
    last = lax.fori_loop(0, rows, step, start, unroll=8)
    for lane, (value, decay) in zip(lanes, last):
        ends[net.z, pl.ds(0, TP), lane] = decay
        ends[net.z, pl.ds(TP, TP), lane] = value
    line.to_all(ends, es, er)
    entering = jnp.zeros((TP, head), F32)
    for z in range(seq - 1):
        later = ends[z, pl.ds(0, TP)] * entering + ends[z, pl.ds(TP, TP)]
        entering = jnp.where(z < net.z, later, entering)
    carry[...] = entering

    def join(i, _):
        m, s = 3 - i // 2, 1 - lax.rem(i, 2)
        slot = net.slot(m, s)
        at = pl.ds(pl.multiple_of(slot * rows, rows), rows)
        first = carry[pl.ds(slot, 1), :]
        states = read_halves(inflow, at) + read_halves(retain, at) * first
        state[slot, pl.ds(0, 8)] = jnp.broadcast_to(first, (8, head))
        state[slot, pl.ds(8, rows)] = states
        joined = glu_product(branch[slot], states).astype(BF)
        part[s, m] = dot(joined, wout[...]).astype(BF)
        for n in range(TP):
            @pl.when(i == n)
            def _():
                after_corner_first(scatter, n)

        return 0

    lax.fori_loop(0, TP, join, 0)
    saves.append(pltpu.make_async_copy(state, state_out, sem.at[8]))
    saves[-1].start()
    scatter.edges()

    @pl.when(net.z < seq - 1)
    def _():
        lax.fori_loop(0, TP, lambda i, _: (halo(i).wait_send(), 0)[1], 0)

    scatter.finish()
    end_forward(scatter, residual_ref, gain_ref, out_ref, normed_ref)
    if not gathered:
        gather.finish()
    for save in saves:
        save.wait()


def rec_scratch(pack, width):
    seq, _, both = pack.shape
    return [
        pltpu.VMEM((width, both), BF),
        pltpu.VMEM((both // 2, both), BF),
        pltpu.VMEM((both // 2, width), BF),
    ]


def rec_forward(x, residual, gain, pack, small, slots):
    gathered = x.ndim == 3
    rows, width = residual.shape
    seq, _, head = pack.shape
    head = head // 2
    shape = jax.ShapeDtypeStruct
    dma = pltpu.SemaphoreType.DMA
    tokens = TP * rows
    result = list(pl.pallas_call(
        partial(rec_forward_kernel, gathered),
        in_specs=[ANY, VM, VM, ANY, VM, pl.BlockSpec(memory_space=pltpu.SMEM)],
        out_specs=[VM, VM, ANY, ANY, ANY, ANY, ANY],
        out_shape=[
            shape((rows, width), F32),
            shape((rows, width), BF),
            shape((8, 128) if gathered else (TP, rows, width), BF),
            shape((TP, rows, head), F32),
            shape((TP, rows + 8, head), F32),
            shape((TP, rows, head), BF),
            shape((TP, rows + 8, head), F32),
        ],
        scratch_shapes=plane_scratch(rows, width)
        + rec_scratch(pack, width)
        + [
            pltpu.VMEM((TP, rows, head), F32),
            pltpu.VMEM((TP, rows + 8, head), F32),
            pltpu.VMEM((TP, rows, head), BF),
            pltpu.VMEM((TP, rows + 8, head), F32),
            pltpu.VMEM((head // 128, tokens, 128), F32),
            pltpu.VMEM((head // 128, tokens, 128), F32),
            pltpu.VMEM((seq, 2 * TP, head), F32),
            pltpu.VMEM((TP, head), F32),
            dma((TP,)), dma((TP,)), dma((seq - 1,)), dma((seq - 1,)), dma((9 + 5 * seq,)),
        ],
        compiler_params=pltpu.CompilerParams(
            collective_id=5 if gathered else 3, has_side_effects=True, vmem_limit_bytes=58 << 20
        ),
        cost_estimate=pl.CostEstimate(
            flops=70 * 10**9, bytes_accessed=30 << 20, transcendentals=0
        ),
        name="rec_forward_first" if gathered else "rec_forward",
    )(x, residual, gain.reshape(1, -1), pack, small, slots))
    if gathered:
        result[2] = x
    return result


def rec_backward_kernel(
    g_ref, upstream_ref, values_ref, gain_ref, pack_ref, small_ref, slots_ref,
    x_ref, branch_ref, stream_ref, conv_ref, state_ref,
    grad_ref, low_ref, gain_out, gcol_ref, channel_ref,
    full, part, near, wide, far, gs, gr, ss, sr,
    col, gates, wout, xs, branch, stream, conv, state,
    retain, direct, suffix, joined, both, gpre, mixed, ends, carry, hs, hr, es, er, sem,
):
    net = Net()
    seq = ends.shape[0]
    line = Line(net, seq)
    gather = Gather(net, full, gs, gr)
    scatter = Scatter(net, part, near, wide, far, ss, sr)
    rows, width = full.shape[1], full.shape[2]
    head = gates.shape[0]
    own = pltpu.make_async_copy(g_ref, full.at[net.t], sem.at[0])
    loads = [
        pltpu.make_async_copy(a, b, sem.at[1 + n])
        for n, (a, b) in enumerate(
            (
                (branch_ref, branch), (state_ref, state), (conv_ref, conv), (stream_ref, stream),
                (x_ref, xs),
            )
        )
    ]
    loads = unpack_rec(pack_ref, col, wout, gates, sem, 9) + loads
    for load in [own] + loads:
        load.start()
    net.enter(line.others)
    own.wait()
    gather.begin()

    @pl.when(net.z == seq - 1)
    def _():
        mixed[:, pl.ds(rows, 8), :] = jnp.zeros((TP, 8, head), F32)

    channel_ref[...] = jnp.zeros_like(channel_ref)
    for load in loads[:-2]:
        load.wait()

    def gate_parts(slot):
        positions = net.z * rows + lax.broadcasted_iota(jnp.int32, (rows, head), 0)
        length, offset = slots_ref[slot, 0], slots_ref[slot, 1]
        inside = inside_of(positions, offset, length)
        restart = (positions == 0) | (inside != inside_of(positions - 1, offset, length))
        pre = dot(conv[slot], gates[...])
        rate = sigmoid(pre[:, :head] + small_ref[pl.ds(CONV + 1, 1), :])
        admit = sigmoid(pre[:, head:] + small_ref[pl.ds(CONV + 2, 1), :])
        log_retain = rate * small_ref[pl.ds(CONV + 3, 1), :]
        return positions, offset, length, inside, restart, rate, admit, log_retain

    def open_block(m, s):
        slot = net.slot(m, s)
        at = pl.ds(pl.multiple_of(slot * rows, rows), rows)
        grad_joined = dot_nt(full[slot], wout[...])
        act, slope = gelu_parts(branch[slot])
        states = state[slot, pl.ds(8, rows)]
        joined[at] = (act * states).astype(BF)
        both[at, :head] = (grad_joined * states * slope).astype(BF)
        write_halves(direct, at, grad_joined * act)
        _, _, _, _, restart, _, _, log_retain = gate_parts(slot)
        write_halves(retain, at, jnp.where(restart, 0.0, jnp.exp(log_retain)))

    steps(gather, None, open_block)
    lanes = [pl.ds(i, 128) for i in range(0, head, 128)]

    def step(i, carried):
        at = pl.ds(rows - 1 - i, TP, stride=rows)
        result = []
        for n, (value, decay, ahead) in enumerate(carried):
            value = ahead * value + direct[n, at]
            decay = ahead * decay
            direct[n, at] = value
            suffix[n, at] = decay
            result.append((value, decay, retain[n, at]))
        return tuple(result)

    one = jnp.minimum(retain[0, pl.ds(0, TP)] + 2.0, 1.0)
    last = lax.fori_loop(
        0, rows, step, tuple((jnp.zeros((TP, 128), F32), one, one) for _ in lanes), unroll=8
    )
    for lane, (value, decay, first) in zip(lanes, last):
        ends[net.z, pl.ds(0, TP), lane] = first * decay
        ends[net.z, pl.ds(TP, TP), lane] = first * value
    line.to_all(ends, es, er)
    entering = jnp.zeros((TP, head), F32)
    for z in range(seq - 1, 0, -1):
        earlier = ends[z, pl.ds(0, TP)] * entering + ends[z, pl.ds(TP, TP)]
        entering = jnp.where(z > net.z, earlier, entering)
    carry[...] = entering
    loads[-2].wait()

    def halo(i):
        slot = net.slot(3 - i // 2, 1 - lax.rem(i, 2))
        return remote(
            mixed.at[slot, pl.ds(0, 8)], mixed.at[slot, pl.ds(rows, 8)],
            hs.at[i], hr.at[i], line.before,
        )

    def through_gates(i):
        slot = net.slot(3 - i // 2, 1 - lax.rem(i, 2))
        at = pl.ds(pl.multiple_of(slot * rows, rows), rows)
        grad_states = read_halves(direct, at) + read_halves(suffix, at) * carry[pl.ds(slot, 1), :]
        positions, offset, length, inside, restart, rate, admit, log_retain = gate_parts(slot)
        low = conv[slot].astype(F32)
        kept = jnp.exp(log_retain)
        root = jnp.sqrt(one_minus_exp(2.0 * log_retain))
        scale = jnp.where(restart, 1.0, root)
        grad_admit = grad_states * scale * low
        grad_scale = grad_states * admit * low
        grad_log = grad_states * state[slot, pl.ds(7, rows)] * kept - grad_scale * kept * kept / root
        grad_log = jnp.where(restart, 0.0, grad_log)
        rate_part = grad_log * small_ref[pl.ds(CONV + 3, 1), :] * rate * (1.0 - rate)
        admit_part = grad_admit * admit * (1.0 - admit)
        gpre[at, :head] = rate_part.astype(BF)
        gpre[at, head:] = admit_part.astype(BF)
        grad_mixed = grad_states * scale * admit + dot_nt(gpre[at], gates[...])
        mixed[slot, pl.ds(0, rows)] = grad_mixed

        @pl.when(net.z > 0)
        def _():
            halo(i).start()

        sums = [jnp.sum(grad_mixed * stream[slot, pl.ds(8, rows)], axis=0, keepdims=True)]
        for j in range(1, CONV):
            same = jnp.where(inside == inside_of(positions - j, offset, length), 1.0, 0.0)
            sums.append(
                jnp.sum(
                    grad_mixed * stream[slot, pl.ds(8 - j, rows)] * same, axis=0, keepdims=True
                )
            )
        for term in (grad_mixed, rate_part, admit_part, grad_log * rate):
            sums.append(jnp.sum(term, axis=0, keepdims=True))
        for n, term in enumerate(sums):
            channel_ref[pl.ds(n, 1), :] += term

    def to_input(i):
        m, s = 3 - i // 2, 1 - lax.rem(i, 2)
        slot = net.slot(m, s)
        at = pl.ds(pl.multiple_of(slot * rows, rows), rows)

        @pl.when(net.z < seq - 1)
        def _():
            halo(i).wait_recv()

        positions = net.z * rows + lax.broadcasted_iota(jnp.int32, (rows, head), 0)
        length, offset = slots_ref[slot, 0], slots_ref[slot, 1]
        inside = inside_of(positions, offset, length)
        grad_stream = small_ref[pl.ds(0, 1), :] * mixed[slot, pl.ds(0, rows)]
        for j in range(1, CONV):
            same = jnp.where(inside == inside_of(positions + j, offset, length), 1.0, 0.0)
            grad_stream += small_ref[pl.ds(j, 1), :] * mixed[slot, pl.ds(j, rows)] * same
        both[at, head:] = grad_stream.astype(BF)
        part[s, m] = dot_nt(both[at], col[...]).astype(BF)

    def one_block(i, _):
        @pl.when(i < TP)
        def _():
            through_gates(i)

        @pl.when(i >= LATER)
        def _():
            to_input(i - LATER)

        for n in range(TP):
            @pl.when(i == n + LATER)
            def _():
                after_corner_first(scatter, n)

        return 0

    lax.fori_loop(0, TP + LATER, one_block, 0)
    scatter.edges()
    loads[-1].wait()
    own_rows = width // (TP * seq)
    tile = 2 * seq * own_rows

    def columns(j, _):
        x = xs[:, pl.ds(pl.multiple_of(j * tile, 128), tile)]
        product = dot_tn(x, both[...]).astype(BF)
        for r in range(2):
            for z in range(seq):
                low = (r * seq + z) * own_rows
                at = pl.ds(pl.multiple_of((2 * j + r) * own_rows, own_rows), own_rows)
                gcol_ref[z, at] = product[low : low + own_rows]
        return 0

    lax.fori_loop(0, TP // 2, columns, 0)
    low_conv = conv[...].reshape(TP * rows, head)
    product = dot_tn(low_conv, gpre[...]).astype(BF)
    third, base, part_head = width // 3, width // seq, head // seq
    for z in range(seq):
        low = base + 3 * part_head
        gcol_ref[z, low : low + part_head] = product[z * part_head : (z + 1) * part_head]
    for j in range(3):
        at = pl.ds(j * third, third)
        product = dot_tn(joined[...], full[:, :, at].reshape(TP * rows, third)).astype(BF)
        for z in range(seq):
            low = base + j * part_head
            gcol_ref[z, low : low + part_head] = product[z * part_head : (z + 1) * part_head]

    @pl.when(net.z > 0)
    def _():
        lax.fori_loop(0, TP, lambda i, _: (halo(i).wait_send(), 0)[1], 0)

    scatter.finish()
    end_backward(scatter, upstream_ref, values_ref, gain_ref, grad_ref, low_ref, gain_out)
    gather.finish()


def rec_backward(g, upstream, values, gain, pack, small, slots, saved):
    rows, width = g.shape
    seq, _, head = pack.shape
    head = head // 2
    tokens = TP * rows
    shape = jax.ShapeDtypeStruct
    dma = pltpu.SemaphoreType.DMA
    x, branch, stream, conv, state = saved
    return pl.pallas_call(
        rec_backward_kernel,
        in_specs=[ANY, VM, VM, VM, ANY, VM, pl.BlockSpec(memory_space=pltpu.SMEM)]
        + [ANY] * 5,
        out_specs=[VM] * 5,
        out_shape=[
            shape((rows, width), F32),
            shape((rows, width), BF),
            shape((1, width), F32),
            shape(pack.shape, BF),
            shape((8, head), F32),
        ],
        scratch_shapes=plane_scratch(rows, width)
        + rec_scratch(pack, width)
        + [
            pltpu.VMEM((tokens, width), BF),
            pltpu.VMEM(branch.shape, F32),
            pltpu.VMEM(stream.shape, F32),
            pltpu.VMEM(conv.shape, BF),
            pltpu.VMEM(state.shape, F32),
            pltpu.VMEM((head // 128, tokens, 128), F32),
            pltpu.VMEM((head // 128, tokens, 128), F32),
            pltpu.VMEM((head // 128, tokens, 128), F32),
            pltpu.VMEM((tokens, head), BF),
            pltpu.VMEM((tokens, 2 * head), BF),
            pltpu.VMEM((tokens, 2 * head), BF),
            pltpu.VMEM((TP, rows + 8, head), F32),
            pltpu.VMEM((seq, 2 * TP, head), F32),
            pltpu.VMEM((TP, head), F32),
            dma((TP,)), dma((TP,)), dma((seq - 1,)), dma((seq - 1,)), dma((9 + 5 * seq,)),
        ],
        compiler_params=pltpu.CompilerParams(
            collective_id=4, has_side_effects=True, vmem_limit_bytes=60 << 20
        ),
        cost_estimate=pl.CostEstimate(
            flops=80 * 10**9, bytes_accessed=30 << 20, transcendentals=0
        ),
        name="rec_backward",
    )(
        g, upstream, values, gain.reshape(1, -1), pack, small, slots,
        x.reshape(tokens, width), branch, stream, conv, state,
    )


def open_kernel(
    x_ref, small_ref, gain_ref, slot_ref, pack_ref,
    small_out, gain_out, slot_out, full_out, pack_out,
    full, smalls, gains, slots, gs, gr, ps, pr, sem,
):
    net = Net()
    seq = smalls.shape[0]
    line = Line(net, seq)
    gather = Gather(net, full, gs, gr)
    plane = [net.device(m, s) for m in range(4) for s in range(2)][1:]
    mine = [
        pltpu.make_async_copy(small_ref, smalls.at[net.z], sem.at[0]),
        pltpu.make_async_copy(gain_ref, gains.at[net.z], sem.at[1]),
        pltpu.make_async_copy(slot_ref, slots.at[net.t], sem.at[2]),
    ]
    own_pack = pltpu.make_async_copy(pack_ref, pack_out.at[net.z], sem.at[4])
    for copy in mine + [own_pack]:
        copy.start()
    net.enter(line.others + [net.device(1, 1), net.device(2, 1), net.device(3, 0), net.device(3, 1)])
    for copy in mine:
        copy.wait()

    sends, arrivals = [], []

    def push(ref, own, source, to):
        n = len(sends)
        at, from_at = ref.at[own], ref.at[source]
        sends.append(remote(at, at, ps.at[n], pr.at[n], to))
        arrivals.append(remote(from_at, from_at, ps.at[n], pr.at[n], to))

    for ref in (gains, smalls):
        for d, to in enumerate(line.others):
            push(ref, net.z, lax.rem(net.z + seq - 1 - d, seq), to)
    for n, to in enumerate(plane):
        m, s = (n + 1) // 2, (n + 1) % 2
        push(slots, net.t, net.slot(m, s), to)
    for copy in sends:
        copy.start()
    small_sends, small_arrivals = list(sends), list(arrivals)
    for d, to in enumerate(line.others):
        n = len(sends)
        source = lax.rem(net.z + seq - 1 - d, seq)
        sends.append(remote(pack_ref, pack_out.at[net.z], ps.at[n], pr.at[n], to))
        arrivals.append(remote(pack_ref, pack_out.at[source], ps.at[n], pr.at[n], to))
        sends[-1].start()
    for copy in arrivals[: seq - 1]:
        copy.wait_recv()
    rows, width = x_ref.shape
    part, chunk = width // seq, 32

    def norm(i, _):
        at = pl.ds(pl.multiple_of(i * chunk, chunk), chunk)
        value = x_ref[at].astype(F32)
        scale = lax.rsqrt(jnp.mean(value * value, axis=-1, keepdims=True) + EPSILON)
        for z in range(seq):
            low = z * part
            full[net.t, at, low : low + part] = (
                value[:, low : low + part] * scale * gains[z, pl.ds(0, 1), :]
            ).astype(BF)
        return 0

    lax.fori_loop(0, rows // chunk, norm, 0)
    gather.begin()
    for copy in small_arrivals[seq - 1 :]:
        copy.wait_recv()
    saves = [
        pltpu.make_async_copy(a, b, sem.at[n])
        for n, (a, b) in enumerate(((smalls, small_out), (gains, gain_out), (slots, slot_out)))
    ]
    for save in saves:
        save.start()
    for n in range(1, TP):
        gather.before(n)
    gather.finish()
    saves.append(pltpu.make_async_copy(full, full_out, sem.at[3]))
    saves[-1].start()
    for copy in arrivals[len(small_arrivals) :]:
        copy.wait_recv()
    for copy in sends:
        copy.wait_send()
    own_pack.wait()
    for save in saves:
        save.wait()


def opening(seq, x, small, gain, slot, pack):
    rows, width = x.shape
    shape = jax.ShapeDtypeStruct
    dma = pltpu.SemaphoreType.DMA
    pushes = 3 * (seq - 1) + TP - 1
    return pl.pallas_call(
        open_kernel,
        in_specs=[VM, ANY, ANY, ANY, ANY],
        out_specs=[ANY] * 5,
        out_shape=[
            shape((seq,) + small.shape, F32),
            shape((seq,) + gain.shape, F32),
            shape((TP,) + slot.shape, jnp.int32),
            shape((TP, rows, width), BF),
            shape((seq,) + pack.shape, BF),
        ],
        scratch_shapes=[
            pltpu.VMEM((TP, rows, width), BF),
            pltpu.VMEM((seq,) + small.shape, F32),
            pltpu.VMEM((seq,) + gain.shape, F32),
            pltpu.VMEM((TP,) + slot.shape, jnp.int32),
            dma((10,)), dma((10,)), dma((pushes,)), dma((pushes,)), dma((5,)),
        ],
        compiler_params=pltpu.CompilerParams(
            collective_id=6, has_side_effects=True, vmem_limit_bytes=40 << 20
        ),
        cost_estimate=pl.CostEstimate(
            flops=40 * 10**9, bytes_accessed=10 << 20, transcendentals=0
        ),
        name="opening",
    )(x, small, gain, slot, pack)


def close_kernel(
    gain_ref, channel_ref, *refs
):
    count = (len(refs) - 8) // 2
    blocks, (gain_out, channel_out), moved = refs[:count], refs[count : count + 2], refs[
        count + 2 : 2 * count + 2
    ]
    plane_gain, line_gain, line_channel, ps, pr, sem = refs[2 * count + 2 :]
    net = Net()
    seq = line_gain.shape[0]
    line = Line(net, seq)
    plane = [net.device(m, s) for m in range(4) for s in range(2)][1:]
    slots = [net.slot(m, s) for m in range(4) for s in range(2)][1:]
    own = [
        pltpu.make_async_copy(block.at[net.t], out.at[net.t], sem.at[n])
        for n, (block, out) in enumerate(zip(blocks, moved))
    ]
    plane_gain[net.t] = gain_ref[...]
    line_channel[net.z] = channel_ref[...]
    for copy in own:
        copy.start()
    net.enter(line.others + [net.device(1, 1), net.device(2, 1), net.device(3, 0), net.device(3, 1)])
    used = []

    def push(src, dst, landed, to):
        n = len(used)
        used.append(remote(src, dst, ps.at[n], pr.at[n], to))
        used[-1].start()
        return remote(src, landed, ps.at[n], pr.at[n], to)

    gains = [
        push(plane_gain.at[net.t], plane_gain.at[net.t], plane_gain.at[slot], to)
        for slot, to in zip(slots, plane)
    ]
    sources = [lax.rem(net.z + seq - 1 - d, seq) for d in range(seq - 1)]
    rest = [
        push(line_channel.at[net.z], line_channel.at[net.z], line_channel.at[source], to)
        for source, to in zip(sources, line.others)
    ]
    for block, out in zip(blocks, moved):
        for slot, to in zip(slots, plane):
            rest.append(push(block.at[slot], out.at[net.t], out.at[slot], to))
    for copy in gains:
        copy.wait_recv()
    total = plane_gain[0]
    for t in range(1, TP):
        total += plane_gain[t]
    line_gain[net.z] = total
    for source, to in zip(sources, line.others):
        rest.append(push(line_gain.at[net.z], line_gain.at[net.z], line_gain.at[source], to))
    for copy in rest:
        copy.wait_recv()
    total, channel = line_gain[0], line_channel[0]
    for z in range(1, seq):
        total += line_gain[z]
        channel += line_channel[z]
    gain_out[...] = total
    channel_out[...] = channel
    for copy in used:
        copy.wait_send()
    for copy in own:
        copy.wait()


def closing(seq, gains, channels, blocks):
    shape = jax.ShapeDtypeStruct
    dma = pltpu.SemaphoreType.DMA
    pushes = (TP - 1) * (1 + len(blocks)) + 2 * (seq - 1)
    return pl.pallas_call(
        close_kernel,
        in_specs=[VM, VM] + [ANY] * len(blocks),
        out_specs=[VM, VM] + [ANY] * len(blocks),
        out_shape=[shape(gains.shape, F32), shape(channels.shape, F32)]
        + [shape(block.shape, block.dtype) for block in blocks],
        scratch_shapes=[
            pltpu.VMEM((TP,) + gains.shape, F32),
            pltpu.VMEM((seq,) + gains.shape, F32),
            pltpu.VMEM((seq,) + channels.shape, F32),
            dma((pushes,)), dma((pushes,)), dma((len(blocks),)),
        ],
        compiler_params=pltpu.CompilerParams(
            collective_id=7, has_side_effects=True, vmem_limit_bytes=40 << 20
        ),
        cost_estimate=pl.CostEstimate(
            flops=40 * 10**9, bytes_accessed=10 << 20, transcendentals=0
        ),
        name="closing",
    )(gains, channels, *blocks)


def layer_backward(upstream, upstream_low, w, saved, slots, pending):
    residual, kept, middle, kept_two = saved
    pending_mlp, pending_rec = pending
    upstream_low, pending_mlp = lax.optimization_barrier((upstream_low, pending_mlp))
    grad_middle, mid_low, grad_gain_two, g_mlp = mlp_backward(
        upstream_low, upstream, middle, w["gain"][1], w["mlp"], *kept_two
    )
    mlp_share = over_seq(g_mlp)
    mid_low, pending_rec = lax.optimization_barrier((mid_low, pending_rec))
    grad, grad_low, grad_gain_one, g_rec, channel = rec_backward(
        mid_low, grad_middle, residual, w["gain"][0], w["rec"], w["small"], slots, kept
    )
    g_rec, mlp_share = lax.optimization_barrier((g_rec, mlp_share))
    rec_share = over_seq(g_rec)
    slope = 8.0 * jax.nn.sigmoid(-w["decay"])
    channel = jnp.concatenate([channel[:7], channel[7:] * slope], 0)
    gains = jnp.concatenate([grad_gain_one, grad_gain_two], 0)
    return grad, grad_low, (mlp_share, rec_share), channel, gains, (pending_mlp, pending_rec)


def over_seq(value):
    return lax.psum_scatter(value, "seq", scatter_dimension=0, tiled=False)


def columns(parts):
    return jnp.moveaxis(parts, 0, 1).reshape(parts.shape[1], -1)


def owned_grads(plan, mlp_share, rec_share, mlp, rec, width, head, units):
    base = width // plan.seq
    h, u = head // plan.seq, units // plan.seq
    out = [rec_share[base + i * h : base + (i + 1) * h] for i in range(3)]
    gates = rec_share[base + 3 * h :]
    rest, blocks = mlp_split(width, 2 * units)
    down = [mlp_share[base + u :, i * rest : (i + 1) * rest] for i in range(blocks)]
    grads = [
        columns(rec[:, :, :head]),
        columns(rec[:, :, head:]),
        gates[:, :head],
        gates[:, head:],
        jnp.concatenate(out, 1),
        columns(mlp[:, :, :units]),
        columns(mlp[:, :, units:]),
        jnp.concatenate([mlp_share[base : base + u], jnp.concatenate(down, 0)], 1),
    ]
    return [to_owners(plan, g.astype(F32), 0) for g in grads]


def local(plan, *args):
    (
        block_input, cotangent, lengths, offsets, norm_gains, branch_proj, stream_proj, conv_kernel,
        conv_bias, rate_proj, admit_proj, gate_bias, decay_logit, out_proj, mlp_gate, mlp_up,
        mlp_down,
    ) = args
    tp, dp, seq = plan.tp, plan.dp, plan.seq
    t = lax.axis_index("rep") % tp
    z = lax.axis_index("seq")
    rows = block_input.shape[0]
    head = branch_proj.shape[2] // tp
    units = mlp_gate.shape[2] // tp

    channels = conv_kernel.shape[2]
    small = jnp.concatenate([conv_kernel, conv_bias[:, None], gate_bias, decay_logit[:, None]], 1)
    small = small.reshape(LAYERS * 8, channels).astype(F32)
    slot = jnp.pad(jnp.stack([lengths, offsets], 1), ((0, 7), (0, 126)))
    def col(weight, layer, width):
        return lax.dynamic_slice_in_dim(weight[layer], t * width, width, 1)

    def chunk(weight, layer):
        size = weight.shape[1] // tp
        return lax.dynamic_slice_in_dim(weight[layer], t * size, size, 0)

    def below(rows, twice):
        rest, blocks = mlp_split(rows.shape[1], twice)
        low = rows.shape[0] // blocks
        side = [rows[i * low : (i + 1) * low, twice:] for i in range(blocks)]
        return jnp.concatenate([rows[:, :twice], jnp.concatenate(side, 1)], 0)

    def rec_pack(l, ready):
        out = chunk(out_proj, l)
        gates = jnp.concatenate([chunk(rate_proj, l), chunk(admit_proj, l)], 1)
        out = [out[:, i * 2 * head : (i + 1) * 2 * head] for i in range(3)] + [gates]
        out, ready = lax.optimization_barrier((jnp.concatenate(out, 0), ready))
        rec = jnp.concatenate([col(branch_proj, l, head), col(stream_proj, l, head)], 1)
        return jnp.concatenate([rec, owner_chunks(plan, out)], 0), ready

    def mlp_pack(l, ready):
        down, ready = lax.optimization_barrier((below(chunk(mlp_down, l), 2 * units), ready))
        mlp = jnp.concatenate([col(mlp_gate, l, units), col(mlp_up, l, units)], 1)
        return jnp.concatenate([mlp, owner_chunks(plan, down)], 0), ready

    pack, _ = rec_pack(0, ())
    smalls, gains, layout, normed, rec = opening(
        seq, block_input, small, norm_gains.reshape(2 * LAYERS, -1).astype(F32), slot, pack
    )
    layout = layout[:, 0, :2]
    gains = jnp.moveaxis(gains, 0, 1).reshape(LAYERS, 2, -1)
    smalls = jnp.moveaxis(smalls, 0, 1).reshape(LAYERS, 8, -1)
    smalls = lax.dynamic_slice_in_dim(smalls, t * head, head, 2)


    residual = block_input.astype(F32)
    saved_all, weights = [], []
    for l in range(LAYERS):
        if l == 0:
            pack, rec = mlp_pack(l, rec)
        else:
            pack, normed = mlp_pack(l, normed)
        w = dict(
            gain=gains[l],
            small=jnp.concatenate([smalls[l, :7], -8.0 * jax.nn.softplus(-smalls[l, 7:])], 0),
            decay=smalls[l, 7:],
            rec=rec,
            mlp=lax.all_gather(pack, "seq"),
        )
        weights.append(w)
        kept = rec_forward(normed, residual, w["gain"][1], w["rec"], w["small"], layout)
        middle, normed_two, *kept = kept
        if l + 1 < LAYERS:
            pack, normed_two = rec_pack(l + 1, normed_two)
            rec = lax.all_gather(pack, "seq")
        output, normed, *kept_two = mlp_forward(
            normed_two, middle, gains[(l + 1) % LAYERS, 0], w["mlp"]
        )
        saved_all.append((residual, kept, middle, kept_two))
        residual = output
    positions = z * rows + jnp.arange(rows, dtype=jnp.int32)
    inside = (positions >= offsets[0]) & (positions < offsets[0] + lengths[0])
    gradient = cotangent.astype(F32) * inside.astype(F32)[:, None]

    gradient_low = gradient.astype(BF)
    shares = [None] * LAYERS
    channel_all, gain_all = [None] * LAYERS, [None] * LAYERS
    for l in reversed(range(LAYERS)):
        gradient, gradient_low, shares[l], channel_all[l], gain_all[l], pending = layer_backward(
            gradient, gradient_low, weights[l], saved_all[l], layout,
            ((), ()) if l + 1 == LAYERS else shares[l + 1],
        )
        if l + 1 < LAYERS:
            shares[l + 1] = pending
    width = block_input.shape[1]
    base = width // seq

    def by_slot(share):
        return share[:base].reshape(tp, -1, share.shape[1])

    blocks = [by_slot(shares[l][0]) for l in range(LAYERS)]
    blocks += [by_slot(shares[l][1]) for l in range(1, LAYERS)]
    gains, channel, *blocks = closing(
        seq, jnp.concatenate(gain_all, 0), jnp.concatenate(channel_all, 0), blocks
    )
    last = lax.all_to_all(
        by_slot(shares[0][1]), "rep", split_axis=0, concat_axis=0, axis_index_groups=plan.tp_groups
    )
    mlps, recs = blocks[:LAYERS], [last] + blocks[LAYERS:]
    outs = [
        owned_grads(plan, *shares[l], mlps[l], recs[l], width, head, units) for l in range(LAYERS)
    ]
    big = [jnp.stack([outs[l][i] for l in range(LAYERS)]) for i in range(8)]

    channel = lax.dynamic_slice_in_dim(channel, z * (head // seq), head // seq, 1)
    channel = to_owners(plan, channel, 1).reshape(LAYERS, 8, -1)
    if dp > 1:
        gains = lax.psum(gains, "rep", axis_index_groups=plan.dp_groups)
    own = gains.shape[1] // (plan.rep * seq)
    owner = lax.axis_index(("rep", "seq"))
    gains = lax.dynamic_slice_in_dim(gains, owner * own, own, 1).reshape(LAYERS, 2, own)
    return (
        residual.astype(BF),
        gradient,
        gains,
        big[0],
        big[1],
        channel[:, :CONV],
        channel[:, CONV],
        big[2],
        big[3],
        channel[:, CONV + 1 : CONV + 3],
        channel[:, CONV + 3],
        big[4],
        big[5],
        big[6],
        big[7],
    )


def solution(mesh):
    tokens = P(("rep", "seq"), None)
    rows = P(None, "seq", None)
    last3 = P(None, None, "seq")
    last2 = P(None, "seq")
    own_rows = P(None, ("rep", "seq"), None)
    own3 = P(None, None, ("rep", "seq"))
    own2 = P(None, ("rep", "seq"))

    def whole(*args):
        heads = args[9].shape[1] // args[9].shape[2]
        plan = Plan(mesh, heads)
        return jax.shard_map(
            partial(local, plan),
            mesh=mesh,
            in_specs=(
                tokens, tokens, P("rep"), P("rep"), last3, rows, rows, last3, last2, rows, rows,
                last3, last2, rows, rows, rows, rows,
            ),
            out_specs=(
                tokens, tokens, own3, own_rows, own_rows, own3, own2, own_rows, own_rows, own3,
                own2, own_rows, own_rows, own_rows, own_rows,
            ),
            check_vma=False,
        )(*args)

    return whole
```

```python
from functools import partial

import jax
import jax.numpy as jnp
from jax import lax
from jax.experimental import pallas as pl
from jax.experimental.pallas import tpu as pltpu
from jax.sharding import PartitionSpec as P

CONV = 4
LAYERS = 2
EPSILON = 1e-06
BF = jnp.bfloat16
F32 = jnp.float32


def dot(a, b):
    return jnp.dot(a, b, preferred_element_type=F32)


def dot_tn(a, b):
    return lax.dot_general(a, b, (((0,), (0,)), ((), ())), preferred_element_type=F32)


def dot_nt(a, b):
    return lax.dot_general(a, b, (((1,), (1,)), ((), ())), preferred_element_type=F32)


def glu_product(gate_in, value_in):
    return jax.nn.gelu(gate_in, approximate=True) * value_in


class Plan:
    def __init__(self, mesh, heads):
        self.rep = mesh.shape["rep"]
        self.seq = mesh.shape["seq"]
        self.tp = min(heads, self.rep)
        self.dp = self.rep // self.tp
        tp, dp = self.tp, self.dp
        self.tp_groups = None if dp == 1 else [[d * tp + t for t in range(tp)] for d in range(dp)]
        self.dp_groups = [[d * tp + t for d in range(dp)] for t in range(tp)]


def owner_chunks(plan, value):
    tp, seq = plan.tp, plan.seq
    pairs = []
    for d in range(plan.dp):
        for j in range(tp):
            for z in range(seq):
                o = tp * z + j
                pairs.append(((d * tp + j) * seq + z, (d * tp + o // seq) * seq + o % seq))
    return lax.ppermute(value, ("rep", "seq"), pairs)


def to_owners(plan, chunk, axis):
    if plan.dp == 1:
        return chunk
    part = lax.psum_scatter(
        chunk, "rep", scatter_dimension=axis, tiled=True, axis_index_groups=plan.dp_groups
    )
    tp, seq, dp = plan.tp, plan.seq, plan.dp
    pairs = [
        ((d * tp + t) * seq + z, (t * seq + z) * dp + d)
        for d in range(dp)
        for t in range(tp)
        for z in range(seq)
    ]
    return lax.ppermute(part, ("rep", "seq"), pairs)


MESH = pl.DeviceIdType.MESH
ANY = pl.BlockSpec(memory_space=pl.ANY)
VM = pl.BlockSpec(memory_space=pltpu.VMEM)
TP = 8
LATER = 3


class Net:
    def __init__(self):
        rep = lax.axis_index("rep")
        self.z = lax.axis_index("seq")
        self.t = lax.rem(rep, TP)
        self.base = rep - self.t
        chip = self.t // 2
        self.k = lax.rem(self.t, 2)
        self.b0 = lax.rem(chip, 2)
        self.b1 = chip // 2

    def slot(self, m, s):
        b0 = lax.rem(self.b0 + m % 2, 2)
        b1 = lax.rem(self.b1 + m // 2, 2)
        return (b1 * 2 + b0) * 2 + lax.rem(self.k + s, 2)

    def device(self, m, s):
        return (self.base + self.slot(m, s), self.z)

    def enter(self, extra=(), more=0):
        barrier = pltpu.get_barrier_semaphore()
        devices = [self.device(1, 0), self.device(2, 0), self.device(0, 1)] + list(extra)
        for device in devices:
            pl.semaphore_signal(barrier, inc=1, device_id=device, device_id_type=MESH)
        pl.semaphore_wait(barrier, len(devices) + more)


def remote(src, dst, send, recv, device):
    return pltpu.make_async_remote_copy(
        src_ref=src, dst_ref=dst, send_sem=send, recv_sem=recv, device_id=device,
        device_id_type=MESH,
    )


class Gather:
    def __init__(self, net, full, send, recv):
        self.net, self.full, self.send, self.recv = net, full, send, recv
        half = full.shape[1] // 2
        a, b, whole = pl.ds(0, half), pl.ds(half, half), pl.ds(0, 2 * half)
        x, y, sib = net.device(1, 0), net.device(2, 0), net.device(0, 1)
        self.plan = [
            (0, a, x, 1), (0, b, y, 2), (0, b, x, 1), (0, a, y, 2), (2, b, x, 3), (1, a, y, 3),
            (0, whole, sib, 0), (1, whole, sib, 1), (2, whole, sib, 2), (3, whole, sib, 3),
        ]

    def copy(self, i):
        m, rows, to, _ = self.plan[i]
        at = self.full.at[self.net.slot(m, 0), rows]
        return remote(at, at, self.send.at[i], self.recv.at[i], to)

    def arrived(self, i):
        _, rows, to, m = self.plan[i]
        at = self.full.at[self.net.slot(m, 0 if i < 6 else 1), rows]
        remote(at, at, self.send.at[i], self.recv.at[i], to).wait_recv()

    def begin(self):
        for i in (0, 1, 2, 3, 6):
            self.copy(i).start()

    def before(self, n):
        if n == 1:
            self.arrived(6)
        if n == 2:
            self.arrived(0)
            self.copy(5).start()
            self.arrived(1)
            self.copy(4).start()
            self.arrived(2)
            self.copy(7).start()
        if n == 3:
            self.arrived(7)
        if n == 4:
            self.arrived(3)
            self.copy(8).start()
        if n == 5:
            self.arrived(8)
        if n == 6:
            self.arrived(4)
            self.arrived(5)
            self.copy(9).start()
        if n == 7:
            self.arrived(9)

    def finish(self):
        for i in range(10):
            self.copy(i).wait_send()


class Scatter:
    def __init__(self, net, part, near, wide, far, send, recv):
        self.net, self.part, self.near = net, part, near
        self.wide, self.far, self.send, self.recv = wide, far, send, recv
        self.rows = part.shape[2]
        half = self.rows // 2
        a, b, whole = pl.ds(0, half), pl.ds(half, half), pl.ds(0, 2 * half)
        self.a, self.b = a, b
        x, y, sib = net.device(1, 0), net.device(2, 0), net.device(0, 1)
        self.plan = [
            (part.at[1, m], near.at[m], sib) for m in range(4)
        ] + [
            (part.at[0, 3, a], wide.at[0], x),
            (part.at[0, 3, b], wide.at[1], y),
            (part.at[0, 1, a], far.at[0, a], x),
            (part.at[0, 2, b], far.at[1, b], y),
            (part.at[0, 1, b], far.at[0, b], x),
            (part.at[0, 2, a], far.at[1, a], y),
        ]

    def copy(self, i):
        src, dst, to = self.plan[i]
        return remote(src, dst, self.send.at[i], self.recv.at[i], to)

    def add(self, m, start, count, other):
        def some(i, carry):
            at = pl.ds(pl.multiple_of(start + i * 64, 64), 64)
            from_at = pl.ds(pl.multiple_of(i * 64, 64), 64)
            total = self.part[0, m, at].astype(F32) + other[from_at].astype(F32)
            self.part[0, m, at] = total.astype(BF)
            return carry

        lax.fori_loop(0, count // 64, some, 0)

    def after(self, n):
        if n == 1:
            self.copy(0).start()
        if n == 3:
            self.copy(1).start()
        if n == 4:
            self.copy(1).wait_recv()
            self.add(1, 0, self.rows, self.near.at[1])
            self.copy(6).start()
        if n == 5:
            self.copy(2).start()
        if n == 6:
            self.copy(2).wait_recv()
            self.add(2, 0, self.rows, self.near.at[2])
            self.copy(7).start()
        if n == 7:
            self.copy(3).start()

    def corner(self):
        self.copy(3).wait_recv()
        self.add(3, 0, self.rows, self.near.at[3])
        self.copy(4).start()
        self.copy(5).start()

    def edges(self):
        half = self.rows // 2
        self.copy(4).wait_recv()
        self.add(2, 0, half, self.wide.at[0])
        self.copy(9).start()
        self.copy(5).wait_recv()
        self.add(1, half, half, self.wide.at[1])
        self.copy(8).start()
        self.copy(0).wait_recv()

    def finish(self):
        for i in (6, 7, 8, 9):
            self.copy(i).wait_recv()
        for i in range(10):
            self.copy(i).wait_send()

    def total(self, at):
        own = self.part[0, 0, at].astype(F32) + self.near[0, at].astype(F32)
        return own + self.far[0, at].astype(F32) + self.far[1, at].astype(F32)


def plane_scratch(rows, width):
    dma = pltpu.SemaphoreType.DMA
    return [
        pltpu.VMEM((TP, rows, width), BF),
        pltpu.VMEM((2, 4, rows, width), BF),
        pltpu.VMEM((4, rows, width), BF),
        pltpu.VMEM((2, rows // 2, width), BF),
        pltpu.VMEM((2, rows, width), BF),
        dma((10,)), dma((10,)), dma((10,)), dma((10,)),
    ]


def steps(gather, scatter, compute):
    def one(i, carry):
        for n in range(1, 2 * 4):
            @pl.when(i == n)
            def _():
                if gather is not None:
                    gather.before(n)

        compute(i // 2, lax.rem(i, 2))
        for n in range(2 * 4):
            @pl.when(i == n)
            def _():
                if scatter is not None:
                    scatter.after(n)

        return carry

    lax.fori_loop(0, 2 * 4, one, 0)


def end_forward(scatter, residual, gain, out, normed):
    rows, chunk = out.shape[0], 32

    def some(i, carry):
        at = pl.ds(pl.multiple_of(i * chunk, chunk), chunk)
        value = residual[at] + scatter.total(at)
        out[at] = value
        scale = lax.rsqrt(jnp.mean(value * value, axis=-1, keepdims=True) + EPSILON)
        normed[at] = (value * scale * gain[...]).astype(BF)
        return carry

    lax.fori_loop(0, rows // chunk, some, 0)


def end_backward(scatter, upstream, values, gain, grad, grad_low, grad_gain):
    rows, chunk = grad.shape[0], 32
    grad_gain[...] = jnp.zeros_like(grad_gain)

    def some(i, carry):
        at = pl.ds(pl.multiple_of(i * chunk, chunk), chunk)
        value, given = values[at], scatter.total(at)
        scale = lax.rsqrt(jnp.mean(value * value, axis=-1, keepdims=True) + EPSILON)
        scaled = given * gain[...]
        mean = jnp.mean(value * scaled, axis=-1, keepdims=True)
        result = upstream[at] + scale * scaled - value * (scale * scale * scale * mean)
        grad[at] = result
        grad_low[at] = result.astype(BF)
        grad_gain[...] += jnp.sum(given * value * scale, axis=0, keepdims=True)
        return carry

    lax.fori_loop(0, rows // chunk, some, 0)


GELU_A = 0.7978845608028654
GELU_B = 0.044715


def gelu_parts(v):
    square = v * v
    tanh = jnp.tanh(GELU_A * (v + GELU_B * v * square))
    half = 0.5 * (1.0 + tanh)
    slope = half + 0.5 * v * (1.0 - tanh * tanh) * (GELU_A * (1.0 + 3.0 * GELU_B * square))
    return v * half, slope


def copy_list(pairs, sem, first):
    return [
        pltpu.make_async_copy(src, dst, sem.at[first + n]) for n, (src, dst) in enumerate(pairs)
    ]


def unpack_rec(pack, col, wout, gates, sem, first):
    seq, both = pack.shape[0], pack.shape[2]
    rows, part = col.shape[0] // seq, gates.shape[0] // seq
    pairs = []
    for z in range(seq):
        pairs.append((pack.at[z, pl.ds(0, rows)], col.at[pl.ds(z * rows, rows)]))
        own = pl.ds(z * part, part)
        for j in range(3):
            pairs.append(
                (pack.at[z, pl.ds(rows + j * part, part)], wout.at[own, pl.ds(j * both, both)])
            )
        pairs.append((pack.at[z, pl.ds(rows + 3 * part, part)], gates.at[own]))
    return copy_list(pairs, sem, first)


def mlp_split(width, twice):
    rest = width - twice
    return rest, twice // rest


def unpack_mlp(pack, col, down, sem, first):
    seq, twice = pack.shape[0], pack.shape[2]
    rows, part = col.shape[0] // seq, down.shape[0] // seq
    rest, blocks = mlp_split(down.shape[1], twice)
    low = part // blocks
    pairs = []
    for z in range(seq):
        pairs.append((pack.at[z, pl.ds(0, rows)], col.at[pl.ds(z * rows, rows)]))
        pairs.append(
            (pack.at[z, pl.ds(rows, part)], down.at[pl.ds(z * part, part), pl.ds(0, twice)])
        )
        for n in range(blocks):
            pairs.append(
                (
                    pack.at[z, pl.ds(rows + part, low), pl.ds(n * rest, rest)],
                    down.at[pl.ds(z * part + n * low, low), pl.ds(twice, rest)],
                )
            )
    return copy_list(pairs, sem, first)


def mlp_forward_kernel(
    x_ref, residual_ref, gain_ref, pack_ref,
    out_ref, normed_ref, full_out, up_out,
    full, part, near, wide, far, gs, gr, ss, sr, col, wd, ups, sem,
):
    net = Net()
    gather = Gather(net, full, gs, gr)
    scatter = Scatter(net, part, near, wide, far, ss, sr)
    n = 5 * pack_ref.shape[0]
    own = pltpu.make_async_copy(x_ref, full.at[net.t], sem.at[n])
    own.start()
    weights = unpack_mlp(pack_ref, col, wd, sem, 0)
    for copy in weights:
        copy.start()
    net.enter()
    own.wait()
    gather.begin()
    for copy in weights:
        copy.wait()

    units = wd.shape[0]

    def compute(m, s):
        slot = net.slot(m, s)
        x = full[slot]
        up = dot(x, col[...])
        ups[slot] = up.astype(BF)
        hidden = glu_product(up[:, :units], up[:, units:]).astype(BF)
        part[s, m] = dot(hidden, wd[...]).astype(BF)

    steps(gather, scatter, compute)
    saves = [
        pltpu.make_async_copy(full, full_out, sem.at[n + 1]),
        pltpu.make_async_copy(ups, up_out, sem.at[n + 2]),
    ]
    for copy in saves:
        copy.start()
    scatter.corner()
    scatter.edges()
    scatter.finish()
    end_forward(scatter, residual_ref, gain_ref, out_ref, normed_ref)
    gather.finish()
    for copy in saves:
        copy.wait()


def mlp_forward(x, residual, gain, pack):
    rows, width = x.shape
    seq, _, twice = pack.shape
    shape = jax.ShapeDtypeStruct
    return pl.pallas_call(
        mlp_forward_kernel,
        in_specs=[ANY, VM, VM, ANY],
        out_specs=[VM, VM, ANY, ANY],
        out_shape=[
            shape((rows, width), F32),
            shape((rows, width), BF),
            shape((TP, rows, width), BF),
            shape((TP, rows, twice), BF),
        ],
        scratch_shapes=plane_scratch(rows, width)
        + [
            pltpu.VMEM((width, twice), BF),
            pltpu.VMEM((twice // 2, width), BF),
            pltpu.VMEM((TP, rows, twice), BF),
            pltpu.SemaphoreType.DMA((5 * seq + 4,)),
        ],
        compiler_params=pltpu.CompilerParams(
            collective_id=1, has_side_effects=True, vmem_limit_bytes=58 << 20
        ),
        cost_estimate=pl.CostEstimate(
            flops=60 * 10**9, bytes_accessed=30 << 20, transcendentals=0
        ),
        name="mlp_forward",
    )(x, residual, gain.reshape(1, -1), pack)


def mlp_backward_kernel(
    g_ref, upstream_ref, values_ref, gain_ref, pack_ref, x_ref, up_ref,
    grad_ref, low_ref, gain_out, gcol_ref,
    full, part, near, wide, far, gs, gr, ss, sr, col, wd, xs, ups, hid, sem,
):
    net = Net()
    gather = Gather(net, full, gs, gr)
    scatter = Scatter(net, part, near, wide, far, ss, sr)
    seq = pack_ref.shape[0]
    n = 5 * seq
    own = pltpu.make_async_copy(g_ref, full.at[net.t], sem.at[n])
    own.start()
    loads = unpack_mlp(pack_ref, col, wd, sem, 0) + [
        pltpu.make_async_copy(up_ref, ups, sem.at[n + 1]),
    ]
    late = pltpu.make_async_copy(x_ref, xs, sem.at[n + 3])
    for copy in loads + [late]:
        copy.start()
    net.enter()
    own.wait()
    gather.begin()
    for copy in loads:
        copy.wait()
    rows, units = full.shape[1], wd.shape[0]

    def compute(m, s):
        slot = net.slot(m, s)
        at = pl.ds(pl.multiple_of(slot * rows, rows), rows)
        grad_hidden = dot_nt(full[slot], wd[...])
        up = ups[at].astype(F32)
        act, slope = gelu_parts(up[:, :units])
        up_value = up[:, units:]
        hid[at] = (act * up_value).astype(BF)
        grads = jnp.concatenate([grad_hidden * up_value * slope, grad_hidden * act], 1).astype(BF)
        ups[at] = grads
        part[s, m] = dot_nt(grads, col[...]).astype(BF)

    steps(gather, scatter, compute)
    late.wait()
    scatter.corner()
    width = full.shape[2]
    own_rows = width // (TP * seq)
    tile = 2 * seq * own_rows
    base = width // seq

    def columns(j, carry):
        x = xs[:, pl.ds(pl.multiple_of(j * tile, 128), tile)]
        product = dot_tn(x, ups[...]).astype(BF)
        for r in range(2):
            for z in range(seq):
                low = (r * seq + z) * own_rows
                at = pl.ds(pl.multiple_of((2 * j + r) * own_rows, own_rows), own_rows)
                gcol_ref[z, at] = product[low : low + own_rows]
        return carry

    lax.fori_loop(0, TP // 2, columns, 0)
    scatter.edges()

    tokens = full.shape[0] * rows
    part_units = units // seq
    rest, blocks = mlp_split(width, 2 * units)
    low = part_units // blocks
    hidden = hid[...]
    for first in range(0, width, width // 2):
        at = pl.ds(first, width // 2)
        product = dot_tn(hidden, full[:, :, at].reshape(tokens, width // 2)).astype(BF)
        beside = min(2 * units - first, width // 2)
        for z in range(seq):
            own = product[z * part_units : (z + 1) * part_units]
            gcol_ref[z, base : base + part_units, first : first + beside] = own[:, :beside]
            if beside < width // 2:
                for n in range(blocks):
                    gcol_ref[z, base + part_units :, n * rest : (n + 1) * rest] = own[
                        n * low : (n + 1) * low, beside:
                    ]
    scatter.finish()
    end_backward(scatter, upstream_ref, values_ref, gain_ref, grad_ref, low_ref, gain_out)
    gather.finish()


def mlp_backward(g, upstream, values, gain, pack, x, up):
    rows, width = g.shape
    seq, _, twice = pack.shape
    tokens = TP * rows
    shape = jax.ShapeDtypeStruct
    return pl.pallas_call(
        mlp_backward_kernel,
        in_specs=[ANY, VM, VM, VM, ANY, ANY, ANY],
        out_specs=[VM, VM, VM, VM],
        out_shape=[
            shape((rows, width), F32),
            shape((rows, width), BF),
            shape((1, width), F32),
            shape(pack.shape, BF),
        ],
        scratch_shapes=plane_scratch(rows, width)
        + [
            pltpu.VMEM((width, twice), BF),
            pltpu.VMEM((twice // 2, width), BF),
            pltpu.VMEM((tokens, width), BF),
            pltpu.VMEM((tokens, twice), BF),
            pltpu.VMEM((tokens, twice // 2), BF),
            pltpu.SemaphoreType.DMA((5 * seq + 4,)),
        ],
        compiler_params=pltpu.CompilerParams(
            collective_id=2, has_side_effects=True, vmem_limit_bytes=60 << 20
        ),
        cost_estimate=pl.CostEstimate(
            flops=70 * 10**9, bytes_accessed=30 << 20, transcendentals=0
        ),
        name="mlp_backward",
    )(
        g, upstream, values, gain.reshape(1, -1), pack, x.reshape(tokens, width),
        up.reshape(tokens, twice),
    )


def after_corner_first(scatter, n):
    if n % 2 == 0:
        scatter.copy(3 - n // 2).start()
    if n == 3:
        scatter.corner()
    if n == 5:
        scatter.copy(2).wait_recv()
        scatter.add(2, 0, scatter.rows, scatter.near.at[2])
        scatter.copy(7).start()
    if n == 7:
        scatter.copy(1).wait_recv()
        scatter.add(1, 0, scatter.rows, scatter.near.at[1])
        scatter.copy(6).start()


class Line:
    def __init__(self, net, count):
        self.net, self.count = net, count
        self.others = [(net.base + net.t, lax.rem(net.z + d, count)) for d in range(1, count)]
        self.next = (net.base + net.t, net.z + 1)
        self.before = (net.base + net.t, net.z - 1)

    def to_all(self, ends, send, recv):
        at = ends.at[self.net.z]
        copies = [
            remote(at, at, send.at[d], recv.at[d], to) for d, to in enumerate(self.others)
        ]
        for copy in copies:
            copy.start()
        for d, copy in enumerate(copies):
            source = lax.rem(self.net.z + self.count - 1 - d, self.count)
            from_at = ends.at[source]
            remote(from_at, from_at, send.at[d], recv.at[d], self.others[d]).wait_recv()
        for copy in copies:
            copy.wait_send()


def inside_of(positions, offset, length):
    return jnp.where((positions >= offset) & (positions < offset + length), 1.0, 0.0)


def read_halves(ref, at):
    return jnp.concatenate([ref[n, at] for n in range(ref.shape[0])], 1)


def write_halves(ref, at, value):
    for n in range(ref.shape[0]):
        ref[n, at] = value[:, n * 128 : (n + 1) * 128]


def one_minus_exp(v):
    series = 1.0 + v * (1.0 / 7.0)
    for n in (6.0, 5.0, 4.0, 3.0, 2.0):
        series = 1.0 + v * (1.0 / n) * series
    return jnp.where(v > -0.35, -v * series, 1.0 - jnp.exp(v))


def sigmoid(v):
    return 1.0 / (1.0 + jnp.exp(-v))


def rec_forward_kernel(
    gathered,
    x_ref, residual_ref, gain_ref, pack_ref, small_ref, slots_ref,
    out_ref, normed_ref, full_out, branch_out, stream_out, conv_out, state_out,
    full, part, near, wide, far, gs, gr, ss, sr,
    col, gates, wout, branch, stream, conv, state, retain, inflow, ends, carry, hs, hr, es, er, sem,
):
    net = Net()
    seq = ends.shape[0]
    line = Line(net, seq)
    gather = Gather(net, full, gs, gr)
    scatter = Scatter(net, part, near, wide, far, ss, sr)
    rows = full.shape[1]
    head = gates.shape[0]
    own = pltpu.make_async_copy(x_ref, full if gathered else full.at[net.t], sem.at[0])
    loads = unpack_rec(pack_ref, col, wout, gates, sem, 9)
    for load in [own] + loads:
        load.start()
    net.enter(line.others)
    own.wait()
    if not gathered:
        gather.begin()

    @pl.when(net.z == 0)
    def _():
        stream[:, pl.ds(0, 8), :] = jnp.zeros((TP, 8, head), F32)

    for load in loads:
        load.wait()

    def halo(i):
        slot = net.slot(i // 2, lax.rem(i, 2))
        return remote(
            stream.at[slot, pl.ds(rows, 8)], stream.at[slot, pl.ds(0, 8)],
            hs.at[i], hr.at[i], line.next,
        )

    def project(i):
        slot = net.slot(i // 2, lax.rem(i, 2))
        both = dot(full[slot], col[...])
        branch[slot] = both[:, :head]
        stream[slot, pl.ds(8, rows)] = both[:, head:]

        @pl.when(net.z < seq - 1)
        def _():
            halo(i).start()

    def gate(i):
        slot = net.slot(i // 2, lax.rem(i, 2))

        @pl.when(net.z > 0)
        def _():
            halo(i).wait_recv()

        length, offset = slots_ref[slot, 0], slots_ref[slot, 1]
        positions = net.z * rows + lax.broadcasted_iota(jnp.int32, (rows, head), 0)
        inside = inside_of(positions, offset, length)
        mixed = small_ref[pl.ds(CONV, 1), :] + small_ref[pl.ds(0, 1), :] * stream[slot, pl.ds(8, rows)]
        restart = positions == 0
        for j in range(1, CONV):
            same = jnp.where(inside == inside_of(positions - j, offset, length), 1.0, 0.0)
            if j == 1:
                restart = restart | (same == 0.0)
            mixed += small_ref[pl.ds(j, 1), :] * stream[slot, pl.ds(8 - j, rows)] * same
        low = mixed.astype(BF)
        conv[slot] = low
        pre = dot(low, gates[...])
        rate = sigmoid(pre[:, :head] + small_ref[pl.ds(CONV + 1, 1), :])
        admit = sigmoid(pre[:, head:] + small_ref[pl.ds(CONV + 2, 1), :])
        log_retain = rate * small_ref[pl.ds(CONV + 3, 1), :]
        at = pl.ds(pl.multiple_of(slot * rows, rows), rows)
        write_halves(retain, at, jnp.where(restart, 0.0, jnp.exp(log_retain)))
        scale = jnp.where(restart, 1.0, jnp.sqrt(one_minus_exp(2.0 * log_retain)))
        write_halves(inflow, at, scale * admit * low.astype(F32))

    def one(i, _):
        for n in range(1, TP):
            @pl.when(i == n)
            def _():
                if not gathered:
                    gather.before(n)

        @pl.when(i < TP)
        def _():
            project(i)

        @pl.when(i >= LATER)
        def _():
            gate(i - LATER)

        return 0

    lax.fori_loop(0, TP + LATER, one, 0)
    saves = [
        pltpu.make_async_copy(branch, branch_out, sem.at[5]),
        pltpu.make_async_copy(stream, stream_out, sem.at[6]),
        pltpu.make_async_copy(conv, conv_out, sem.at[7]),
    ]
    if not gathered:
        saves.append(pltpu.make_async_copy(full, full_out, sem.at[4]))
    for save in saves:
        save.start()

    lanes = [pl.ds(i, 128) for i in range(0, head, 128)]

    def step(p, carried):
        at = pl.ds(p, TP, stride=rows)
        result = []
        for n, (value, decay) in enumerate(carried):
            a = retain[n, at]
            value = a * value + inflow[n, at]
            decay = a * decay
            inflow[n, at] = value
            retain[n, at] = decay
            result.append((value, decay))
        return tuple(result)

    start = tuple((jnp.zeros((TP, 128), F32), jnp.ones((TP, 128), F32)) for _ in lanes)
    last = lax.fori_loop(0, rows, step, start, unroll=8)
    for lane, (value, decay) in zip(lanes, last):
        ends[net.z, pl.ds(0, TP), lane] = decay
        ends[net.z, pl.ds(TP, TP), lane] = value
    line.to_all(ends, es, er)
    entering = jnp.zeros((TP, head), F32)
    for z in range(seq - 1):
        later = ends[z, pl.ds(0, TP)] * entering + ends[z, pl.ds(TP, TP)]
        entering = jnp.where(z < net.z, later, entering)
    carry[...] = entering

    def join(i, _):
        m, s = 3 - i // 2, 1 - lax.rem(i, 2)
        slot = net.slot(m, s)
        at = pl.ds(pl.multiple_of(slot * rows, rows), rows)
        first = carry[pl.ds(slot, 1), :]
        states = read_halves(inflow, at) + read_halves(retain, at) * first
        state[slot, pl.ds(0, 8)] = jnp.broadcast_to(first, (8, head))
        state[slot, pl.ds(8, rows)] = states
        joined = glu_product(branch[slot], states).astype(BF)
        part[s, m] = dot(joined, wout[...]).astype(BF)
        for n in range(TP):
            @pl.when(i == n)
            def _():
                after_corner_first(scatter, n)

        return 0

    lax.fori_loop(0, TP, join, 0)
    saves.append(pltpu.make_async_copy(state, state_out, sem.at[8]))
    saves[-1].start()
    scatter.edges()

    @pl.when(net.z < seq - 1)
    def _():
        lax.fori_loop(0, TP, lambda i, _: (halo(i).wait_send(), 0)[1], 0)

    scatter.finish()
    end_forward(scatter, residual_ref, gain_ref, out_ref, normed_ref)
    if not gathered:
        gather.finish()
    for save in saves:
        save.wait()


def rec_scratch(pack, width):
    seq, _, both = pack.shape
    return [
        pltpu.VMEM((width, both), BF),
        pltpu.VMEM((both // 2, both), BF),
        pltpu.VMEM((both // 2, width), BF),
    ]


def rec_forward(x, residual, gain, pack, small, slots):
    gathered = x.ndim == 3
    rows, width = residual.shape
    seq, _, head = pack.shape
    head = head // 2
    shape = jax.ShapeDtypeStruct
    dma = pltpu.SemaphoreType.DMA
    tokens = TP * rows
    result = list(pl.pallas_call(
        partial(rec_forward_kernel, gathered),
        in_specs=[ANY, VM, VM, ANY, VM, pl.BlockSpec(memory_space=pltpu.SMEM)],
        out_specs=[VM, VM, ANY, ANY, ANY, ANY, ANY],
        out_shape=[
            shape((rows, width), F32),
            shape((rows, width), BF),
            shape((8, 128) if gathered else (TP, rows, width), BF),
            shape((TP, rows, head), F32),
            shape((TP, rows + 8, head), F32),
            shape((TP, rows, head), BF),
            shape((TP, rows + 8, head), F32),
        ],
        scratch_shapes=plane_scratch(rows, width)
        + rec_scratch(pack, width)
        + [
            pltpu.VMEM((TP, rows, head), F32),
            pltpu.VMEM((TP, rows + 8, head), F32),
            pltpu.VMEM((TP, rows, head), BF),
            pltpu.VMEM((TP, rows + 8, head), F32),
            pltpu.VMEM((head // 128, tokens, 128), F32),
            pltpu.VMEM((head // 128, tokens, 128), F32),
            pltpu.VMEM((seq, 2 * TP, head), F32),
            pltpu.VMEM((TP, head), F32),
            dma((TP,)), dma((TP,)), dma((seq - 1,)), dma((seq - 1,)), dma((9 + 5 * seq,)),
        ],
        compiler_params=pltpu.CompilerParams(
            collective_id=5 if gathered else 3, has_side_effects=True, vmem_limit_bytes=58 << 20
        ),
        cost_estimate=pl.CostEstimate(
            flops=70 * 10**9, bytes_accessed=30 << 20, transcendentals=0
        ),
        name="rec_forward_first" if gathered else "rec_forward",
    )(x, residual, gain.reshape(1, -1), pack, small, slots))
    if gathered:
        result[2] = x
    return result


def rec_backward_kernel(
    g_ref, upstream_ref, values_ref, gain_ref, pack_ref, small_ref, slots_ref,
    x_ref, branch_ref, stream_ref, conv_ref, state_ref,
    grad_ref, low_ref, gain_out, gcol_ref, channel_ref,
    full, part, near, wide, far, gs, gr, ss, sr,
    col, gates, wout, xs, branch, stream, conv, state,
    retain, direct, suffix, joined, both, gpre, mixed, ends, carry, hs, hr, es, er, sem,
):
    net = Net()
    seq = ends.shape[0]
    line = Line(net, seq)
    gather = Gather(net, full, gs, gr)
    scatter = Scatter(net, part, near, wide, far, ss, sr)
    rows, width = full.shape[1], full.shape[2]
    head = gates.shape[0]
    own = pltpu.make_async_copy(g_ref, full.at[net.t], sem.at[0])
    loads = [
        pltpu.make_async_copy(a, b, sem.at[1 + n])
        for n, (a, b) in enumerate(
            (
                (branch_ref, branch), (state_ref, state), (conv_ref, conv), (stream_ref, stream),
                (x_ref, xs),
            )
        )
    ]
    loads = unpack_rec(pack_ref, col, wout, gates, sem, 9) + loads
    for load in [own] + loads:
        load.start()
    net.enter(line.others)
    own.wait()
    gather.begin()

    @pl.when(net.z == seq - 1)
    def _():
        mixed[:, pl.ds(rows, 8), :] = jnp.zeros((TP, 8, head), F32)

    channel_ref[...] = jnp.zeros_like(channel_ref)
    for load in loads[:-2]:
        load.wait()

    def gate_parts(slot):
        positions = net.z * rows + lax.broadcasted_iota(jnp.int32, (rows, head), 0)
        length, offset = slots_ref[slot, 0], slots_ref[slot, 1]
        inside = inside_of(positions, offset, length)
        restart = (positions == 0) | (inside != inside_of(positions - 1, offset, length))
        pre = dot(conv[slot], gates[...])
        rate = sigmoid(pre[:, :head] + small_ref[pl.ds(CONV + 1, 1), :])
        admit = sigmoid(pre[:, head:] + small_ref[pl.ds(CONV + 2, 1), :])
        log_retain = rate * small_ref[pl.ds(CONV + 3, 1), :]
        return positions, offset, length, inside, restart, rate, admit, log_retain

    def open_block(m, s):
        slot = net.slot(m, s)
        at = pl.ds(pl.multiple_of(slot * rows, rows), rows)
        grad_joined = dot_nt(full[slot], wout[...])
        act, slope = gelu_parts(branch[slot])
        states = state[slot, pl.ds(8, rows)]
        joined[at] = (act * states).astype(BF)
        both[at, :head] = (grad_joined * states * slope).astype(BF)
        write_halves(direct, at, grad_joined * act)
        _, _, _, _, restart, _, _, log_retain = gate_parts(slot)
        write_halves(retain, at, jnp.where(restart, 0.0, jnp.exp(log_retain)))

    steps(gather, None, open_block)
    lanes = [pl.ds(i, 128) for i in range(0, head, 128)]

    def step(i, carried):
        at = pl.ds(rows - 1 - i, TP, stride=rows)
        result = []
        for n, (value, decay, ahead) in enumerate(carried):
            value = ahead * value + direct[n, at]
            decay = ahead * decay
            direct[n, at] = value
            suffix[n, at] = decay
            result.append((value, decay, retain[n, at]))
        return tuple(result)

    one = jnp.minimum(retain[0, pl.ds(0, TP)] + 2.0, 1.0)
    last = lax.fori_loop(
        0, rows, step, tuple((jnp.zeros((TP, 128), F32), one, one) for _ in lanes), unroll=8
    )
    for lane, (value, decay, first) in zip(lanes, last):
        ends[net.z, pl.ds(0, TP), lane] = first * decay
        ends[net.z, pl.ds(TP, TP), lane] = first * value
    line.to_all(ends, es, er)
    entering = jnp.zeros((TP, head), F32)
    for z in range(seq - 1, 0, -1):
        earlier = ends[z, pl.ds(0, TP)] * entering + ends[z, pl.ds(TP, TP)]
        entering = jnp.where(z > net.z, earlier, entering)
    carry[...] = entering
    loads[-2].wait()

    def halo(i):
        slot = net.slot(3 - i // 2, 1 - lax.rem(i, 2))
        return remote(
            mixed.at[slot, pl.ds(0, 8)], mixed.at[slot, pl.ds(rows, 8)],
            hs.at[i], hr.at[i], line.before,
        )

    def through_gates(i):
        slot = net.slot(3 - i // 2, 1 - lax.rem(i, 2))
        at = pl.ds(pl.multiple_of(slot * rows, rows), rows)
        grad_states = read_halves(direct, at) + read_halves(suffix, at) * carry[pl.ds(slot, 1), :]
        positions, offset, length, inside, restart, rate, admit, log_retain = gate_parts(slot)
        low = conv[slot].astype(F32)
        kept = jnp.exp(log_retain)
        root = jnp.sqrt(one_minus_exp(2.0 * log_retain))
        scale = jnp.where(restart, 1.0, root)
        grad_admit = grad_states * scale * low
        grad_scale = grad_states * admit * low
        grad_log = grad_states * state[slot, pl.ds(7, rows)] * kept - grad_scale * kept * kept / root
        grad_log = jnp.where(restart, 0.0, grad_log)
        rate_part = grad_log * small_ref[pl.ds(CONV + 3, 1), :] * rate * (1.0 - rate)
        admit_part = grad_admit * admit * (1.0 - admit)
        gpre[at, :head] = rate_part.astype(BF)
        gpre[at, head:] = admit_part.astype(BF)
        grad_mixed = grad_states * scale * admit + dot_nt(gpre[at], gates[...])
        mixed[slot, pl.ds(0, rows)] = grad_mixed

        @pl.when(net.z > 0)
        def _():
            halo(i).start()

        sums = [jnp.sum(grad_mixed * stream[slot, pl.ds(8, rows)], axis=0, keepdims=True)]
        for j in range(1, CONV):
            same = jnp.where(inside == inside_of(positions - j, offset, length), 1.0, 0.0)
            sums.append(
                jnp.sum(
                    grad_mixed * stream[slot, pl.ds(8 - j, rows)] * same, axis=0, keepdims=True
                )
            )
        for term in (grad_mixed, rate_part, admit_part, grad_log * rate):
            sums.append(jnp.sum(term, axis=0, keepdims=True))
        for n, term in enumerate(sums):
            channel_ref[pl.ds(n, 1), :] += term

    def to_input(i):
        m, s = 3 - i // 2, 1 - lax.rem(i, 2)
        slot = net.slot(m, s)
        at = pl.ds(pl.multiple_of(slot * rows, rows), rows)

        @pl.when(net.z < seq - 1)
        def _():
            halo(i).wait_recv()

        positions = net.z * rows + lax.broadcasted_iota(jnp.int32, (rows, head), 0)
        length, offset = slots_ref[slot, 0], slots_ref[slot, 1]
        inside = inside_of(positions, offset, length)
        grad_stream = small_ref[pl.ds(0, 1), :] * mixed[slot, pl.ds(0, rows)]
        for j in range(1, CONV):
            same = jnp.where(inside == inside_of(positions + j, offset, length), 1.0, 0.0)
            grad_stream += small_ref[pl.ds(j, 1), :] * mixed[slot, pl.ds(j, rows)] * same
        both[at, head:] = grad_stream.astype(BF)
        part[s, m] = dot_nt(both[at], col[...]).astype(BF)

    def one_block(i, _):
        @pl.when(i < TP)
        def _():
            through_gates(i)

        @pl.when(i >= LATER)
        def _():
            to_input(i - LATER)

        for n in range(TP):
            @pl.when(i == n + LATER)
            def _():
                after_corner_first(scatter, n)

        return 0

    lax.fori_loop(0, TP + LATER, one_block, 0)
    scatter.edges()
    loads[-1].wait()
    own_rows = width // (TP * seq)
    tile = 2 * seq * own_rows

    def columns(j, _):
        x = xs[:, pl.ds(pl.multiple_of(j * tile, 128), tile)]
        product = dot_tn(x, both[...]).astype(BF)
        for r in range(2):
            for z in range(seq):
                low = (r * seq + z) * own_rows
                at = pl.ds(pl.multiple_of((2 * j + r) * own_rows, own_rows), own_rows)
                gcol_ref[z, at] = product[low : low + own_rows]
        return 0

    lax.fori_loop(0, TP // 2, columns, 0)
    low_conv = conv[...].reshape(TP * rows, head)
    product = dot_tn(low_conv, gpre[...]).astype(BF)
    third, base, part_head = width // 3, width // seq, head // seq
    for z in range(seq):
        low = base + 3 * part_head
        gcol_ref[z, low : low + part_head] = product[z * part_head : (z + 1) * part_head]
    for j in range(3):
        at = pl.ds(j * third, third)
        product = dot_tn(joined[...], full[:, :, at].reshape(TP * rows, third)).astype(BF)
        for z in range(seq):
            low = base + j * part_head
            gcol_ref[z, low : low + part_head] = product[z * part_head : (z + 1) * part_head]

    @pl.when(net.z > 0)
    def _():
        lax.fori_loop(0, TP, lambda i, _: (halo(i).wait_send(), 0)[1], 0)

    scatter.finish()
    end_backward(scatter, upstream_ref, values_ref, gain_ref, grad_ref, low_ref, gain_out)
    gather.finish()


def rec_backward(g, upstream, values, gain, pack, small, slots, saved):
    rows, width = g.shape
    seq, _, head = pack.shape
    head = head // 2
    tokens = TP * rows
    shape = jax.ShapeDtypeStruct
    dma = pltpu.SemaphoreType.DMA
    x, branch, stream, conv, state = saved
    return pl.pallas_call(
        rec_backward_kernel,
        in_specs=[ANY, VM, VM, VM, ANY, VM, pl.BlockSpec(memory_space=pltpu.SMEM)]
        + [ANY] * 5,
        out_specs=[VM] * 5,
        out_shape=[
            shape((rows, width), F32),
            shape((rows, width), BF),
            shape((1, width), F32),
            shape(pack.shape, BF),
            shape((8, head), F32),
        ],
        scratch_shapes=plane_scratch(rows, width)
        + rec_scratch(pack, width)
        + [
            pltpu.VMEM((tokens, width), BF),
            pltpu.VMEM(branch.shape, F32),
            pltpu.VMEM(stream.shape, F32),
            pltpu.VMEM(conv.shape, BF),
            pltpu.VMEM(state.shape, F32),
            pltpu.VMEM((head // 128, tokens, 128), F32),
            pltpu.VMEM((head // 128, tokens, 128), F32),
            pltpu.VMEM((head // 128, tokens, 128), F32),
            pltpu.VMEM((tokens, head), BF),
            pltpu.VMEM((tokens, 2 * head), BF),
            pltpu.VMEM((tokens, 2 * head), BF),
            pltpu.VMEM((TP, rows + 8, head), F32),
            pltpu.VMEM((seq, 2 * TP, head), F32),
            pltpu.VMEM((TP, head), F32),
            dma((TP,)), dma((TP,)), dma((seq - 1,)), dma((seq - 1,)), dma((9 + 5 * seq,)),
        ],
        compiler_params=pltpu.CompilerParams(
            collective_id=4, has_side_effects=True, vmem_limit_bytes=60 << 20
        ),
        cost_estimate=pl.CostEstimate(
            flops=80 * 10**9, bytes_accessed=30 << 20, transcendentals=0
        ),
        name="rec_backward",
    )(
        g, upstream, values, gain.reshape(1, -1), pack, small, slots,
        x.reshape(tokens, width), branch, stream, conv, state,
    )


def open_kernel(
    x_ref, small_ref, gain_ref, slot_ref, pack_ref, col_ref, rows_ref, later_ref,
    small_out, gain_out, slot_out, full_out, pack_out, mlp_out, later_out,
    full, smalls, gains, slots, gs, gr, ps, pr, sem,
):
    net = Net()
    seq = smalls.shape[0]
    line = Line(net, seq)
    gather = Gather(net, full, gs, gr)
    plane = [net.device(m, s) for m in range(4) for s in range(2)][1:]
    mine = [
        pltpu.make_async_copy(small_ref, smalls.at[net.z], sem.at[0]),
        pltpu.make_async_copy(gain_ref, gains.at[net.z], sem.at[1]),
        pltpu.make_async_copy(slot_ref, slots.at[net.t], sem.at[2]),
    ]
    col_rows = col_ref.shape[0]
    below = mlp_out.at[pl.ds(col_rows, rows_ref.shape[0])]
    here = [
        pltpu.make_async_copy(pack_ref, pack_out.at[net.z], sem.at[4]),
        pltpu.make_async_copy(col_ref, mlp_out.at[pl.ds(0, col_rows)], sem.at[5]),
    ]
    for copy in mine + here:
        copy.start()
    held, owned = TP * net.z + net.t, seq * net.t + net.z
    owner, giver = (held // seq, lax.rem(held, seq)), (lax.rem(owned, TP), owned // TP)
    away = held != owned
    barrier = pltpu.get_barrier_semaphore()

    @pl.when(away)
    def _():
        for t, z in (owner, giver):
            pl.semaphore_signal(barrier, inc=1, device_id=(net.base + t, z), device_id_type=MESH)
    net.enter(
        line.others + [net.device(1, 1), net.device(2, 1), net.device(3, 0), net.device(3, 1)],
        jnp.where(away, 2, 0),
    )
    for copy in mine:
        copy.wait()

    sends, arrivals = [], []

    def push(ref, own, source, to):
        n = len(sends)
        at, from_at = ref.at[own], ref.at[source]
        sends.append(remote(at, at, ps.at[n], pr.at[n], to))
        arrivals.append(remote(from_at, from_at, ps.at[n], pr.at[n], to))

    for ref in (gains, smalls):
        for d, to in enumerate(line.others):
            push(ref, net.z, lax.rem(net.z + seq - 1 - d, seq), to)
    for n, to in enumerate(plane):
        m, s = (n + 1) // 2, (n + 1) % 2
        push(slots, net.t, net.slot(m, s), to)
    for copy in sends:
        copy.start()
    first = len(sends)

    def hop(way, e):
        n = first + 2 * e + (0 if way > 0 else 1)
        to = (net.base + net.t, net.z + way)
        at = pack_ref if e == 0 else pack_out.at[net.z - way * e]
        lands = pack_out.at[net.z - way * e]
        return remote(at, lands, ps.at[n], pr.at[n], to)

    def forward(way, e):
        place = net.z if way > 0 else seq - 1 - net.z

        @pl.when((place >= e) & (place < seq - 1))
        def _():
            if e > 0:
                landed(way, e - 1)
            hop(way, e).start()

        if e > 0:
            @pl.when((place >= e) & (place == seq - 1))
            def _():
                landed(way, e - 1)

    def landed(way, e):
        n = first + 2 * e + (0 if way > 0 else 1)
        from_at = pack_out.at[net.z - way * (e + 1)]
        remote(from_at, from_at, ps.at[n], pr.at[n], (net.base + net.t, net.z)).wait_recv()

    def last(way):
        place = net.z if way > 0 else seq - 1 - net.z

        @pl.when(place == seq - 1)
        def _():
            landed(way, seq - 2)

        for e in range(seq - 1):
            @pl.when((place >= e) & (place < seq - 1))
            def _():
                hop(way, e).wait_send()

    forward(1, 0)
    forward(-1, 0)
    n = first + 2 * (seq - 1)
    owner_id = (net.base + owner[0], owner[1])
    moved = [
        remote(rows_ref, below, ps.at[n], pr.at[n], owner_id),
        remote(later_ref, later_out, ps.at[n + 1], pr.at[n + 1], owner_id),
    ]
    kept = [
        pltpu.make_async_copy(rows_ref, below, sem.at[6]),
        pltpu.make_async_copy(later_ref, later_out, sem.at[7]),
    ]

    @pl.when(away)
    def _():
        for copy in moved:
            copy.start()

    @pl.when(held == owned)
    def _():
        for copy in kept:
            copy.start()

    for copy in arrivals[: seq - 1]:
        copy.wait_recv()
    rows, width = x_ref.shape
    part, chunk = width // seq, 32

    def norm(i, _):
        at = pl.ds(pl.multiple_of(i * chunk, chunk), chunk)
        value = x_ref[at].astype(F32)
        scale = lax.rsqrt(jnp.mean(value * value, axis=-1, keepdims=True) + EPSILON)
        for z in range(seq):
            low = z * part
            full[net.t, at, low : low + part] = (
                value[:, low : low + part] * scale * gains[z, pl.ds(0, 1), :]
            ).astype(BF)
        return 0

    lax.fori_loop(0, rows // chunk, norm, 0)
    gather.begin()
    for copy in arrivals[seq - 1 :]:
        copy.wait_recv()
    saves = [
        pltpu.make_async_copy(a, b, sem.at[n])
        for n, (a, b) in enumerate(((smalls, small_out), (gains, gain_out), (slots, slot_out)))
    ]
    for save in saves:
        save.start()
    for n in range(1, TP):
        gather.before(n)
        if n == 2:
            forward(1, 1)
            forward(-1, 1)
    gather.finish()
    saves.append(pltpu.make_async_copy(full, full_out, sem.at[3]))
    saves[-1].start()
    for e in range(2, seq - 1):
        forward(1, e)
        forward(-1, e)
    last(1)
    last(-1)

    @pl.when(away)
    def _():
        for copy in moved:
            copy.wait()

    @pl.when(held == owned)
    def _():
        for copy in kept:
            copy.wait()

    for copy in sends:
        copy.wait_send()
    for copy in here:
        copy.wait()
    for save in saves:
        save.wait()


def opening(seq, x, small, gain, slot, pack, col, below, later):
    rows, width = x.shape
    shape = jax.ShapeDtypeStruct
    dma = pltpu.SemaphoreType.DMA
    pushes = 4 * (seq - 1) + TP - 1 + 2
    return pl.pallas_call(
        open_kernel,
        in_specs=[VM] + [ANY] * 7,
        out_specs=[ANY] * 7,
        out_shape=[
            shape((seq,) + small.shape, F32),
            shape((seq,) + gain.shape, F32),
            shape((TP,) + slot.shape, jnp.int32),
            shape((TP, rows, width), BF),
            shape((seq,) + pack.shape, BF),
            shape((col.shape[0] + below.shape[0], col.shape[1]), BF),
            shape(later.shape, BF),
        ],
        scratch_shapes=[
            pltpu.VMEM((TP, rows, width), BF),
            pltpu.VMEM((seq,) + small.shape, F32),
            pltpu.VMEM((seq,) + gain.shape, F32),
            pltpu.VMEM((TP,) + slot.shape, jnp.int32),
            dma((10,)), dma((10,)), dma((pushes,)), dma((pushes,)), dma((8,)),
        ],
        compiler_params=pltpu.CompilerParams(
            collective_id=6, has_side_effects=True, vmem_limit_bytes=40 << 20
        ),
        cost_estimate=pl.CostEstimate(
            flops=40 * 10**9, bytes_accessed=10 << 20, transcendentals=0
        ),
        name="opening",
    )(x, small, gain, slot, pack, col, below, later)


def close_kernel(
    gain_ref, channel_ref, *refs
):
    count = (len(refs) - 8) // 2
    blocks, (gain_out, channel_out), moved = refs[:count], refs[count : count + 2], refs[
        count + 2 : 2 * count + 2
    ]
    plane_gain, line_gain, line_channel, ps, pr, sem = refs[2 * count + 2 :]
    net = Net()
    seq = line_gain.shape[0]
    line = Line(net, seq)
    plane = [net.device(m, s) for m in range(4) for s in range(2)][1:]
    slots = [net.slot(m, s) for m in range(4) for s in range(2)][1:]
    own = [
        pltpu.make_async_copy(block.at[net.t], out.at[net.t], sem.at[n])
        for n, (block, out) in enumerate(zip(blocks, moved))
    ]
    plane_gain[net.t] = gain_ref[...]
    line_channel[net.z] = channel_ref[...]
    for copy in own:
        copy.start()
    net.enter(line.others + [net.device(1, 1), net.device(2, 1), net.device(3, 0), net.device(3, 1)])
    used = []

    def push(src, dst, landed, to):
        n = len(used)
        used.append(remote(src, dst, ps.at[n], pr.at[n], to))
        used[-1].start()
        return remote(src, landed, ps.at[n], pr.at[n], to)

    gains = [
        push(plane_gain.at[net.t], plane_gain.at[net.t], plane_gain.at[slot], to)
        for slot, to in zip(slots, plane)
    ]
    sources = [lax.rem(net.z + seq - 1 - d, seq) for d in range(seq - 1)]
    rest = [
        push(line_channel.at[net.z], line_channel.at[net.z], line_channel.at[source], to)
        for source, to in zip(sources, line.others)
    ]
    for block, out in zip(blocks, moved):
        for slot, to in zip(slots, plane):
            rest.append(push(block.at[slot], out.at[net.t], out.at[slot], to))
    for copy in gains:
        copy.wait_recv()
    total = plane_gain[0]
    for t in range(1, TP):
        total += plane_gain[t]
    line_gain[net.z] = total
    for source, to in zip(sources, line.others):
        rest.append(push(line_gain.at[net.z], line_gain.at[net.z], line_gain.at[source], to))
    for copy in rest:
        copy.wait_recv()
    total, channel = line_gain[0], line_channel[0]
    for z in range(1, seq):
        total += line_gain[z]
        channel += line_channel[z]
    gain_out[...] = total
    channel_out[...] = channel
    for copy in used:
        copy.wait_send()
    for copy in own:
        copy.wait()


def closing(seq, gains, channels, blocks):
    shape = jax.ShapeDtypeStruct
    dma = pltpu.SemaphoreType.DMA
    pushes = (TP - 1) * (1 + len(blocks)) + 2 * (seq - 1)
    return pl.pallas_call(
        close_kernel,
        in_specs=[VM, VM] + [ANY] * len(blocks),
        out_specs=[VM, VM] + [ANY] * len(blocks),
        out_shape=[shape(gains.shape, F32), shape(channels.shape, F32)]
        + [shape(block.shape, block.dtype) for block in blocks],
        scratch_shapes=[
            pltpu.VMEM((TP,) + gains.shape, F32),
            pltpu.VMEM((seq,) + gains.shape, F32),
            pltpu.VMEM((seq,) + channels.shape, F32),
            dma((pushes,)), dma((pushes,)), dma((len(blocks),)),
        ],
        compiler_params=pltpu.CompilerParams(
            collective_id=7, has_side_effects=True, vmem_limit_bytes=40 << 20
        ),
        cost_estimate=pl.CostEstimate(
            flops=40 * 10**9, bytes_accessed=10 << 20, transcendentals=0
        ),
        name="closing",
    )(gains, channels, *blocks)


def layer_backward(upstream, upstream_low, w, saved, slots, pending):
    residual, kept, middle, kept_two = saved
    pending_mlp, pending_rec = pending
    upstream_low, pending_mlp = lax.optimization_barrier((upstream_low, pending_mlp))
    grad_middle, mid_low, grad_gain_two, g_mlp = mlp_backward(
        upstream_low, upstream, middle, w["gain"][1], w["mlp"], *kept_two
    )
    mlp_share = over_seq(g_mlp)
    mid_low, pending_rec = lax.optimization_barrier((mid_low, pending_rec))
    grad, grad_low, grad_gain_one, g_rec, channel = rec_backward(
        mid_low, grad_middle, residual, w["gain"][0], w["rec"], w["small"], slots, kept
    )
    g_rec, mlp_share = lax.optimization_barrier((g_rec, mlp_share))
    rec_share = over_seq(g_rec)
    slope = 8.0 * jax.nn.sigmoid(-w["decay"])
    channel = jnp.concatenate([channel[:7], channel[7:] * slope], 0)
    gains = jnp.concatenate([grad_gain_one, grad_gain_two], 0)
    return grad, grad_low, (mlp_share, rec_share), channel, gains, (pending_mlp, pending_rec)


def over_seq(value):
    return lax.psum_scatter(value, "seq", scatter_dimension=0, tiled=False)


def columns(parts):
    return jnp.moveaxis(parts, 0, 1).reshape(parts.shape[1], -1)


def owned_grads(plan, mlp_share, rec_share, mlp, rec, width, head, units):
    base = width // plan.seq
    h, u = head // plan.seq, units // plan.seq
    out = [rec_share[base + i * h : base + (i + 1) * h] for i in range(3)]
    gates = rec_share[base + 3 * h :]
    rest, blocks = mlp_split(width, 2 * units)
    down = [mlp_share[base + u :, i * rest : (i + 1) * rest] for i in range(blocks)]
    grads = [
        columns(rec[:, :, :head]),
        columns(rec[:, :, head:]),
        gates[:, :head],
        gates[:, head:],
        jnp.concatenate(out, 1),
        columns(mlp[:, :, :units]),
        columns(mlp[:, :, units:]),
        jnp.concatenate([mlp_share[base : base + u], jnp.concatenate(down, 0)], 1),
    ]
    return [to_owners(plan, g.astype(F32), 0) for g in grads]


def local(plan, *args):
    (
        block_input, cotangent, lengths, offsets, norm_gains, branch_proj, stream_proj, conv_kernel,
        conv_bias, rate_proj, admit_proj, gate_bias, decay_logit, out_proj, mlp_gate, mlp_up,
        mlp_down,
    ) = args
    tp, dp, seq = plan.tp, plan.dp, plan.seq
    t = lax.axis_index("rep") % tp
    z = lax.axis_index("seq")
    rows = block_input.shape[0]
    head = branch_proj.shape[2] // tp
    units = mlp_gate.shape[2] // tp

    channels = conv_kernel.shape[2]
    small = jnp.concatenate([conv_kernel, conv_bias[:, None], gate_bias, decay_logit[:, None]], 1)
    small = small.reshape(LAYERS * 8, channels).astype(F32)
    slot = jnp.pad(jnp.stack([lengths, offsets], 1), ((0, 7), (0, 126)))
    def col(weight, layer, width, t):
        size = (1, weight.shape[1], width)
        return lax.dynamic_slice(weight, (layer, 0, t * width), size)[0]

    def chunk(weight, layer, t):
        size = weight.shape[1] // tp
        return lax.dynamic_slice(weight, (layer, t * size, 0), (1, size, weight.shape[2]))[0]

    def below(rows, twice):
        rest, blocks = mlp_split(rows.shape[1], twice)
        low = rows.shape[0] // blocks
        side = [rows[i * low : (i + 1) * low, twice:] for i in range(blocks)]
        return jnp.concatenate([rows[:, :twice], jnp.concatenate(side, 1)], 0)

    def rec_rows(l, t):
        out = chunk(out_proj, l, t)
        gates = jnp.concatenate([chunk(rate_proj, l, t), chunk(admit_proj, l, t)], 1)
        out = [out[:, i * 2 * head : (i + 1) * 2 * head] for i in range(3)] + [gates]
        return jnp.concatenate(out, 0)

    def rec_pack(l, rows_of, t):
        rec = jnp.concatenate([col(branch_proj, l, head, t), col(stream_proj, l, head, t)], 1)
        return jnp.concatenate([rec, rows_of], 0)

    def mlp_rows(l, t):
        return below(chunk(mlp_down, l, t), 2 * units)

    def mlp_cols(l, t):
        return jnp.concatenate([col(mlp_gate, l, units, t), col(mlp_up, l, units, t)], 1)

    pack = rec_pack(0, owner_chunks(plan, rec_rows(0, t)), t)
    smalls, gains, layout, normed, rec, mlp, rec_owned = opening(
        seq, block_input, small, norm_gains.reshape(2 * LAYERS, -1).astype(F32), slot, pack,
        mlp_cols(0, t), mlp_rows(0, t), rec_rows(1, t),
    )
    mlp, rec = lax.optimization_barrier((mlp, rec))
    layout = layout[:, 0, :2]
    gains = jnp.moveaxis(gains, 0, 1).reshape(LAYERS, 2, -1)
    smalls = jnp.moveaxis(smalls, 0, 1).reshape(LAYERS, 8, -1)
    smalls = lax.dynamic_slice_in_dim(smalls, t * head, head, 2)


    residual = block_input.astype(F32)
    saved_all, weights = [], []
    for l in range(LAYERS):
        if l > 0:
            mlp_owned, t, normed = lax.optimization_barrier((mlp_owned, t, normed))
            mlp = jnp.concatenate([mlp_cols(l, t), mlp_owned], 0)
        w = dict(
            gain=gains[l],
            small=jnp.concatenate([smalls[l, :7], -8.0 * jax.nn.softplus(-smalls[l, 7:])], 0),
            decay=smalls[l, 7:],
            rec=rec,
            mlp=lax.all_gather(mlp, "seq"),
        )
        weights.append(w)
        kept = rec_forward(normed, residual, w["gain"][1], w["rec"], w["small"], layout)
        middle, normed_two, *kept = kept
        if l + 1 < LAYERS:
            rows_of, t, normed_two = lax.optimization_barrier((rec_owned, t, normed_two))
            rec = lax.all_gather(rec_pack(l + 1, rows_of, t), "seq")
            mlp_owned = owner_chunks(plan, mlp_rows(l + 1, t))
        output, normed, *kept_two = mlp_forward(
            normed_two, middle, gains[(l + 1) % LAYERS, 0], w["mlp"]
        )
        saved_all.append((residual, kept, middle, kept_two))
        residual = output
    positions = z * rows + jnp.arange(rows, dtype=jnp.int32)
    inside = (positions >= offsets[0]) & (positions < offsets[0] + lengths[0])
    gradient = cotangent.astype(F32) * inside.astype(F32)[:, None]

    gradient_low = gradient.astype(BF)
    shares = [None] * LAYERS
    channel_all, gain_all = [None] * LAYERS, [None] * LAYERS
    for l in reversed(range(LAYERS)):
        gradient, gradient_low, shares[l], channel_all[l], gain_all[l], pending = layer_backward(
            gradient, gradient_low, weights[l], saved_all[l], layout,
            ((), ()) if l + 1 == LAYERS else shares[l + 1],
        )
        if l + 1 < LAYERS:
            shares[l + 1] = pending
    width = block_input.shape[1]
    base = width // seq

    def by_slot(share):
        return share[:base].reshape(tp, -1, share.shape[1])

    blocks = [by_slot(shares[l][0]) for l in range(LAYERS)]
    blocks += [by_slot(shares[l][1]) for l in range(1, LAYERS)]
    gains, channel, *blocks = closing(
        seq, jnp.concatenate(gain_all, 0), jnp.concatenate(channel_all, 0), blocks
    )
    last = lax.all_to_all(
        by_slot(shares[0][1]), "rep", split_axis=0, concat_axis=0, axis_index_groups=plan.tp_groups
    )
    mlps, recs = blocks[:LAYERS], [last] + blocks[LAYERS:]
    outs = [
        owned_grads(plan, *shares[l], mlps[l], recs[l], width, head, units) for l in range(LAYERS)
    ]
    big = [jnp.stack([outs[l][i] for l in range(LAYERS)]) for i in range(8)]

    channel = lax.dynamic_slice_in_dim(channel, z * (head // seq), head // seq, 1)
    channel = to_owners(plan, channel, 1).reshape(LAYERS, 8, -1)
    if dp > 1:
        gains = lax.psum(gains, "rep", axis_index_groups=plan.dp_groups)
    own = gains.shape[1] // (plan.rep * seq)
    owner = lax.axis_index(("rep", "seq"))
    gains = lax.dynamic_slice_in_dim(gains, owner * own, own, 1).reshape(LAYERS, 2, own)
    return (
        residual.astype(BF),
        gradient,
        gains,
        big[0],
        big[1],
        channel[:, :CONV],
        channel[:, CONV],
        big[2],
        big[3],
        channel[:, CONV + 1 : CONV + 3],
        channel[:, CONV + 3],
        big[4],
        big[5],
        big[6],
        big[7],
    )


def solution(mesh):
    tokens = P(("rep", "seq"), None)
    rows = P(None, "seq", None)
    last3 = P(None, None, "seq")
    last2 = P(None, "seq")
    own_rows = P(None, ("rep", "seq"), None)
    own3 = P(None, None, ("rep", "seq"))
    own2 = P(None, ("rep", "seq"))

    def whole(*args):
        heads = args[9].shape[1] // args[9].shape[2]
        plan = Plan(mesh, heads)
        return jax.shard_map(
            partial(local, plan),
            mesh=mesh,
            in_specs=(
                tokens, tokens, P("rep"), P("rep"), last3, rows, rows, last3, last2, rows, rows,
                last3, last2, rows, rows, rows, rows,
            ),
            out_specs=(
                tokens, tokens, own3, own_rows, own_rows, own3, own2, own_rows, own_rows, own3,
                own2, own_rows, own_rows, own_rows, own_rows,
            ),
            check_vma=False,
        )(*args)

    return whole
```

```python
from functools import partial

import jax
import jax.numpy as jnp
from jax import lax
from jax.experimental import pallas as pl
from jax.experimental.pallas import tpu as pltpu
from jax.sharding import PartitionSpec as P

CONV = 4
LAYERS = 2
EPSILON = 1e-06
BF = jnp.bfloat16
F32 = jnp.float32


def dot(a, b):
    return jnp.dot(a, b, preferred_element_type=F32)


def dot_tn(a, b):
    return lax.dot_general(a, b, (((0,), (0,)), ((), ())), preferred_element_type=F32)


def dot_nt(a, b):
    return lax.dot_general(a, b, (((1,), (1,)), ((), ())), preferred_element_type=F32)


def glu_product(gate_in, value_in):
    return jax.nn.gelu(gate_in, approximate=True) * value_in


class Plan:
    def __init__(self, mesh, heads):
        self.rep = mesh.shape["rep"]
        self.seq = mesh.shape["seq"]
        self.tp = min(heads, self.rep)
        self.dp = self.rep // self.tp
        tp, dp = self.tp, self.dp
        self.tp_groups = None if dp == 1 else [[d * tp + t for t in range(tp)] for d in range(dp)]
        self.dp_groups = [[d * tp + t for d in range(dp)] for t in range(tp)]


def owner_chunks(plan, value):
    tp, seq = plan.tp, plan.seq
    pairs = []
    for d in range(plan.dp):
        for j in range(tp):
            for z in range(seq):
                o = tp * z + j
                pairs.append(((d * tp + j) * seq + z, (d * tp + o // seq) * seq + o % seq))
    return lax.ppermute(value, ("rep", "seq"), pairs)


def to_owners(plan, chunk, axis):
    if plan.dp == 1:
        return chunk
    part = lax.psum_scatter(
        chunk, "rep", scatter_dimension=axis, tiled=True, axis_index_groups=plan.dp_groups
    )
    tp, seq, dp = plan.tp, plan.seq, plan.dp
    pairs = [
        ((d * tp + t) * seq + z, (t * seq + z) * dp + d)
        for d in range(dp)
        for t in range(tp)
        for z in range(seq)
    ]
    return lax.ppermute(part, ("rep", "seq"), pairs)


MESH = pl.DeviceIdType.MESH
ANY = pl.BlockSpec(memory_space=pl.ANY)
VM = pl.BlockSpec(memory_space=pltpu.VMEM)
TP = 8
LATER = 3


class Net:
    def __init__(self):
        rep = lax.axis_index("rep")
        self.z = lax.axis_index("seq")
        self.t = lax.rem(rep, TP)
        self.base = rep - self.t
        chip = self.t // 2
        self.k = lax.rem(self.t, 2)
        self.b0 = lax.rem(chip, 2)
        self.b1 = chip // 2

    def slot(self, m, s):
        b0 = lax.rem(self.b0 + m % 2, 2)
        b1 = lax.rem(self.b1 + m // 2, 2)
        return (b1 * 2 + b0) * 2 + lax.rem(self.k + s, 2)

    def device(self, m, s):
        return (self.base + self.slot(m, s), self.z)

    def enter(self, extra=()):
        barrier = pltpu.get_barrier_semaphore()
        devices = [self.device(1, 0), self.device(2, 0), self.device(0, 1)] + list(extra)
        for device in devices:
            pl.semaphore_signal(barrier, inc=1, device_id=device, device_id_type=MESH)
        pl.semaphore_wait(barrier, len(devices))


def remote(src, dst, send, recv, device):
    return pltpu.make_async_remote_copy(
        src_ref=src, dst_ref=dst, send_sem=send, recv_sem=recv, device_id=device,
        device_id_type=MESH,
    )


class Gather:
    def __init__(self, net, full, send, recv):
        self.net, self.full, self.send, self.recv = net, full, send, recv
        half = full.shape[1] // 2
        a, b, whole = pl.ds(0, half), pl.ds(half, half), pl.ds(0, 2 * half)
        x, y, sib = net.device(1, 0), net.device(2, 0), net.device(0, 1)
        self.plan = [
            (0, a, x, 1), (0, b, y, 2), (0, b, x, 1), (0, a, y, 2), (2, b, x, 3), (1, a, y, 3),
            (0, whole, sib, 0), (1, whole, sib, 1), (2, whole, sib, 2), (3, whole, sib, 3),
        ]

    def copy(self, i):
        m, rows, to, _ = self.plan[i]
        at = self.full.at[self.net.slot(m, 0), rows]
        return remote(at, at, self.send.at[i], self.recv.at[i], to)

    def arrived(self, i):
        _, rows, to, m = self.plan[i]
        at = self.full.at[self.net.slot(m, 0 if i < 6 else 1), rows]
        remote(at, at, self.send.at[i], self.recv.at[i], to).wait_recv()

    def begin(self):
        for i in (0, 1, 2, 3, 6):
            self.copy(i).start()

    def before(self, n):
        if n == 1:
            self.arrived(6)
        if n == 2:
            self.arrived(0)
            self.copy(5).start()
            self.arrived(1)
            self.copy(4).start()
            self.arrived(2)
            self.copy(7).start()
        if n == 3:
            self.arrived(7)
        if n == 4:
            self.arrived(3)
            self.copy(8).start()
        if n == 5:
            self.arrived(8)
        if n == 6:
            self.arrived(4)
            self.arrived(5)
            self.copy(9).start()
        if n == 7:
            self.arrived(9)

    def finish(self):
        for i in range(10):
            self.copy(i).wait_send()


class Scatter:
    def __init__(self, net, part, near, wide, far, send, recv):
        self.net, self.part, self.near = net, part, near
        self.wide, self.far, self.send, self.recv = wide, far, send, recv
        self.rows = part.shape[2]
        half = self.rows // 2
        a, b, whole = pl.ds(0, half), pl.ds(half, half), pl.ds(0, 2 * half)
        self.a, self.b = a, b
        x, y, sib = net.device(1, 0), net.device(2, 0), net.device(0, 1)
        self.plan = [
            (part.at[1, m], near.at[m], sib) for m in range(4)
        ] + [
            (part.at[0, 3, a], wide.at[0], x),
            (part.at[0, 3, b], wide.at[1], y),
            (part.at[0, 1, a], far.at[0, a], x),
            (part.at[0, 2, b], far.at[1, b], y),
            (part.at[0, 1, b], far.at[0, b], x),
            (part.at[0, 2, a], far.at[1, a], y),
        ]

    def copy(self, i):
        src, dst, to = self.plan[i]
        return remote(src, dst, self.send.at[i], self.recv.at[i], to)

    def add(self, m, start, count, other):
        def some(i, carry):
            at = pl.ds(pl.multiple_of(start + i * 64, 64), 64)
            from_at = pl.ds(pl.multiple_of(i * 64, 64), 64)
            total = self.part[0, m, at].astype(F32) + other[from_at].astype(F32)
            self.part[0, m, at] = total.astype(BF)
            return carry

        lax.fori_loop(0, count // 64, some, 0)

    def after(self, n):
        if n == 1:
            self.copy(0).start()
        if n == 3:
            self.copy(1).start()
        if n == 4:
            self.copy(1).wait_recv()
            self.add(1, 0, self.rows, self.near.at[1])
            self.copy(6).start()
        if n == 5:
            self.copy(2).start()
        if n == 6:
            self.copy(2).wait_recv()
            self.add(2, 0, self.rows, self.near.at[2])
            self.copy(7).start()
        if n == 7:
            self.copy(3).start()

    def corner(self):
        self.copy(3).wait_recv()
        self.add(3, 0, self.rows, self.near.at[3])
        self.copy(4).start()
        self.copy(5).start()

    def edges(self):
        half = self.rows // 2
        self.copy(4).wait_recv()
        self.add(2, 0, half, self.wide.at[0])
        self.copy(9).start()
        self.copy(5).wait_recv()
        self.add(1, half, half, self.wide.at[1])
        self.copy(8).start()
        self.copy(0).wait_recv()

    def finish(self):
        for i in (6, 7, 8, 9):
            self.copy(i).wait_recv()
        for i in range(10):
            self.copy(i).wait_send()

    def total(self, at):
        own = self.part[0, 0, at].astype(F32) + self.near[0, at].astype(F32)
        return own + self.far[0, at].astype(F32) + self.far[1, at].astype(F32)


def plane_scratch(rows, width):
    dma = pltpu.SemaphoreType.DMA
    return [
        pltpu.VMEM((TP, rows, width), BF),
        pltpu.VMEM((2, 4, rows, width), BF),
        pltpu.VMEM((4, rows, width), BF),
        pltpu.VMEM((2, rows // 2, width), BF),
        pltpu.VMEM((2, rows, width), BF),
        dma((10,)), dma((10,)), dma((10,)), dma((10,)),
    ]


def steps(gather, scatter, compute):
    def one(i, carry):
        for n in range(1, 2 * 4):
            @pl.when(i == n)
            def _():
                if gather is not None:
                    gather.before(n)

        compute(i // 2, lax.rem(i, 2))
        for n in range(2 * 4):
            @pl.when(i == n)
            def _():
                if scatter is not None:
                    scatter.after(n)

        return carry

    lax.fori_loop(0, 2 * 4, one, 0)


def end_forward(scatter, residual, gain, out, normed):
    rows, chunk = out.shape[0], 32

    def some(i, carry):
        at = pl.ds(pl.multiple_of(i * chunk, chunk), chunk)
        value = residual[at] + scatter.total(at)
        out[at] = value
        scale = lax.rsqrt(jnp.mean(value * value, axis=-1, keepdims=True) + EPSILON)
        normed[at] = (value * scale * gain[...]).astype(BF)
        return carry

    lax.fori_loop(0, rows // chunk, some, 0)


def end_backward(scatter, upstream, values, gain, grad, grad_low, grad_gain):
    rows, chunk = grad.shape[0], 32
    grad_gain[...] = jnp.zeros_like(grad_gain)

    def some(i, carry):
        at = pl.ds(pl.multiple_of(i * chunk, chunk), chunk)
        value, given = values[at], scatter.total(at)
        scale = lax.rsqrt(jnp.mean(value * value, axis=-1, keepdims=True) + EPSILON)
        scaled = given * gain[...]
        mean = jnp.mean(value * scaled, axis=-1, keepdims=True)
        result = upstream[at] + scale * scaled - value * (scale * scale * scale * mean)
        grad[at] = result
        grad_low[at] = result.astype(BF)
        grad_gain[...] += jnp.sum(given * value * scale, axis=0, keepdims=True)
        return carry

    lax.fori_loop(0, rows // chunk, some, 0)


GELU_A = 0.7978845608028654
GELU_B = 0.044715


def gelu_parts(v):
    square = v * v
    tanh = jnp.tanh(GELU_A * (v + GELU_B * v * square))
    half = 0.5 * (1.0 + tanh)
    slope = half + 0.5 * v * (1.0 - tanh * tanh) * (GELU_A * (1.0 + 3.0 * GELU_B * square))
    return v * half, slope


def copy_list(pairs, sem, first):
    return [
        pltpu.make_async_copy(src, dst, sem.at[first + n]) for n, (src, dst) in enumerate(pairs)
    ]


def unpack_rec(pack, col, wout, gates, sem, first):
    seq, both = pack.shape[0], pack.shape[2]
    rows, part = col.shape[0] // seq, gates.shape[0] // seq
    pairs = []
    for z in range(seq):
        pairs.append((pack.at[z, pl.ds(0, rows)], col.at[pl.ds(z * rows, rows)]))
        own = pl.ds(z * part, part)
        for j in range(3):
            pairs.append(
                (pack.at[z, pl.ds(rows + j * part, part)], wout.at[own, pl.ds(j * both, both)])
            )
        pairs.append((pack.at[z, pl.ds(rows + 3 * part, part)], gates.at[own]))
    return copy_list(pairs, sem, first)


def mlp_split(width, twice):
    rest = width - twice
    return rest, twice // rest


def unpack_mlp(pack, col, down, sem, first):
    seq, twice = pack.shape[0], pack.shape[2]
    rows, part = col.shape[0] // seq, down.shape[0] // seq
    rest, blocks = mlp_split(down.shape[1], twice)
    low = part // blocks
    pairs = []
    for z in range(seq):
        pairs.append((pack.at[z, pl.ds(0, rows)], col.at[pl.ds(z * rows, rows)]))
        pairs.append(
            (pack.at[z, pl.ds(rows, part)], down.at[pl.ds(z * part, part), pl.ds(0, twice)])
        )
        for n in range(blocks):
            pairs.append(
                (
                    pack.at[z, pl.ds(rows + part, low), pl.ds(n * rest, rest)],
                    down.at[pl.ds(z * part + n * low, low), pl.ds(twice, rest)],
                )
            )
    return copy_list(pairs, sem, first)


def mlp_forward_kernel(
    x_ref, residual_ref, gain_ref, pack_ref,
    out_ref, normed_ref, full_out, up_out,
    full, part, near, wide, far, gs, gr, ss, sr, col, wd, ups, sem,
):
    net = Net()
    gather = Gather(net, full, gs, gr)
    scatter = Scatter(net, part, near, wide, far, ss, sr)
    n = 5 * pack_ref.shape[0]
    own = pltpu.make_async_copy(x_ref, full.at[net.t], sem.at[n])
    own.start()
    weights = unpack_mlp(pack_ref, col, wd, sem, 0)
    for copy in weights:
        copy.start()
    net.enter()
    own.wait()
    gather.begin()
    for copy in weights:
        copy.wait()

    units = wd.shape[0]

    def compute(m, s):
        slot = net.slot(m, s)
        x = full[slot]
        up = dot(x, col[...])
        ups[slot] = up.astype(BF)
        hidden = glu_product(up[:, :units], up[:, units:]).astype(BF)
        part[s, m] = dot(hidden, wd[...]).astype(BF)

    steps(gather, scatter, compute)
    saves = [
        pltpu.make_async_copy(full, full_out, sem.at[n + 1]),
        pltpu.make_async_copy(ups, up_out, sem.at[n + 2]),
    ]
    for copy in saves:
        copy.start()
    scatter.corner()
    scatter.edges()
    scatter.finish()
    end_forward(scatter, residual_ref, gain_ref, out_ref, normed_ref)
    gather.finish()
    for copy in saves:
        copy.wait()


def mlp_forward(x, residual, gain, pack):
    rows, width = x.shape
    seq, _, twice = pack.shape
    shape = jax.ShapeDtypeStruct
    return pl.pallas_call(
        mlp_forward_kernel,
        in_specs=[ANY, VM, VM, ANY],
        out_specs=[VM, VM, ANY, ANY],
        out_shape=[
            shape((rows, width), F32),
            shape((rows, width), BF),
            shape((TP, rows, width), BF),
            shape((TP, rows, twice), BF),
        ],
        scratch_shapes=plane_scratch(rows, width)
        + [
            pltpu.VMEM((width, twice), BF),
            pltpu.VMEM((twice // 2, width), BF),
            pltpu.VMEM((TP, rows, twice), BF),
            pltpu.SemaphoreType.DMA((5 * seq + 4,)),
        ],
        compiler_params=pltpu.CompilerParams(
            collective_id=1, has_side_effects=True, vmem_limit_bytes=58 << 20
        ),
        cost_estimate=pl.CostEstimate(
            flops=60 * 10**9, bytes_accessed=30 << 20, transcendentals=0
        ),
        name="mlp_forward",
    )(x, residual, gain.reshape(1, -1), pack)


def mlp_backward_kernel(
    g_ref, upstream_ref, values_ref, gain_ref, pack_ref, x_ref, up_ref,
    grad_ref, low_ref, gain_out, gcol_ref,
    full, part, near, wide, far, gs, gr, ss, sr, col, wd, xs, ups, hid, sem,
):
    net = Net()
    gather = Gather(net, full, gs, gr)
    scatter = Scatter(net, part, near, wide, far, ss, sr)
    seq = pack_ref.shape[0]
    n = 5 * seq
    own = pltpu.make_async_copy(g_ref, full.at[net.t], sem.at[n])
    own.start()
    loads = unpack_mlp(pack_ref, col, wd, sem, 0) + [
        pltpu.make_async_copy(up_ref, ups, sem.at[n + 1]),
    ]
    late = pltpu.make_async_copy(x_ref, xs, sem.at[n + 3])
    for copy in loads + [late]:
        copy.start()
    net.enter()
    own.wait()
    gather.begin()
    for copy in loads:
        copy.wait()
    rows, units = full.shape[1], wd.shape[0]

    def compute(m, s):
        slot = net.slot(m, s)
        at = pl.ds(pl.multiple_of(slot * rows, rows), rows)
        grad_hidden = dot_nt(full[slot], wd[...])
        up = ups[at].astype(F32)
        act, slope = gelu_parts(up[:, :units])
        up_value = up[:, units:]
        hid[at] = (act * up_value).astype(BF)
        grads = jnp.concatenate([grad_hidden * up_value * slope, grad_hidden * act], 1).astype(BF)
        ups[at] = grads
        part[s, m] = dot_nt(grads, col[...]).astype(BF)

    steps(gather, scatter, compute)
    late.wait()
    scatter.corner()
    width = full.shape[2]
    own_rows = width // (TP * seq)
    tile = 2 * seq * own_rows
    base = width // seq

    def columns(j, carry):
        x = xs[:, pl.ds(pl.multiple_of(j * tile, 128), tile)]
        product = dot_tn(x, ups[...]).astype(BF)
        for r in range(2):
            for z in range(seq):
                low = (r * seq + z) * own_rows
                at = pl.ds(pl.multiple_of((2 * j + r) * own_rows, own_rows), own_rows)
                gcol_ref[z, at] = product[low : low + own_rows]
        return carry

    lax.fori_loop(0, TP // 2, columns, 0)
    scatter.edges()

    tokens = full.shape[0] * rows
    part_units = units // seq
    rest, blocks = mlp_split(width, 2 * units)
    low = part_units // blocks
    hidden = hid[...]
    for first in range(0, width, width // 2):
        at = pl.ds(first, width // 2)
        product = dot_tn(hidden, full[:, :, at].reshape(tokens, width // 2)).astype(BF)
        beside = min(2 * units - first, width // 2)
        for z in range(seq):
            own = product[z * part_units : (z + 1) * part_units]
            to = lax.rem(net.t + z, seq)
            gcol_ref[to, base : base + part_units, first : first + beside] = own[:, :beside]
            if beside < width // 2:
                for n in range(blocks):
                    gcol_ref[to, base + part_units :, n * rest : (n + 1) * rest] = own[
                        n * low : (n + 1) * low, beside:
                    ]
    scatter.finish()
    end_backward(scatter, upstream_ref, values_ref, gain_ref, grad_ref, low_ref, gain_out)
    gather.finish()


def mlp_backward(g, upstream, values, gain, pack, x, up):
    rows, width = g.shape
    seq, _, twice = pack.shape
    tokens = TP * rows
    shape = jax.ShapeDtypeStruct
    return pl.pallas_call(
        mlp_backward_kernel,
        in_specs=[ANY, VM, VM, VM, ANY, ANY, ANY],
        out_specs=[VM, VM, VM, VM],
        out_shape=[
            shape((rows, width), F32),
            shape((rows, width), BF),
            shape((1, width), F32),
            shape(pack.shape, BF),
        ],
        scratch_shapes=plane_scratch(rows, width)
        + [
            pltpu.VMEM((width, twice), BF),
            pltpu.VMEM((twice // 2, width), BF),
            pltpu.VMEM((tokens, width), BF),
            pltpu.VMEM((tokens, twice), BF),
            pltpu.VMEM((tokens, twice // 2), BF),
            pltpu.SemaphoreType.DMA((5 * seq + 4,)),
        ],
        compiler_params=pltpu.CompilerParams(
            collective_id=2, has_side_effects=True, vmem_limit_bytes=60 << 20
        ),
        cost_estimate=pl.CostEstimate(
            flops=70 * 10**9, bytes_accessed=30 << 20, transcendentals=0
        ),
        name="mlp_backward",
    )(
        g, upstream, values, gain.reshape(1, -1), pack, x.reshape(tokens, width),
        up.reshape(tokens, twice),
    )


def after_corner_first(scatter, n):
    if n % 2 == 0:
        scatter.copy(3 - n // 2).start()
    if n == 3:
        scatter.corner()
    if n == 5:
        scatter.copy(2).wait_recv()
        scatter.add(2, 0, scatter.rows, scatter.near.at[2])
        scatter.copy(7).start()
    if n == 7:
        scatter.copy(1).wait_recv()
        scatter.add(1, 0, scatter.rows, scatter.near.at[1])
        scatter.copy(6).start()


class Line:
    def __init__(self, net, count):
        self.net, self.count = net, count
        self.others = [(net.base + net.t, lax.rem(net.z + d, count)) for d in range(1, count)]
        self.next = (net.base + net.t, net.z + 1)
        self.before = (net.base + net.t, net.z - 1)

    def to_all(self, ends, send, recv):
        at = ends.at[self.net.z]
        copies = [
            remote(at, at, send.at[d], recv.at[d], to) for d, to in enumerate(self.others)
        ]
        for copy in copies:
            copy.start()
        for d, copy in enumerate(copies):
            source = lax.rem(self.net.z + self.count - 1 - d, self.count)
            from_at = ends.at[source]
            remote(from_at, from_at, send.at[d], recv.at[d], self.others[d]).wait_recv()
        for copy in copies:
            copy.wait_send()


def inside_of(positions, offset, length):
    return jnp.where((positions >= offset) & (positions < offset + length), 1.0, 0.0)


def read_halves(ref, at):
    return jnp.concatenate([ref[n, at] for n in range(ref.shape[0])], 1)


def write_halves(ref, at, value):
    for n in range(ref.shape[0]):
        ref[n, at] = value[:, n * 128 : (n + 1) * 128]


def one_minus_exp(v):
    series = 1.0 + v * (1.0 / 7.0)
    for n in (6.0, 5.0, 4.0, 3.0, 2.0):
        series = 1.0 + v * (1.0 / n) * series
    return jnp.where(v > -0.35, -v * series, 1.0 - jnp.exp(v))


def sigmoid(v):
    return 1.0 / (1.0 + jnp.exp(-v))


def rec_forward_kernel(
    gathered,
    x_ref, residual_ref, gain_ref, pack_ref, small_ref, slots_ref,
    out_ref, normed_ref, full_out, branch_out, stream_out, conv_out, state_out,
    full, part, near, wide, far, gs, gr, ss, sr,
    col, gates, wout, branch, stream, conv, state, retain, inflow, ends, carry, hs, hr, es, er, sem,
):
    net = Net()
    seq = ends.shape[0]
    line = Line(net, seq)
    gather = Gather(net, full, gs, gr)
    scatter = Scatter(net, part, near, wide, far, ss, sr)
    rows = full.shape[1]
    head = gates.shape[0]
    own = pltpu.make_async_copy(x_ref, full if gathered else full.at[net.t], sem.at[0])
    loads = unpack_rec(pack_ref, col, wout, gates, sem, 9)
    for load in [own] + loads:
        load.start()
    net.enter(line.others)
    own.wait()
    if not gathered:
        gather.begin()

    @pl.when(net.z == 0)
    def _():
        stream[:, pl.ds(0, 8), :] = jnp.zeros((TP, 8, head), F32)

    for load in loads:
        load.wait()

    def halo(i):
        slot = net.slot(i // 2, lax.rem(i, 2))
        return remote(
            stream.at[slot, pl.ds(rows, 8)], stream.at[slot, pl.ds(0, 8)],
            hs.at[i], hr.at[i], line.next,
        )

    def project(i):
        slot = net.slot(i // 2, lax.rem(i, 2))
        both = dot(full[slot], col[...])
        branch[slot] = both[:, :head]
        stream[slot, pl.ds(8, rows)] = both[:, head:]

        @pl.when(net.z < seq - 1)
        def _():
            halo(i).start()

    def gate(i):
        slot = net.slot(i // 2, lax.rem(i, 2))

        @pl.when(net.z > 0)
        def _():
            halo(i).wait_recv()

        length, offset = slots_ref[slot, 0], slots_ref[slot, 1]
        positions = net.z * rows + lax.broadcasted_iota(jnp.int32, (rows, head), 0)
        inside = inside_of(positions, offset, length)
        mixed = small_ref[pl.ds(CONV, 1), :] + small_ref[pl.ds(0, 1), :] * stream[slot, pl.ds(8, rows)]
        restart = positions == 0
        for j in range(1, CONV):
            same = jnp.where(inside == inside_of(positions - j, offset, length), 1.0, 0.0)
            if j == 1:
                restart = restart | (same == 0.0)
            mixed += small_ref[pl.ds(j, 1), :] * stream[slot, pl.ds(8 - j, rows)] * same
        low = mixed.astype(BF)
        conv[slot] = low
        pre = dot(low, gates[...])
        rate = sigmoid(pre[:, :head] + small_ref[pl.ds(CONV + 1, 1), :])
        admit = sigmoid(pre[:, head:] + small_ref[pl.ds(CONV + 2, 1), :])
        log_retain = rate * small_ref[pl.ds(CONV + 3, 1), :]
        at = pl.ds(pl.multiple_of(slot * rows, rows), rows)
        write_halves(retain, at, jnp.where(restart, 0.0, jnp.exp(log_retain)))
        scale = jnp.where(restart, 1.0, jnp.sqrt(one_minus_exp(2.0 * log_retain)))
        write_halves(inflow, at, scale * admit * low.astype(F32))

    def one(i, _):
        for n in range(1, TP):
            @pl.when(i == n)
            def _():
                if not gathered:
                    gather.before(n)

        @pl.when(i < TP)
        def _():
            project(i)

        @pl.when(i >= LATER)
        def _():
            gate(i - LATER)

        return 0

    lax.fori_loop(0, TP + LATER, one, 0)
    saves = [
        pltpu.make_async_copy(branch, branch_out, sem.at[5]),
        pltpu.make_async_copy(stream, stream_out, sem.at[6]),
        pltpu.make_async_copy(conv, conv_out, sem.at[7]),
    ]
    if not gathered:
        saves.append(pltpu.make_async_copy(full, full_out, sem.at[4]))
    for save in saves:
        save.start()

    lanes = [pl.ds(i, 128) for i in range(0, head, 128)]

    def step(p, carried):
        at = pl.ds(p, TP, stride=rows)
        result = []
        for n, (value, decay) in enumerate(carried):
            a = retain[n, at]
            value = a * value + inflow[n, at]
            decay = a * decay
            inflow[n, at] = value
            retain[n, at] = decay
            result.append((value, decay))
        return tuple(result)

    start = tuple((jnp.zeros((TP, 128), F32), jnp.ones((TP, 128), F32)) for _ in lanes)
    last = lax.fori_loop(0, rows, step, start, unroll=8)
    for lane, (value, decay) in zip(lanes, last):
        ends[net.z, pl.ds(0, TP), lane] = decay
        ends[net.z, pl.ds(TP, TP), lane] = value
    line.to_all(ends, es, er)
    entering = jnp.zeros((TP, head), F32)
    for z in range(seq - 1):
        later = ends[z, pl.ds(0, TP)] * entering + ends[z, pl.ds(TP, TP)]
        entering = jnp.where(z < net.z, later, entering)
    carry[...] = entering

    def join(i, _):
        m, s = 3 - i // 2, 1 - lax.rem(i, 2)
        slot = net.slot(m, s)
        at = pl.ds(pl.multiple_of(slot * rows, rows), rows)
        first = carry[pl.ds(slot, 1), :]
        states = read_halves(inflow, at) + read_halves(retain, at) * first
        state[slot, pl.ds(0, 8)] = jnp.broadcast_to(first, (8, head))
        state[slot, pl.ds(8, rows)] = states
        joined = glu_product(branch[slot], states).astype(BF)
        part[s, m] = dot(joined, wout[...]).astype(BF)
        for n in range(TP):
            @pl.when(i == n)
            def _():
                after_corner_first(scatter, n)

        return 0

    lax.fori_loop(0, TP, join, 0)
    saves.append(pltpu.make_async_copy(state, state_out, sem.at[8]))
    saves[-1].start()
    scatter.edges()

    @pl.when(net.z < seq - 1)
    def _():
        lax.fori_loop(0, TP, lambda i, _: (halo(i).wait_send(), 0)[1], 0)

    scatter.finish()
    end_forward(scatter, residual_ref, gain_ref, out_ref, normed_ref)
    if not gathered:
        gather.finish()
    for save in saves:
        save.wait()


def rec_scratch(pack, width):
    seq, _, both = pack.shape
    return [
        pltpu.VMEM((width, both), BF),
        pltpu.VMEM((both // 2, both), BF),
        pltpu.VMEM((both // 2, width), BF),
    ]


def rec_forward(x, residual, gain, pack, small, slots):
    gathered = x.ndim == 3
    rows, width = residual.shape
    seq, _, head = pack.shape
    head = head // 2
    shape = jax.ShapeDtypeStruct
    dma = pltpu.SemaphoreType.DMA
    tokens = TP * rows
    result = list(pl.pallas_call(
        partial(rec_forward_kernel, gathered),
        in_specs=[ANY, VM, VM, ANY, VM, pl.BlockSpec(memory_space=pltpu.SMEM)],
        out_specs=[VM, VM, ANY, ANY, ANY, ANY, ANY],
        out_shape=[
            shape((rows, width), F32),
            shape((rows, width), BF),
            shape((8, 128) if gathered else (TP, rows, width), BF),
            shape((TP, rows, head), F32),
            shape((TP, rows + 8, head), F32),
            shape((TP, rows, head), BF),
            shape((TP, rows + 8, head), F32),
        ],
        scratch_shapes=plane_scratch(rows, width)
        + rec_scratch(pack, width)
        + [
            pltpu.VMEM((TP, rows, head), F32),
            pltpu.VMEM((TP, rows + 8, head), F32),
            pltpu.VMEM((TP, rows, head), BF),
            pltpu.VMEM((TP, rows + 8, head), F32),
            pltpu.VMEM((head // 128, tokens, 128), F32),
            pltpu.VMEM((head // 128, tokens, 128), F32),
            pltpu.VMEM((seq, 2 * TP, head), F32),
            pltpu.VMEM((TP, head), F32),
            dma((TP,)), dma((TP,)), dma((seq - 1,)), dma((seq - 1,)), dma((9 + 5 * seq,)),
        ],
        compiler_params=pltpu.CompilerParams(
            collective_id=5 if gathered else 3, has_side_effects=True, vmem_limit_bytes=58 << 20
        ),
        cost_estimate=pl.CostEstimate(
            flops=70 * 10**9, bytes_accessed=30 << 20, transcendentals=0
        ),
        name="rec_forward_first" if gathered else "rec_forward",
    )(x, residual, gain.reshape(1, -1), pack, small, slots))
    if gathered:
        result[2] = x
    return result


def rec_backward_kernel(
    g_ref, upstream_ref, values_ref, gain_ref, pack_ref, small_ref, slots_ref,
    x_ref, branch_ref, stream_ref, conv_ref, state_ref,
    grad_ref, low_ref, gain_out, gcol_ref, channel_ref,
    full, part, near, wide, far, gs, gr, ss, sr,
    col, gates, wout, xs, branch, stream, conv, state,
    retain, direct, suffix, joined, both, gpre, mixed, ends, carry, hs, hr, es, er, sem,
):
    net = Net()
    seq = ends.shape[0]
    line = Line(net, seq)
    gather = Gather(net, full, gs, gr)
    scatter = Scatter(net, part, near, wide, far, ss, sr)
    rows, width = full.shape[1], full.shape[2]
    head = gates.shape[0]
    own = pltpu.make_async_copy(g_ref, full.at[net.t], sem.at[0])
    loads = [
        pltpu.make_async_copy(a, b, sem.at[1 + n])
        for n, (a, b) in enumerate(
            (
                (branch_ref, branch), (state_ref, state), (conv_ref, conv), (stream_ref, stream),
                (x_ref, xs),
            )
        )
    ]
    loads = unpack_rec(pack_ref, col, wout, gates, sem, 9) + loads
    for load in [own] + loads:
        load.start()
    net.enter(line.others)
    own.wait()
    gather.begin()

    @pl.when(net.z == seq - 1)
    def _():
        mixed[:, pl.ds(rows, 8), :] = jnp.zeros((TP, 8, head), F32)

    channel_ref[...] = jnp.zeros_like(channel_ref)
    for load in loads[:-2]:
        load.wait()

    def gate_parts(slot):
        positions = net.z * rows + lax.broadcasted_iota(jnp.int32, (rows, head), 0)
        length, offset = slots_ref[slot, 0], slots_ref[slot, 1]
        inside = inside_of(positions, offset, length)
        restart = (positions == 0) | (inside != inside_of(positions - 1, offset, length))
        pre = dot(conv[slot], gates[...])
        rate = sigmoid(pre[:, :head] + small_ref[pl.ds(CONV + 1, 1), :])
        admit = sigmoid(pre[:, head:] + small_ref[pl.ds(CONV + 2, 1), :])
        log_retain = rate * small_ref[pl.ds(CONV + 3, 1), :]
        return positions, offset, length, inside, restart, rate, admit, log_retain

    def open_block(m, s):
        slot = net.slot(m, s)
        at = pl.ds(pl.multiple_of(slot * rows, rows), rows)
        grad_joined = dot_nt(full[slot], wout[...])
        act, slope = gelu_parts(branch[slot])
        states = state[slot, pl.ds(8, rows)]
        joined[at] = (act * states).astype(BF)
        both[at, :head] = (grad_joined * states * slope).astype(BF)
        write_halves(direct, at, grad_joined * act)
        _, _, _, _, restart, _, _, log_retain = gate_parts(slot)
        write_halves(retain, at, jnp.where(restart, 0.0, jnp.exp(log_retain)))

    steps(gather, None, open_block)
    lanes = [pl.ds(i, 128) for i in range(0, head, 128)]

    def step(i, carried):
        at = pl.ds(rows - 1 - i, TP, stride=rows)
        result = []
        for n, (value, decay, ahead) in enumerate(carried):
            value = ahead * value + direct[n, at]
            decay = ahead * decay
            direct[n, at] = value
            suffix[n, at] = decay
            result.append((value, decay, retain[n, at]))
        return tuple(result)

    one = jnp.minimum(retain[0, pl.ds(0, TP)] + 2.0, 1.0)
    last = lax.fori_loop(
        0, rows, step, tuple((jnp.zeros((TP, 128), F32), one, one) for _ in lanes), unroll=8
    )
    for lane, (value, decay, first) in zip(lanes, last):
        ends[net.z, pl.ds(0, TP), lane] = first * decay
        ends[net.z, pl.ds(TP, TP), lane] = first * value
    line.to_all(ends, es, er)
    entering = jnp.zeros((TP, head), F32)
    for z in range(seq - 1, 0, -1):
        earlier = ends[z, pl.ds(0, TP)] * entering + ends[z, pl.ds(TP, TP)]
        entering = jnp.where(z > net.z, earlier, entering)
    carry[...] = entering
    loads[-2].wait()

    def halo(i):
        slot = net.slot(3 - i // 2, 1 - lax.rem(i, 2))
        return remote(
            mixed.at[slot, pl.ds(0, 8)], mixed.at[slot, pl.ds(rows, 8)],
            hs.at[i], hr.at[i], line.before,
        )

    def through_gates(i):
        slot = net.slot(3 - i // 2, 1 - lax.rem(i, 2))
        at = pl.ds(pl.multiple_of(slot * rows, rows), rows)
        grad_states = read_halves(direct, at) + read_halves(suffix, at) * carry[pl.ds(slot, 1), :]
        positions, offset, length, inside, restart, rate, admit, log_retain = gate_parts(slot)
        low = conv[slot].astype(F32)
        kept = jnp.exp(log_retain)
        root = jnp.sqrt(one_minus_exp(2.0 * log_retain))
        scale = jnp.where(restart, 1.0, root)
        grad_admit = grad_states * scale * low
        grad_scale = grad_states * admit * low
        grad_log = grad_states * state[slot, pl.ds(7, rows)] * kept - grad_scale * kept * kept / root
        grad_log = jnp.where(restart, 0.0, grad_log)
        rate_part = grad_log * small_ref[pl.ds(CONV + 3, 1), :] * rate * (1.0 - rate)
        admit_part = grad_admit * admit * (1.0 - admit)
        gpre[at, :head] = rate_part.astype(BF)
        gpre[at, head:] = admit_part.astype(BF)
        grad_mixed = grad_states * scale * admit + dot_nt(gpre[at], gates[...])
        mixed[slot, pl.ds(0, rows)] = grad_mixed

        @pl.when(net.z > 0)
        def _():
            halo(i).start()

        sums = [jnp.sum(grad_mixed * stream[slot, pl.ds(8, rows)], axis=0, keepdims=True)]
        for j in range(1, CONV):
            same = jnp.where(inside == inside_of(positions - j, offset, length), 1.0, 0.0)
            sums.append(
                jnp.sum(
                    grad_mixed * stream[slot, pl.ds(8 - j, rows)] * same, axis=0, keepdims=True
                )
            )
        for term in (grad_mixed, rate_part, admit_part, grad_log * rate):
            sums.append(jnp.sum(term, axis=0, keepdims=True))
        for n, term in enumerate(sums):
            channel_ref[pl.ds(n, 1), :] += term

    def to_input(i):
        m, s = 3 - i // 2, 1 - lax.rem(i, 2)
        slot = net.slot(m, s)
        at = pl.ds(pl.multiple_of(slot * rows, rows), rows)

        @pl.when(net.z < seq - 1)
        def _():
            halo(i).wait_recv()

        positions = net.z * rows + lax.broadcasted_iota(jnp.int32, (rows, head), 0)
        length, offset = slots_ref[slot, 0], slots_ref[slot, 1]
        inside = inside_of(positions, offset, length)
        grad_stream = small_ref[pl.ds(0, 1), :] * mixed[slot, pl.ds(0, rows)]
        for j in range(1, CONV):
            same = jnp.where(inside == inside_of(positions + j, offset, length), 1.0, 0.0)
            grad_stream += small_ref[pl.ds(j, 1), :] * mixed[slot, pl.ds(j, rows)] * same
        both[at, head:] = grad_stream.astype(BF)
        part[s, m] = dot_nt(both[at], col[...]).astype(BF)

    def one_block(i, _):
        @pl.when(i < TP)
        def _():
            through_gates(i)

        @pl.when(i >= LATER)
        def _():
            to_input(i - LATER)

        for n in range(TP):
            @pl.when(i == n + LATER)
            def _():
                after_corner_first(scatter, n)

        return 0

    lax.fori_loop(0, TP + LATER, one_block, 0)
    scatter.edges()
    loads[-1].wait()
    own_rows = width // (TP * seq)
    tile = 2 * seq * own_rows

    def columns(j, _):
        x = xs[:, pl.ds(pl.multiple_of(j * tile, 128), tile)]
        product = dot_tn(x, both[...]).astype(BF)
        for r in range(2):
            for z in range(seq):
                low = (r * seq + z) * own_rows
                at = pl.ds(pl.multiple_of((2 * j + r) * own_rows, own_rows), own_rows)
                gcol_ref[z, at] = product[low : low + own_rows]
        return 0

    lax.fori_loop(0, TP // 2, columns, 0)
    low_conv = conv[...].reshape(TP * rows, head)
    product = dot_tn(low_conv, gpre[...]).astype(BF)
    third, base, part_head = width // 3, width // seq, head // seq
    for z in range(seq):
        low = base + 3 * part_head
        gcol_ref[z, low : low + part_head] = product[z * part_head : (z + 1) * part_head]
    for j in range(3):
        at = pl.ds(j * third, third)
        product = dot_tn(joined[...], full[:, :, at].reshape(TP * rows, third)).astype(BF)
        for z in range(seq):
            low = base + j * part_head
            gcol_ref[z, low : low + part_head] = product[z * part_head : (z + 1) * part_head]

    @pl.when(net.z > 0)
    def _():
        lax.fori_loop(0, TP, lambda i, _: (halo(i).wait_send(), 0)[1], 0)

    scatter.finish()
    end_backward(scatter, upstream_ref, values_ref, gain_ref, grad_ref, low_ref, gain_out)
    gather.finish()


def rec_backward(g, upstream, values, gain, pack, small, slots, saved):
    rows, width = g.shape
    seq, _, head = pack.shape
    head = head // 2
    tokens = TP * rows
    shape = jax.ShapeDtypeStruct
    dma = pltpu.SemaphoreType.DMA
    x, branch, stream, conv, state = saved
    return pl.pallas_call(
        rec_backward_kernel,
        in_specs=[ANY, VM, VM, VM, ANY, VM, pl.BlockSpec(memory_space=pltpu.SMEM)]
        + [ANY] * 5,
        out_specs=[VM] * 5,
        out_shape=[
            shape((rows, width), F32),
            shape((rows, width), BF),
            shape((1, width), F32),
            shape(pack.shape, BF),
            shape((8, head), F32),
        ],
        scratch_shapes=plane_scratch(rows, width)
        + rec_scratch(pack, width)
        + [
            pltpu.VMEM((tokens, width), BF),
            pltpu.VMEM(branch.shape, F32),
            pltpu.VMEM(stream.shape, F32),
            pltpu.VMEM(conv.shape, BF),
            pltpu.VMEM(state.shape, F32),
            pltpu.VMEM((head // 128, tokens, 128), F32),
            pltpu.VMEM((head // 128, tokens, 128), F32),
            pltpu.VMEM((head // 128, tokens, 128), F32),
            pltpu.VMEM((tokens, head), BF),
            pltpu.VMEM((tokens, 2 * head), BF),
            pltpu.VMEM((tokens, 2 * head), BF),
            pltpu.VMEM((TP, rows + 8, head), F32),
            pltpu.VMEM((seq, 2 * TP, head), F32),
            pltpu.VMEM((TP, head), F32),
            dma((TP,)), dma((TP,)), dma((seq - 1,)), dma((seq - 1,)), dma((9 + 5 * seq,)),
        ],
        compiler_params=pltpu.CompilerParams(
            collective_id=4, has_side_effects=True, vmem_limit_bytes=60 << 20
        ),
        cost_estimate=pl.CostEstimate(
            flops=80 * 10**9, bytes_accessed=30 << 20, transcendentals=0
        ),
        name="rec_backward",
    )(
        g, upstream, values, gain.reshape(1, -1), pack, small, slots,
        x.reshape(tokens, width), branch, stream, conv, state,
    )


def open_kernel(
    x_ref, small_ref, gain_ref, slot_ref, pack_ref,
    small_out, gain_out, slot_out, full_out, pack_out,
    full, smalls, gains, slots, gs, gr, ps, pr, sem,
):
    net = Net()
    seq = smalls.shape[0]
    line = Line(net, seq)
    gather = Gather(net, full, gs, gr)
    plane = [net.device(m, s) for m in range(4) for s in range(2)][1:]
    mine = [
        pltpu.make_async_copy(small_ref, smalls.at[net.z], sem.at[0]),
        pltpu.make_async_copy(gain_ref, gains.at[net.z], sem.at[1]),
        pltpu.make_async_copy(slot_ref, slots.at[net.t], sem.at[2]),
    ]
    own_pack = pltpu.make_async_copy(pack_ref, pack_out.at[net.z], sem.at[4])
    for copy in mine + [own_pack]:
        copy.start()
    net.enter(line.others + [net.device(1, 1), net.device(2, 1), net.device(3, 0), net.device(3, 1)])
    for copy in mine:
        copy.wait()

    sends, arrivals = [], []

    def push(ref, own, source, to):
        n = len(sends)
        at, from_at = ref.at[own], ref.at[source]
        sends.append(remote(at, at, ps.at[n], pr.at[n], to))
        arrivals.append(remote(from_at, from_at, ps.at[n], pr.at[n], to))

    for ref in (gains, smalls):
        for d, to in enumerate(line.others):
            push(ref, net.z, lax.rem(net.z + seq - 1 - d, seq), to)
    for n, to in enumerate(plane):
        m, s = (n + 1) // 2, (n + 1) % 2
        push(slots, net.t, net.slot(m, s), to)
    for copy in sends:
        copy.start()
    first = len(sends)

    def hop(way, e):
        n = first + 2 * e + (0 if way > 0 else 1)
        to = (net.base + net.t, net.z + way)
        at = pack_ref if e == 0 else pack_out.at[net.z - way * e]
        lands = pack_out.at[net.z - way * e]
        return remote(at, lands, ps.at[n], pr.at[n], to)

    def forward(way, e):
        place = net.z if way > 0 else seq - 1 - net.z

        @pl.when((place >= e) & (place < seq - 1))
        def _():
            if e > 0:
                landed(way, e - 1)
            hop(way, e).start()

        if e > 0:
            @pl.when((place >= e) & (place == seq - 1))
            def _():
                landed(way, e - 1)

    def landed(way, e):
        n = first + 2 * e + (0 if way > 0 else 1)
        from_at = pack_out.at[net.z - way * (e + 1)]
        remote(from_at, from_at, ps.at[n], pr.at[n], (net.base + net.t, net.z)).wait_recv()

    def last(way):
        place = net.z if way > 0 else seq - 1 - net.z

        @pl.when(place == seq - 1)
        def _():
            landed(way, seq - 2)

        for e in range(seq - 1):
            @pl.when((place >= e) & (place < seq - 1))
            def _():
                hop(way, e).wait_send()

    forward(1, 0)
    forward(-1, 0)
    for copy in arrivals[: seq - 1]:
        copy.wait_recv()
    rows, width = x_ref.shape
    part, chunk = width // seq, 32

    def norm(i, _):
        at = pl.ds(pl.multiple_of(i * chunk, chunk), chunk)
        value = x_ref[at].astype(F32)
        scale = lax.rsqrt(jnp.mean(value * value, axis=-1, keepdims=True) + EPSILON)
        for z in range(seq):
            low = z * part
            full[net.t, at, low : low + part] = (
                value[:, low : low + part] * scale * gains[z, pl.ds(0, 1), :]
            ).astype(BF)
        return 0

    lax.fori_loop(0, rows // chunk, norm, 0)
    gather.begin()
    for copy in arrivals[seq - 1 :]:
        copy.wait_recv()
    saves = [
        pltpu.make_async_copy(a, b, sem.at[n])
        for n, (a, b) in enumerate(((smalls, small_out), (gains, gain_out), (slots, slot_out)))
    ]
    for save in saves:
        save.start()
    for n in range(1, TP):
        gather.before(n)
        if n == 2:
            forward(1, 1)
            forward(-1, 1)
    gather.finish()
    saves.append(pltpu.make_async_copy(full, full_out, sem.at[3]))
    saves[-1].start()
    for e in range(2, seq - 1):
        forward(1, e)
        forward(-1, e)
    last(1)
    last(-1)

    for copy in sends:
        copy.wait_send()
    own_pack.wait()
    for save in saves:
        save.wait()


def opening(seq, x, small, gain, slot, pack):
    rows, width = x.shape
    shape = jax.ShapeDtypeStruct
    dma = pltpu.SemaphoreType.DMA
    pushes = 4 * (seq - 1) + TP - 1
    return pl.pallas_call(
        open_kernel,
        in_specs=[VM] + [ANY] * 4,
        out_specs=[ANY] * 5,
        out_shape=[
            shape((seq,) + small.shape, F32),
            shape((seq,) + gain.shape, F32),
            shape((TP,) + slot.shape, jnp.int32),
            shape((TP, rows, width), BF),
            shape((seq,) + pack.shape, BF),
        ],
        scratch_shapes=[
            pltpu.VMEM((TP, rows, width), BF),
            pltpu.VMEM((seq,) + small.shape, F32),
            pltpu.VMEM((seq,) + gain.shape, F32),
            pltpu.VMEM((TP,) + slot.shape, jnp.int32),
            dma((10,)), dma((10,)), dma((pushes,)), dma((pushes,)), dma((5,)),
        ],
        compiler_params=pltpu.CompilerParams(
            collective_id=6, has_side_effects=True, vmem_limit_bytes=40 << 20
        ),
        cost_estimate=pl.CostEstimate(
            flops=40 * 10**9, bytes_accessed=10 << 20, transcendentals=0
        ),
        name="opening",
    )(x, small, gain, slot, pack)


def close_kernel(layers, gain_ref, channel_ref, *refs):
    rows_in, refs = refs[:layers], refs[layers:]
    count = (len(refs) - 8 - layers) // 2
    blocks, (gain_out, channel_out) = refs[:count], refs[count : count + 2]
    moved, refs = refs[count + 2 : 2 * count + 2], refs[2 * count + 2 :]
    rows_out = refs[:layers]
    plane_gain, line_gain, line_channel, ps, pr, sem = refs[layers:]
    net = Net()
    seq = line_gain.shape[0]
    line = Line(net, seq)
    plane = [net.device(m, s) for m in range(4) for s in range(2)][1:]
    slots = [net.slot(m, s) for m in range(4) for s in range(2)][1:]
    own = [
        pltpu.make_async_copy(block.at[net.t], out.at[net.t], sem.at[n])
        for n, (block, out) in enumerate(zip(blocks, moved))
    ]
    plane_gain[net.t] = gain_ref[...]
    line_channel[net.z] = channel_ref[...]
    for copy in own:
        copy.start()
    net.enter(line.others + [net.device(1, 1), net.device(2, 1), net.device(3, 0), net.device(3, 1)])
    used = []

    def push(src, dst, landed, to):
        n = len(used)
        used.append(remote(src, dst, ps.at[n], pr.at[n], to))
        used[-1].start()
        return remote(src, landed, ps.at[n], pr.at[n], to)

    gains = [
        push(plane_gain.at[net.t], plane_gain.at[net.t], plane_gain.at[slot], to)
        for slot, to in zip(slots, plane)
    ]
    sources = [lax.rem(net.z + seq - 1 - d, seq) for d in range(seq - 1)]
    rest = [
        push(line_channel.at[net.z], line_channel.at[net.z], line_channel.at[source], to)
        for source, to in zip(sources, line.others)
    ]
    for block, out in zip(blocks, moved):
        for slot, to in zip(slots, plane):
            rest.append(push(block.at[slot], out.at[net.t], out.at[slot], to))
    each = TP // seq
    owner = lax.rem(net.z + TP - net.t, seq) * each + net.t // seq
    giver = lax.rem(net.t, each) * seq + lax.rem(net.z + TP - net.t // each, seq)
    first = ps.shape[0] - layers
    rows = [
        remote(src, dst, ps.at[first + l], pr.at[first + l], (net.base + owner, net.z))
        for l, (src, dst) in enumerate(zip(rows_in, rows_out))
    ]
    rows_here = [
        pltpu.make_async_copy(src, dst, sem.at[count + l])
        for l, (src, dst) in enumerate(zip(rows_in, rows_out))
    ]

    @pl.when(owner != net.t)
    def _():
        for copy in rows:
            copy.start()

    @pl.when(owner == net.t)
    def _():
        for copy in rows_here:
            copy.start()

    for copy in gains:
        copy.wait_recv()
    total = plane_gain[0]
    for t in range(1, TP):
        total += plane_gain[t]
    line_gain[net.z] = total
    for source, to in zip(sources, line.others):
        rest.append(push(line_gain.at[net.z], line_gain.at[net.z], line_gain.at[source], to))
    for copy in rest:
        copy.wait_recv()
    total, channel = line_gain[0], line_channel[0]
    for z in range(1, seq):
        total += line_gain[z]
        channel += line_channel[z]
    gain_out[...] = total
    channel_out[...] = channel
    for copy in used:
        copy.wait_send()
    for copy in own:
        copy.wait()

    @pl.when(owner != net.t)
    def _():
        for copy in rows:
            copy.wait_send()

    @pl.when(owner == net.t)
    def _():
        for copy in rows_here:
            copy.wait()

    @pl.when(giver != net.t)
    def _():
        for copy in rows:
            copy.wait_recv()


def closing(seq, gains, channels, rows, blocks):
    shape = jax.ShapeDtypeStruct
    dma = pltpu.SemaphoreType.DMA
    pushes = (TP - 1) * (1 + len(blocks)) + 2 * (seq - 1) + len(rows)
    return pl.pallas_call(
        partial(close_kernel, len(rows)),
        in_specs=[VM, VM] + [ANY] * (len(rows) + len(blocks)),
        out_specs=[VM, VM] + [ANY] * (len(rows) + len(blocks)),
        out_shape=[shape(gains.shape, F32), shape(channels.shape, F32)]
        + [shape(block.shape, block.dtype) for block in blocks + rows],
        scratch_shapes=[
            pltpu.VMEM((TP,) + gains.shape, F32),
            pltpu.VMEM((seq,) + gains.shape, F32),
            pltpu.VMEM((seq,) + channels.shape, F32),
            dma((pushes,)), dma((pushes,)), dma((len(blocks) + len(rows),)),
        ],
        compiler_params=pltpu.CompilerParams(
            collective_id=7, has_side_effects=True, vmem_limit_bytes=40 << 20
        ),
        cost_estimate=pl.CostEstimate(
            flops=40 * 10**9, bytes_accessed=10 << 20, transcendentals=0
        ),
        name="closing",
    )(gains, channels, *rows, *blocks)


def layer_backward(upstream, upstream_low, w, saved, slots, pending):
    residual, kept, middle, kept_two = saved
    pending_mlp, pending_rec = pending
    upstream_low, pending_mlp = lax.optimization_barrier((upstream_low, pending_mlp))
    grad_middle, mid_low, grad_gain_two, g_mlp = mlp_backward(
        upstream_low, upstream, middle, w["gain"][1], w["mlp"], *kept_two
    )
    mlp_share = over_seq(g_mlp)
    mid_low, pending_rec = lax.optimization_barrier((mid_low, pending_rec))
    grad, grad_low, grad_gain_one, g_rec, channel = rec_backward(
        mid_low, grad_middle, residual, w["gain"][0], w["rec"], w["small"], slots, kept
    )
    g_rec, mlp_share = lax.optimization_barrier((g_rec, mlp_share))
    rec_share = over_seq(g_rec)
    slope = 8.0 * jax.nn.sigmoid(-w["decay"])
    channel = jnp.concatenate([channel[:7], channel[7:] * slope], 0)
    gains = jnp.concatenate([grad_gain_one, grad_gain_two], 0)
    return grad, grad_low, (mlp_share, rec_share), channel, gains, (pending_mlp, pending_rec)


def over_seq(value):
    return lax.psum_scatter(value, "seq", scatter_dimension=0, tiled=False)


def columns(parts):
    return jnp.moveaxis(parts, 0, 1).reshape(parts.shape[1], -1)


def unit_columns(parts, seq):
    tp, n, units = parts.shape
    part = units // seq
    places = {}
    for t in range(tp):
        for p in range(seq):
            places[p * tp + t // seq * seq + (t + p) % seq] = (t, p)
    chunks = [places[q] for q in range(tp * seq)]
    return jnp.concatenate([parts[t, :, p * part : (p + 1) * part] for t, p in chunks], 1)


def owned_grads(plan, down_rows, rec_share, mlp, rec, width, head, units):
    base = width // plan.seq
    h, u = head // plan.seq, units // plan.seq
    out = [rec_share[base + i * h : base + (i + 1) * h] for i in range(3)]
    gates = rec_share[base + 3 * h :]
    rest, blocks = mlp_split(width, 2 * units)
    down = [down_rows[u:, i * rest : (i + 1) * rest] for i in range(blocks)]
    grads = [
        columns(rec[:, :, :head]),
        columns(rec[:, :, head:]),
        gates[:, :head],
        gates[:, head:],
        jnp.concatenate(out, 1),
        unit_columns(mlp[:, :, :units], plan.seq),
        unit_columns(mlp[:, :, units:], plan.seq),
        jnp.concatenate([down_rows[:u], jnp.concatenate(down, 0)], 1),
    ]
    return [to_owners(plan, g.astype(F32), 0) for g in grads]


def local(plan, *args):
    (
        block_input, cotangent, lengths, offsets, norm_gains, branch_proj, stream_proj, conv_kernel,
        conv_bias, rate_proj, admit_proj, gate_bias, decay_logit, out_proj, mlp_gate, mlp_up,
        mlp_down,
    ) = args
    tp, dp, seq = plan.tp, plan.dp, plan.seq
    t = lax.axis_index("rep") % tp
    z = lax.axis_index("seq")
    rows = block_input.shape[0]
    head = branch_proj.shape[2] // tp
    units = mlp_gate.shape[2] // tp

    channels = conv_kernel.shape[2]
    small = jnp.concatenate([conv_kernel, conv_bias[:, None], gate_bias, decay_logit[:, None]], 1)
    small = small.reshape(LAYERS * 8, channels).astype(F32)
    slot = jnp.pad(jnp.stack([lengths, offsets], 1), ((0, 7), (0, 126)))
    def col(weight, layer, width, t):
        size = (1, weight.shape[1], width)
        return lax.dynamic_slice(weight, (layer, 0, t * width), size)[0]

    def chunk(weight, layer, t):
        size = weight.shape[1] // tp
        return lax.dynamic_slice(weight, (layer, t * size, 0), (1, size, weight.shape[2]))[0]

    def below(rows, twice):
        rest, blocks = mlp_split(rows.shape[1], twice)
        low = rows.shape[0] // blocks
        side = [rows[i * low : (i + 1) * low, twice:] for i in range(blocks)]
        return jnp.concatenate([rows[:, :twice], jnp.concatenate(side, 1)], 0)

    def rec_rows(l, t):
        out = chunk(out_proj, l, t)
        gates = jnp.concatenate([chunk(rate_proj, l, t), chunk(admit_proj, l, t)], 1)
        out = [out[:, i * 2 * head : (i + 1) * 2 * head] for i in range(3)] + [gates]
        return jnp.concatenate(out, 0)

    def rec_pack(l, rows_of, t):
        rec = jnp.concatenate([col(branch_proj, l, head, t), col(stream_proj, l, head, t)], 1)
        return jnp.concatenate([rec, rows_of], 0)

    def unit_chunk(t, plane):
        return t // seq * seq + (t + plane) % seq

    def mlp_rows(l, t):
        return below(chunk(mlp_down, l, unit_chunk(t, z)), 2 * units)

    def mlp_pack(l, t):
        rows_of, part = mlp_gate.shape[1], units // seq
        cols = [
            lax.dynamic_slice(
                weight, (l, 0, (p * tp + unit_chunk(t, p)) * part), (1, rows_of, part)
            )[0]
            for weight in (mlp_gate, mlp_up)
            for p in range(seq)
        ]
        return jnp.concatenate([jnp.concatenate(cols, 1), mlp_rows(l, t)], 0)

    pack = rec_pack(0, owner_chunks(plan, rec_rows(0, t)), t)
    mlp = mlp_pack(0, t)
    smalls, gains, layout, normed, rec = opening(
        seq, block_input, small, norm_gains.reshape(2 * LAYERS, -1).astype(F32), slot, pack
    )
    t, mlp, rec = lax.optimization_barrier((t, mlp, rec))
    layout = layout[:, 0, :2]
    gains = jnp.moveaxis(gains, 0, 1).reshape(LAYERS, 2, -1)
    smalls = jnp.moveaxis(smalls, 0, 1).reshape(LAYERS, 8, -1)
    smalls = lax.dynamic_slice_in_dim(smalls, t * head, head, 2)


    residual = block_input.astype(F32)
    saved_all, weights = [], []
    for l in range(LAYERS):
        if l > 0:
            mlp, normed = lax.optimization_barrier((mlp, normed))
        w = dict(
            gain=gains[l],
            small=jnp.concatenate([smalls[l, :7], -8.0 * jax.nn.softplus(-smalls[l, 7:])], 0),
            decay=smalls[l, 7:],
            rec=rec,
            mlp=lax.all_gather(mlp, "seq"),
        )
        weights.append(w)
        kept = rec_forward(normed, residual, w["gain"][1], w["rec"], w["small"], layout)
        middle, normed_two, *kept = kept
        if l + 1 < LAYERS:
            t, normed_two = lax.optimization_barrier((t, normed_two))
            pack = rec_pack(l + 1, owner_chunks(plan, rec_rows(l + 1, t)), t)
            mlp, pack, normed_two = lax.optimization_barrier((mlp_pack(l + 1, t), pack, normed_two))
            rec = lax.all_gather(pack, "seq")
        output, normed, *kept_two = mlp_forward(
            normed_two, middle, gains[(l + 1) % LAYERS, 0], w["mlp"]
        )
        saved_all.append((residual, kept, middle, kept_two))
        residual = output
    positions = z * rows + jnp.arange(rows, dtype=jnp.int32)
    inside = (positions >= offsets[0]) & (positions < offsets[0] + lengths[0])
    gradient = cotangent.astype(F32) * inside.astype(F32)[:, None]

    gradient_low = gradient.astype(BF)
    shares = [None] * LAYERS
    channel_all, gain_all = [None] * LAYERS, [None] * LAYERS
    for l in reversed(range(LAYERS)):
        gradient, gradient_low, shares[l], channel_all[l], gain_all[l], pending = layer_backward(
            gradient, gradient_low, weights[l], saved_all[l], layout,
            ((), ()) if l + 1 == LAYERS else shares[l + 1],
        )
        if l + 1 < LAYERS:
            shares[l + 1] = pending
    width = block_input.shape[1]
    base = width // seq

    def by_slot(share):
        return share[:base].reshape(tp, -1, share.shape[1])

    blocks = [by_slot(shares[l][0]) for l in range(LAYERS)]
    blocks += [by_slot(shares[l][1]) for l in range(1, LAYERS)]
    gains, channel, *blocks = closing(
        seq, jnp.concatenate(gain_all, 0), jnp.concatenate(channel_all, 0),
        [shares[l][0][base:] for l in range(LAYERS)], blocks,
    )
    blocks, downs = blocks[:-LAYERS], blocks[-LAYERS:]
    last = lax.all_to_all(
        by_slot(shares[0][1]), "rep", split_axis=0, concat_axis=0, axis_index_groups=plan.tp_groups
    )
    mlps, recs = blocks[:LAYERS], [last] + blocks[LAYERS:]
    outs = [
        owned_grads(plan, downs[l], shares[l][1], mlps[l], recs[l], width, head, units)
        for l in range(LAYERS)
    ]
    big = [jnp.stack([outs[l][i] for l in range(LAYERS)]) for i in range(8)]

    channel = lax.dynamic_slice_in_dim(channel, z * (head // seq), head // seq, 1)
    channel = to_owners(plan, channel, 1).reshape(LAYERS, 8, -1)
    if dp > 1:
        gains = lax.psum(gains, "rep", axis_index_groups=plan.dp_groups)
    own = gains.shape[1] // (plan.rep * seq)
    owner = lax.axis_index(("rep", "seq"))
    gains = lax.dynamic_slice_in_dim(gains, owner * own, own, 1).reshape(LAYERS, 2, own)
    return (
        residual.astype(BF),
        gradient,
        gains,
        big[0],
        big[1],
        channel[:, :CONV],
        channel[:, CONV],
        big[2],
        big[3],
        channel[:, CONV + 1 : CONV + 3],
        channel[:, CONV + 3],
        big[4],
        big[5],
        big[6],
        big[7],
    )


def solution(mesh):
    tokens = P(("rep", "seq"), None)
    rows = P(None, "seq", None)
    last3 = P(None, None, "seq")
    last2 = P(None, "seq")
    own_rows = P(None, ("rep", "seq"), None)
    own3 = P(None, None, ("rep", "seq"))
    own2 = P(None, ("rep", "seq"))

    def whole(*args):
        heads = args[9].shape[1] // args[9].shape[2]
        plan = Plan(mesh, heads)
        return jax.shard_map(
            partial(local, plan),
            mesh=mesh,
            in_specs=(
                tokens, tokens, P("rep"), P("rep"), last3, rows, rows, last3, last2, rows, rows,
                last3, last2, rows, rows, rows, rows,
            ),
            out_specs=(
                tokens, tokens, own3, own_rows, own_rows, own3, own2, own_rows, own_rows, own3,
                own2, own_rows, own_rows, own_rows, own_rows,
            ),
            check_vma=False,
        )(*args)

    return whole
```

```python
from functools import partial

import jax
import jax.numpy as jnp
from jax import lax
from jax.experimental import pallas as pl
from jax.experimental.pallas import tpu as pltpu
from jax.sharding import PartitionSpec as P

CONV = 4
LAYERS = 2
EPSILON = 1e-06
BF = jnp.bfloat16
F32 = jnp.float32


def dot(a, b):
    return jnp.dot(a, b, preferred_element_type=F32)


def dot_tn(a, b):
    return lax.dot_general(a, b, (((0,), (0,)), ((), ())), preferred_element_type=F32)


def dot_nt(a, b):
    return lax.dot_general(a, b, (((1,), (1,)), ((), ())), preferred_element_type=F32)


def glu_product(gate_in, value_in):
    return jax.nn.gelu(gate_in, approximate=True) * value_in


class Plan:
    def __init__(self, mesh, heads):
        self.rep = mesh.shape["rep"]
        self.seq = mesh.shape["seq"]
        self.tp = min(heads, self.rep)
        self.dp = self.rep // self.tp
        tp, dp = self.tp, self.dp
        self.tp_groups = None if dp == 1 else [[d * tp + t for t in range(tp)] for d in range(dp)]
        self.dp_groups = [[d * tp + t for d in range(dp)] for t in range(tp)]


def owner_chunks(plan, value):
    tp, seq = plan.tp, plan.seq
    pairs = []
    for d in range(plan.dp):
        for j in range(tp):
            for z in range(seq):
                o = tp * z + j
                pairs.append(((d * tp + j) * seq + z, (d * tp + o // seq) * seq + o % seq))
    return lax.ppermute(value, ("rep", "seq"), pairs)


def to_owners(plan, chunk, axis):
    if plan.dp == 1:
        return chunk
    part = lax.psum_scatter(
        chunk, "rep", scatter_dimension=axis, tiled=True, axis_index_groups=plan.dp_groups
    )
    tp, seq, dp = plan.tp, plan.seq, plan.dp
    pairs = [
        ((d * tp + t) * seq + z, (t * seq + z) * dp + d)
        for d in range(dp)
        for t in range(tp)
        for z in range(seq)
    ]
    return lax.ppermute(part, ("rep", "seq"), pairs)


MESH = pl.DeviceIdType.MESH
ANY = pl.BlockSpec(memory_space=pl.ANY)
VM = pl.BlockSpec(memory_space=pltpu.VMEM)
TP = 8
LATER = 3


class Net:
    def __init__(self):
        rep = lax.axis_index("rep")
        self.z = lax.axis_index("seq")
        self.t = lax.rem(rep, TP)
        self.base = rep - self.t
        chip = self.t // 2
        self.k = lax.rem(self.t, 2)
        self.b0 = lax.rem(chip, 2)
        self.b1 = chip // 2

    def slot(self, m, s):
        b0 = lax.rem(self.b0 + m % 2, 2)
        b1 = lax.rem(self.b1 + m // 2, 2)
        return (b1 * 2 + b0) * 2 + lax.rem(self.k + s, 2)

    def device(self, m, s):
        return (self.base + self.slot(m, s), self.z)

    def enter(self, extra=()):
        barrier = pltpu.get_barrier_semaphore()
        devices = [self.device(1, 0), self.device(2, 0), self.device(0, 1)] + list(extra)
        for device in devices:
            pl.semaphore_signal(barrier, inc=1, device_id=device, device_id_type=MESH)
        pl.semaphore_wait(barrier, len(devices))


def remote(src, dst, send, recv, device):
    return pltpu.make_async_remote_copy(
        src_ref=src, dst_ref=dst, send_sem=send, recv_sem=recv, device_id=device,
        device_id_type=MESH,
    )


class Gather:
    def __init__(self, net, full, send, recv):
        self.net, self.full, self.send, self.recv = net, full, send, recv
        half = full.shape[1] // 2
        a, b, whole = pl.ds(0, half), pl.ds(half, half), pl.ds(0, 2 * half)
        x, y, sib = net.device(1, 0), net.device(2, 0), net.device(0, 1)
        self.plan = [
            (0, a, x, 1), (0, b, y, 2), (0, b, x, 1), (0, a, y, 2), (2, b, x, 3), (1, a, y, 3),
            (0, whole, sib, 0), (1, whole, sib, 1), (2, whole, sib, 2), (3, whole, sib, 3),
        ]

    def copy(self, i):
        m, rows, to, _ = self.plan[i]
        at = self.full.at[self.net.slot(m, 0), rows]
        return remote(at, at, self.send.at[i], self.recv.at[i], to)

    def arrived(self, i):
        _, rows, to, m = self.plan[i]
        at = self.full.at[self.net.slot(m, 0 if i < 6 else 1), rows]
        remote(at, at, self.send.at[i], self.recv.at[i], to).wait_recv()

    def begin(self):
        for i in (0, 1, 2, 3, 6):
            self.copy(i).start()

    def before(self, n):
        if n == 1:
            self.arrived(6)
        if n == 2:
            self.arrived(0)
            self.copy(5).start()
            self.arrived(1)
            self.copy(4).start()
            self.arrived(2)
            self.copy(7).start()
        if n == 3:
            self.arrived(7)
        if n == 4:
            self.arrived(3)
            self.copy(8).start()
        if n == 5:
            self.arrived(8)
        if n == 6:
            self.arrived(4)
            self.arrived(5)
            self.copy(9).start()
        if n == 7:
            self.arrived(9)

    def finish(self):
        for i in range(10):
            self.copy(i).wait_send()


class Scatter:
    def __init__(self, net, part, near, wide, far, send, recv):
        self.net, self.part, self.near = net, part, near
        self.wide, self.far, self.send, self.recv = wide, far, send, recv
        self.rows = part.shape[2]
        half = self.rows // 2
        a, b, whole = pl.ds(0, half), pl.ds(half, half), pl.ds(0, 2 * half)
        self.a, self.b = a, b
        x, y, sib = net.device(1, 0), net.device(2, 0), net.device(0, 1)
        self.plan = [
            (part.at[1, m], near.at[m], sib) for m in range(4)
        ] + [
            (part.at[0, 3, a], wide.at[0], x),
            (part.at[0, 3, b], wide.at[1], y),
            (part.at[0, 1, a], far.at[0, a], x),
            (part.at[0, 2, b], far.at[1, b], y),
            (part.at[0, 1, b], far.at[0, b], x),
            (part.at[0, 2, a], far.at[1, a], y),
        ]

    def copy(self, i):
        src, dst, to = self.plan[i]
        return remote(src, dst, self.send.at[i], self.recv.at[i], to)

    def add(self, m, start, count, other):
        def some(i, carry):
            at = pl.ds(pl.multiple_of(start + i * 64, 64), 64)
            from_at = pl.ds(pl.multiple_of(i * 64, 64), 64)
            total = self.part[0, m, at].astype(F32) + other[from_at].astype(F32)
            self.part[0, m, at] = total.astype(BF)
            return carry

        lax.fori_loop(0, count // 64, some, 0)

    def after(self, n):
        if n == 1:
            self.copy(0).start()
        if n == 3:
            self.copy(1).start()
        if n == 4:
            self.copy(1).wait_recv()
            self.add(1, 0, self.rows, self.near.at[1])
            self.copy(6).start()
        if n == 5:
            self.copy(2).start()
        if n == 6:
            self.copy(2).wait_recv()
            self.add(2, 0, self.rows, self.near.at[2])
            self.copy(7).start()
        if n == 7:
            self.copy(3).start()

    def corner(self):
        self.copy(3).wait_recv()
        self.add(3, 0, self.rows, self.near.at[3])
        self.copy(4).start()
        self.copy(5).start()

    def edges(self):
        half = self.rows // 2
        self.copy(4).wait_recv()
        self.add(2, 0, half, self.wide.at[0])
        self.copy(9).start()
        self.copy(5).wait_recv()
        self.add(1, half, half, self.wide.at[1])
        self.copy(8).start()
        self.copy(0).wait_recv()

    def finish(self):
        for i in (6, 7, 8, 9):
            self.copy(i).wait_recv()
        for i in range(10):
            self.copy(i).wait_send()

    def total(self, at):
        own = self.part[0, 0, at].astype(F32) + self.near[0, at].astype(F32)
        return own + self.far[0, at].astype(F32) + self.far[1, at].astype(F32)


class Exchange:
    def __init__(self, net, seq, blocks, moved, rows_in, rows_out, send, recv, own):
        self.net = net
        self.blocks, self.moved, self.rows_in, self.rows_out = blocks, moved, rows_in, rows_out
        self.send, self.recv, self.own = send, recv, own
        self.others = [(m, s) for m in range(4) for s in range(2)][1:]
        each = TP // seq
        self.owner = lax.rem(net.z + TP - net.t, seq) * each + net.t // seq
        self.giver = lax.rem(net.t, each) * seq + lax.rem(net.z + TP - net.t // each, seq)

    def pushes(self, arriving=False):
        copies = []
        for block, out in zip(self.blocks, self.moved):
            for m, s in self.others:
                n, slot = len(copies), self.net.slot(m, s)
                copies.append(
                    remote(
                        block.at[slot], out.at[slot if arriving else self.net.t],
                        self.send.at[n], self.recv.at[n], self.net.device(m, s),
                    )
                )
        return copies

    def rows(self):
        first = len(self.blocks) * len(self.others)
        to = (self.net.base + self.owner, self.net.z)
        return [
            remote(src, dst, self.send.at[first + n], self.recv.at[first + n], to)
            for n, (src, dst) in enumerate(zip(self.rows_in, self.rows_out))
        ]

    def kept(self):
        copies = []
        for block, out in zip(self.blocks, self.moved):
            at = self.own.at[len(copies)]
            copies.append(pltpu.make_async_copy(block.at[self.net.t], out.at[self.net.t], at))
        return copies

    def rows_kept(self):
        first = len(self.blocks)
        return [
            pltpu.make_async_copy(src, dst, self.own.at[first + n])
            for n, (src, dst) in enumerate(zip(self.rows_in, self.rows_out))
        ]

    def begin(self):
        for copy in self.kept() + self.pushes():
            copy.start()

        @pl.when(self.owner != self.net.t)
        def _():
            for copy in self.rows():
                copy.start()

        @pl.when(self.owner == self.net.t)
        def _():
            for copy in self.rows_kept():
                copy.start()

    def finish(self):
        for copy in self.pushes(arriving=True):
            copy.wait_recv()
        for copy in self.pushes():
            copy.wait_send()
        for copy in self.kept():
            copy.wait()

        @pl.when(self.owner != self.net.t)
        def _():
            for copy in self.rows():
                copy.wait_send()

        @pl.when(self.owner == self.net.t)
        def _():
            for copy in self.rows_kept():
                copy.wait()

        @pl.when(self.giver != self.net.t)
        def _():
            for copy in self.rows():
                copy.wait_recv()


def exchange_scratch(blocks, rows):
    dma, count = pltpu.SemaphoreType.DMA, (TP - 1) * len(blocks) + len(rows)
    return [dma((count,)), dma((count,)), dma((len(blocks) + len(rows),))]


def plane_scratch(rows, width):
    dma = pltpu.SemaphoreType.DMA
    return [
        pltpu.VMEM((TP, rows, width), BF),
        pltpu.VMEM((2, 4, rows, width), BF),
        pltpu.VMEM((4, rows, width), BF),
        pltpu.VMEM((2, rows // 2, width), BF),
        pltpu.VMEM((2, rows, width), BF),
        dma((10,)), dma((10,)), dma((10,)), dma((10,)),
    ]


def steps(gather, scatter, compute):
    def one(i, carry):
        for n in range(1, 2 * 4):
            @pl.when(i == n)
            def _():
                if gather is not None:
                    gather.before(n)

        compute(i // 2, lax.rem(i, 2))
        for n in range(2 * 4):
            @pl.when(i == n)
            def _():
                if scatter is not None:
                    scatter.after(n)

        return carry

    lax.fori_loop(0, 2 * 4, one, 0)


def end_forward(scatter, residual, gain, out, normed):
    rows, chunk = out.shape[0], 32

    def some(i, carry):
        at = pl.ds(pl.multiple_of(i * chunk, chunk), chunk)
        value = residual[at] + scatter.total(at)
        out[at] = value
        scale = lax.rsqrt(jnp.mean(value * value, axis=-1, keepdims=True) + EPSILON)
        normed[at] = (value * scale * gain[...]).astype(BF)
        return carry

    lax.fori_loop(0, rows // chunk, some, 0)


def end_backward(scatter, upstream, values, gain, grad, grad_low, grad_gain):
    rows, chunk = grad.shape[0], 32
    grad_gain[...] = jnp.zeros_like(grad_gain)

    def some(i, carry):
        at = pl.ds(pl.multiple_of(i * chunk, chunk), chunk)
        value, given = values[at], scatter.total(at)
        scale = lax.rsqrt(jnp.mean(value * value, axis=-1, keepdims=True) + EPSILON)
        scaled = given * gain[...]
        mean = jnp.mean(value * scaled, axis=-1, keepdims=True)
        result = upstream[at] + scale * scaled - value * (scale * scale * scale * mean)
        grad[at] = result
        grad_low[at] = result.astype(BF)
        grad_gain[...] += jnp.sum(given * value * scale, axis=0, keepdims=True)
        return carry

    lax.fori_loop(0, rows // chunk, some, 0)


GELU_A = 0.7978845608028654
GELU_B = 0.044715


def gelu_parts(v):
    square = v * v
    tanh = jnp.tanh(GELU_A * (v + GELU_B * v * square))
    half = 0.5 * (1.0 + tanh)
    slope = half + 0.5 * v * (1.0 - tanh * tanh) * (GELU_A * (1.0 + 3.0 * GELU_B * square))
    return v * half, slope


def copy_list(pairs, sem, first):
    return [
        pltpu.make_async_copy(src, dst, sem.at[first + n]) for n, (src, dst) in enumerate(pairs)
    ]


def unpack_rec(pack, col, wout, gates, sem, first):
    seq, both = pack.shape[0], pack.shape[2]
    rows, part = col.shape[0] // seq, gates.shape[0] // seq
    pairs = []
    for z in range(seq):
        pairs.append((pack.at[z, pl.ds(0, rows)], col.at[pl.ds(z * rows, rows)]))
        own = pl.ds(z * part, part)
        for j in range(3):
            pairs.append(
                (pack.at[z, pl.ds(rows + j * part, part)], wout.at[own, pl.ds(j * both, both)])
            )
        pairs.append((pack.at[z, pl.ds(rows + 3 * part, part)], gates.at[own]))
    return copy_list(pairs, sem, first)


def mlp_split(width, twice):
    rest = width - twice
    return rest, twice // rest


def unpack_mlp(pack, col, down, sem, first):
    seq, twice = pack.shape[0], pack.shape[2]
    rows, part = col.shape[0] // seq, down.shape[0] // seq
    rest, blocks = mlp_split(down.shape[1], twice)
    low = part // blocks
    pairs = []
    for z in range(seq):
        pairs.append((pack.at[z, pl.ds(0, rows)], col.at[pl.ds(z * rows, rows)]))
        pairs.append(
            (pack.at[z, pl.ds(rows, part)], down.at[pl.ds(z * part, part), pl.ds(0, twice)])
        )
        for n in range(blocks):
            pairs.append(
                (
                    pack.at[z, pl.ds(rows + part, low), pl.ds(n * rest, rest)],
                    down.at[pl.ds(z * part + n * low, low), pl.ds(twice, rest)],
                )
            )
    return copy_list(pairs, sem, first)


def mlp_forward_kernel(
    x_ref, residual_ref, gain_ref, pack_ref,
    out_ref, normed_ref, full_out, up_out,
    full, part, near, wide, far, gs, gr, ss, sr, col, wd, ups, sem,
):
    net = Net()
    gather = Gather(net, full, gs, gr)
    scatter = Scatter(net, part, near, wide, far, ss, sr)
    n = 5 * pack_ref.shape[0]
    own = pltpu.make_async_copy(x_ref, full.at[net.t], sem.at[n])
    own.start()
    weights = unpack_mlp(pack_ref, col, wd, sem, 0)
    for copy in weights:
        copy.start()
    net.enter()
    own.wait()
    gather.begin()
    for copy in weights:
        copy.wait()

    units = wd.shape[0]

    def compute(m, s):
        slot = net.slot(m, s)
        x = full[slot]
        up = dot(x, col[...])
        ups[slot] = up.astype(BF)
        hidden = glu_product(up[:, :units], up[:, units:]).astype(BF)
        part[s, m] = dot(hidden, wd[...]).astype(BF)

    steps(gather, scatter, compute)
    saves = [
        pltpu.make_async_copy(full, full_out, sem.at[n + 1]),
        pltpu.make_async_copy(ups, up_out, sem.at[n + 2]),
    ]
    for copy in saves:
        copy.start()
    scatter.corner()
    scatter.edges()
    scatter.finish()
    end_forward(scatter, residual_ref, gain_ref, out_ref, normed_ref)
    gather.finish()
    for copy in saves:
        copy.wait()


def mlp_forward(x, residual, gain, pack):
    rows, width = x.shape
    seq, _, twice = pack.shape
    shape = jax.ShapeDtypeStruct
    return pl.pallas_call(
        mlp_forward_kernel,
        in_specs=[ANY, VM, VM, ANY],
        out_specs=[VM, VM, ANY, ANY],
        out_shape=[
            shape((rows, width), F32),
            shape((rows, width), BF),
            shape((TP, rows, width), BF),
            shape((TP, rows, twice), BF),
        ],
        scratch_shapes=plane_scratch(rows, width)
        + [
            pltpu.VMEM((width, twice), BF),
            pltpu.VMEM((twice // 2, width), BF),
            pltpu.VMEM((TP, rows, twice), BF),
            pltpu.SemaphoreType.DMA((5 * seq + 4,)),
        ],
        compiler_params=pltpu.CompilerParams(
            collective_id=1, has_side_effects=True, vmem_limit_bytes=58 << 20
        ),
        cost_estimate=pl.CostEstimate(
            flops=60 * 10**9, bytes_accessed=30 << 20, transcendentals=0
        ),
        name="mlp_forward",
    )(x, residual, gain.reshape(1, -1), pack)


def mlp_backward_kernel(
    g_ref, upstream_ref, values_ref, gain_ref, pack_ref, x_ref, up_ref,
    grad_ref, low_ref, gain_out, gcol_ref,
    full, part, near, wide, far, gs, gr, ss, sr, col, wd, xs, ups, hid, sem,
):
    net = Net()
    gather = Gather(net, full, gs, gr)
    scatter = Scatter(net, part, near, wide, far, ss, sr)
    seq = pack_ref.shape[0]
    n = 5 * seq
    own = pltpu.make_async_copy(g_ref, full.at[net.t], sem.at[n])
    own.start()
    loads = unpack_mlp(pack_ref, col, wd, sem, 0) + [
        pltpu.make_async_copy(up_ref, ups, sem.at[n + 1]),
    ]
    late = pltpu.make_async_copy(x_ref, xs, sem.at[n + 3])
    for copy in loads + [late]:
        copy.start()
    net.enter()
    own.wait()
    gather.begin()
    for copy in loads:
        copy.wait()
    rows, units = full.shape[1], wd.shape[0]

    def compute(m, s):
        slot = net.slot(m, s)
        at = pl.ds(pl.multiple_of(slot * rows, rows), rows)
        grad_hidden = dot_nt(full[slot], wd[...])
        up = ups[at].astype(F32)
        act, slope = gelu_parts(up[:, :units])
        up_value = up[:, units:]
        hid[at] = (act * up_value).astype(BF)
        grads = jnp.concatenate([grad_hidden * up_value * slope, grad_hidden * act], 1).astype(BF)
        ups[at] = grads
        part[s, m] = dot_nt(grads, col[...]).astype(BF)

    steps(gather, scatter, compute)
    late.wait()
    scatter.corner()
    width = full.shape[2]
    own_rows = width // (TP * seq)
    tile = 2 * seq * own_rows
    base = width // seq

    def columns(j, carry):
        x = xs[:, pl.ds(pl.multiple_of(j * tile, 128), tile)]
        product = dot_tn(x, ups[...]).astype(BF)
        for r in range(2):
            for z in range(seq):
                low = (r * seq + z) * own_rows
                at = pl.ds(pl.multiple_of((2 * j + r) * own_rows, own_rows), own_rows)
                gcol_ref[z, at] = product[low : low + own_rows]
        return carry

    lax.fori_loop(0, TP // 2, columns, 0)
    scatter.edges()

    tokens = full.shape[0] * rows
    part_units = units // seq
    rest, blocks = mlp_split(width, 2 * units)
    low = part_units // blocks
    hidden = hid[...]
    for first in range(0, width, width // 2):
        at = pl.ds(first, width // 2)
        product = dot_tn(hidden, full[:, :, at].reshape(tokens, width // 2)).astype(BF)
        beside = min(2 * units - first, width // 2)
        for z in range(seq):
            own = product[z * part_units : (z + 1) * part_units]
            to = lax.rem(net.t + z, seq)
            gcol_ref[to, base : base + part_units, first : first + beside] = own[:, :beside]
            if beside < width // 2:
                for n in range(blocks):
                    gcol_ref[to, base + part_units :, n * rest : (n + 1) * rest] = own[
                        n * low : (n + 1) * low, beside:
                    ]
    scatter.finish()
    end_backward(scatter, upstream_ref, values_ref, gain_ref, grad_ref, low_ref, gain_out)
    gather.finish()


def mlp_backward(g, upstream, values, gain, pack, x, up):
    rows, width = g.shape
    seq, _, twice = pack.shape
    tokens = TP * rows
    shape = jax.ShapeDtypeStruct
    return pl.pallas_call(
        mlp_backward_kernel,
        in_specs=[ANY, VM, VM, VM, ANY, ANY, ANY],
        out_specs=[VM, VM, VM, VM],
        out_shape=[
            shape((rows, width), F32),
            shape((rows, width), BF),
            shape((1, width), F32),
            shape(pack.shape, BF),
        ],
        scratch_shapes=plane_scratch(rows, width)
        + [
            pltpu.VMEM((width, twice), BF),
            pltpu.VMEM((twice // 2, width), BF),
            pltpu.VMEM((tokens, width), BF),
            pltpu.VMEM((tokens, twice), BF),
            pltpu.VMEM((tokens, twice // 2), BF),
            pltpu.SemaphoreType.DMA((5 * seq + 4,)),
        ],
        compiler_params=pltpu.CompilerParams(
            collective_id=2, has_side_effects=True, vmem_limit_bytes=60 << 20
        ),
        cost_estimate=pl.CostEstimate(
            flops=70 * 10**9, bytes_accessed=30 << 20, transcendentals=0
        ),
        name="mlp_backward",
    )(
        g, upstream, values, gain.reshape(1, -1), pack, x.reshape(tokens, width),
        up.reshape(tokens, twice),
    )


def after_corner_first(scatter, n):
    if n % 2 == 0:
        scatter.copy(3 - n // 2).start()
    if n == 3:
        scatter.corner()
    if n == 5:
        scatter.copy(2).wait_recv()
        scatter.add(2, 0, scatter.rows, scatter.near.at[2])
        scatter.copy(7).start()
    if n == 7:
        scatter.copy(1).wait_recv()
        scatter.add(1, 0, scatter.rows, scatter.near.at[1])
        scatter.copy(6).start()


class Line:
    def __init__(self, net, count):
        self.net, self.count = net, count
        self.others = [(net.base + net.t, lax.rem(net.z + d, count)) for d in range(1, count)]
        self.next = (net.base + net.t, net.z + 1)
        self.before = (net.base + net.t, net.z - 1)

    def to_all(self, ends, send, recv):
        at = ends.at[self.net.z]
        copies = [
            remote(at, at, send.at[d], recv.at[d], to) for d, to in enumerate(self.others)
        ]
        for copy in copies:
            copy.start()
        for d, copy in enumerate(copies):
            source = lax.rem(self.net.z + self.count - 1 - d, self.count)
            from_at = ends.at[source]
            remote(from_at, from_at, send.at[d], recv.at[d], self.others[d]).wait_recv()
        for copy in copies:
            copy.wait_send()


def inside_of(positions, offset, length):
    return jnp.where((positions >= offset) & (positions < offset + length), 1.0, 0.0)


def read_halves(ref, at):
    return jnp.concatenate([ref[n, at] for n in range(ref.shape[0])], 1)


def write_halves(ref, at, value):
    for n in range(ref.shape[0]):
        ref[n, at] = value[:, n * 128 : (n + 1) * 128]


def one_minus_exp(v):
    series = 1.0 + v * (1.0 / 7.0)
    for n in (6.0, 5.0, 4.0, 3.0, 2.0):
        series = 1.0 + v * (1.0 / n) * series
    return jnp.where(v > -0.35, -v * series, 1.0 - jnp.exp(v))


def sigmoid(v):
    return 1.0 / (1.0 + jnp.exp(-v))


def rec_forward_kernel(
    gathered,
    x_ref, residual_ref, gain_ref, pack_ref, small_ref, slots_ref,
    out_ref, normed_ref, full_out, branch_out, stream_out, conv_out, state_out,
    full, part, near, wide, far, gs, gr, ss, sr,
    col, gates, wout, branch, stream, conv, state, retain, inflow, ends, carry, hs, hr, es, er, sem,
):
    net = Net()
    seq = ends.shape[0]
    line = Line(net, seq)
    gather = Gather(net, full, gs, gr)
    scatter = Scatter(net, part, near, wide, far, ss, sr)
    rows = full.shape[1]
    head = gates.shape[0]
    own = pltpu.make_async_copy(x_ref, full if gathered else full.at[net.t], sem.at[0])
    loads = unpack_rec(pack_ref, col, wout, gates, sem, 9)
    for load in [own] + loads:
        load.start()
    net.enter(line.others)
    own.wait()
    if not gathered:
        gather.begin()

    @pl.when(net.z == 0)
    def _():
        stream[:, pl.ds(0, 8), :] = jnp.zeros((TP, 8, head), F32)

    for load in loads:
        load.wait()

    def halo(i):
        slot = net.slot(i // 2, lax.rem(i, 2))
        return remote(
            stream.at[slot, pl.ds(rows, 8)], stream.at[slot, pl.ds(0, 8)],
            hs.at[i], hr.at[i], line.next,
        )

    def project(i):
        slot = net.slot(i // 2, lax.rem(i, 2))
        both = dot(full[slot], col[...])
        branch[slot] = both[:, :head]
        stream[slot, pl.ds(8, rows)] = both[:, head:]

        @pl.when(net.z < seq - 1)
        def _():
            halo(i).start()

    def gate(i):
        slot = net.slot(i // 2, lax.rem(i, 2))

        @pl.when(net.z > 0)
        def _():
            halo(i).wait_recv()

        length, offset = slots_ref[slot, 0], slots_ref[slot, 1]
        positions = net.z * rows + lax.broadcasted_iota(jnp.int32, (rows, head), 0)
        inside = inside_of(positions, offset, length)
        mixed = small_ref[pl.ds(CONV, 1), :] + small_ref[pl.ds(0, 1), :] * stream[slot, pl.ds(8, rows)]
        restart = positions == 0
        for j in range(1, CONV):
            same = jnp.where(inside == inside_of(positions - j, offset, length), 1.0, 0.0)
            if j == 1:
                restart = restart | (same == 0.0)
            mixed += small_ref[pl.ds(j, 1), :] * stream[slot, pl.ds(8 - j, rows)] * same
        low = mixed.astype(BF)
        conv[slot] = low
        pre = dot(low, gates[...])
        rate = sigmoid(pre[:, :head] + small_ref[pl.ds(CONV + 1, 1), :])
        admit = sigmoid(pre[:, head:] + small_ref[pl.ds(CONV + 2, 1), :])
        log_retain = rate * small_ref[pl.ds(CONV + 3, 1), :]
        at = pl.ds(pl.multiple_of(slot * rows, rows), rows)
        write_halves(retain, at, jnp.where(restart, 0.0, jnp.exp(log_retain)))
        scale = jnp.where(restart, 1.0, jnp.sqrt(one_minus_exp(2.0 * log_retain)))
        write_halves(inflow, at, scale * admit * low.astype(F32))

    def one(i, _):
        for n in range(1, TP):
            @pl.when(i == n)
            def _():
                if not gathered:
                    gather.before(n)

        @pl.when(i < TP)
        def _():
            project(i)

        @pl.when(i >= LATER)
        def _():
            gate(i - LATER)

        return 0

    lax.fori_loop(0, TP + LATER, one, 0)
    saves = [
        pltpu.make_async_copy(branch, branch_out, sem.at[5]),
        pltpu.make_async_copy(stream, stream_out, sem.at[6]),
        pltpu.make_async_copy(conv, conv_out, sem.at[7]),
    ]
    if not gathered:
        saves.append(pltpu.make_async_copy(full, full_out, sem.at[4]))
    for save in saves:
        save.start()

    lanes = [pl.ds(i, 128) for i in range(0, head, 128)]

    def step(p, carried):
        at = pl.ds(p, TP, stride=rows)
        result = []
        for n, (value, decay) in enumerate(carried):
            a = retain[n, at]
            value = a * value + inflow[n, at]
            decay = a * decay
            inflow[n, at] = value
            retain[n, at] = decay
            result.append((value, decay))
        return tuple(result)

    start = tuple((jnp.zeros((TP, 128), F32), jnp.ones((TP, 128), F32)) for _ in lanes)
    last = lax.fori_loop(0, rows, step, start, unroll=8)
    for lane, (value, decay) in zip(lanes, last):
        ends[net.z, pl.ds(0, TP), lane] = decay
        ends[net.z, pl.ds(TP, TP), lane] = value
    line.to_all(ends, es, er)
    entering = jnp.zeros((TP, head), F32)
    for z in range(seq - 1):
        later = ends[z, pl.ds(0, TP)] * entering + ends[z, pl.ds(TP, TP)]
        entering = jnp.where(z < net.z, later, entering)
    carry[...] = entering

    def join(i, _):
        m, s = 3 - i // 2, 1 - lax.rem(i, 2)
        slot = net.slot(m, s)
        at = pl.ds(pl.multiple_of(slot * rows, rows), rows)
        first = carry[pl.ds(slot, 1), :]
        states = read_halves(inflow, at) + read_halves(retain, at) * first
        state[slot, pl.ds(0, 8)] = jnp.broadcast_to(first, (8, head))
        state[slot, pl.ds(8, rows)] = states
        joined = glu_product(branch[slot], states).astype(BF)
        part[s, m] = dot(joined, wout[...]).astype(BF)
        for n in range(TP):
            @pl.when(i == n)
            def _():
                after_corner_first(scatter, n)

        return 0

    lax.fori_loop(0, TP, join, 0)
    saves.append(pltpu.make_async_copy(state, state_out, sem.at[8]))
    saves[-1].start()
    scatter.edges()

    @pl.when(net.z < seq - 1)
    def _():
        lax.fori_loop(0, TP, lambda i, _: (halo(i).wait_send(), 0)[1], 0)

    scatter.finish()
    end_forward(scatter, residual_ref, gain_ref, out_ref, normed_ref)
    if not gathered:
        gather.finish()
    for save in saves:
        save.wait()


def rec_scratch(pack, width):
    seq, _, both = pack.shape
    return [
        pltpu.VMEM((width, both), BF),
        pltpu.VMEM((both // 2, both), BF),
        pltpu.VMEM((both // 2, width), BF),
    ]


def rec_forward(x, residual, gain, pack, small, slots):
    gathered = x.ndim == 3
    rows, width = residual.shape
    seq, _, head = pack.shape
    head = head // 2
    shape = jax.ShapeDtypeStruct
    dma = pltpu.SemaphoreType.DMA
    tokens = TP * rows
    result = list(pl.pallas_call(
        partial(rec_forward_kernel, gathered),
        in_specs=[ANY, VM, VM, ANY, VM, pl.BlockSpec(memory_space=pltpu.SMEM)],
        out_specs=[VM, VM, ANY, ANY, ANY, ANY, ANY],
        out_shape=[
            shape((rows, width), F32),
            shape((rows, width), BF),
            shape((8, 128) if gathered else (TP, rows, width), BF),
            shape((TP, rows, head), F32),
            shape((TP, rows + 8, head), F32),
            shape((TP, rows, head), BF),
            shape((TP, rows + 8, head), F32),
        ],
        scratch_shapes=plane_scratch(rows, width)
        + rec_scratch(pack, width)
        + [
            pltpu.VMEM((TP, rows, head), F32),
            pltpu.VMEM((TP, rows + 8, head), F32),
            pltpu.VMEM((TP, rows, head), BF),
            pltpu.VMEM((TP, rows + 8, head), F32),
            pltpu.VMEM((head // 128, tokens, 128), F32),
            pltpu.VMEM((head // 128, tokens, 128), F32),
            pltpu.VMEM((seq, 2 * TP, head), F32),
            pltpu.VMEM((TP, head), F32),
            dma((TP,)), dma((TP,)), dma((seq - 1,)), dma((seq - 1,)), dma((9 + 5 * seq,)),
        ],
        compiler_params=pltpu.CompilerParams(
            collective_id=5 if gathered else 3, has_side_effects=True, vmem_limit_bytes=58 << 20
        ),
        cost_estimate=pl.CostEstimate(
            flops=70 * 10**9, bytes_accessed=30 << 20, transcendentals=0
        ),
        name="rec_forward_first" if gathered else "rec_forward",
    )(x, residual, gain.reshape(1, -1), pack, small, slots))
    if gathered:
        result[2] = x
    return result


def rec_backward_kernel(
    count, g_ref, upstream_ref, values_ref, gain_ref, pack_ref, small_ref, slots_ref,
    x_ref, branch_ref, stream_ref, conv_ref, state_ref, *refs
):
    given, refs = refs[:count], refs[count:]
    grad_ref, low_ref, gain_out, gcol_ref, channel_ref, *refs = refs
    taken, refs = refs[:count], refs[count:]
    (
        full, part, near, wide, far, gs, gr, ss, sr,
    col, gates, wout, xs, branch, stream, conv, state,
    retain, direct, suffix, joined, both, gpre, mixed, ends, carry, hs, hr, es, er, sem, *sems,
    ) = refs
    net = Net()
    seq = ends.shape[0]
    line = Line(net, seq)
    gather = Gather(net, full, gs, gr)
    scatter = Scatter(net, part, near, wide, far, ss, sr)
    rows, width = full.shape[1], full.shape[2]
    head = gates.shape[0]
    own = pltpu.make_async_copy(g_ref, full.at[net.t], sem.at[0])
    loads = [
        pltpu.make_async_copy(a, b, sem.at[1 + n])
        for n, (a, b) in enumerate(
            (
                (branch_ref, branch), (state_ref, state), (conv_ref, conv), (stream_ref, stream),
                (x_ref, xs),
            )
        )
    ]
    loads = unpack_rec(pack_ref, col, wout, gates, sem, 9) + loads
    for load in [own] + loads:
        load.start()
    if count:
        exchange = Exchange(
            net, seq, given[:-1], taken[:-1], given[-1:], taken[-1:], *sems
        )
        net.enter(
            line.others + [net.device(1, 1), net.device(2, 1), net.device(3, 0), net.device(3, 1)]
        )
    else:
        net.enter(line.others)
    own.wait()
    gather.begin()

    @pl.when(net.z == seq - 1)
    def _():
        mixed[:, pl.ds(rows, 8), :] = jnp.zeros((TP, 8, head), F32)

    channel_ref[...] = jnp.zeros_like(channel_ref)
    for load in loads[:-2]:
        load.wait()

    def gate_parts(slot):
        positions = net.z * rows + lax.broadcasted_iota(jnp.int32, (rows, head), 0)
        length, offset = slots_ref[slot, 0], slots_ref[slot, 1]
        inside = inside_of(positions, offset, length)
        restart = (positions == 0) | (inside != inside_of(positions - 1, offset, length))
        pre = dot(conv[slot], gates[...])
        rate = sigmoid(pre[:, :head] + small_ref[pl.ds(CONV + 1, 1), :])
        admit = sigmoid(pre[:, head:] + small_ref[pl.ds(CONV + 2, 1), :])
        log_retain = rate * small_ref[pl.ds(CONV + 3, 1), :]
        return positions, offset, length, inside, restart, rate, admit, log_retain

    def open_block(m, s):
        slot = net.slot(m, s)
        at = pl.ds(pl.multiple_of(slot * rows, rows), rows)
        grad_joined = dot_nt(full[slot], wout[...])
        act, slope = gelu_parts(branch[slot])
        states = state[slot, pl.ds(8, rows)]
        joined[at] = (act * states).astype(BF)
        both[at, :head] = (grad_joined * states * slope).astype(BF)
        write_halves(direct, at, grad_joined * act)
        _, _, _, _, restart, _, _, log_retain = gate_parts(slot)
        write_halves(retain, at, jnp.where(restart, 0.0, jnp.exp(log_retain)))

    steps(gather, None, open_block)
    if count:
        exchange.begin()
    lanes = [pl.ds(i, 128) for i in range(0, head, 128)]

    def step(i, carried):
        at = pl.ds(rows - 1 - i, TP, stride=rows)
        result = []
        for n, (value, decay, ahead) in enumerate(carried):
            value = ahead * value + direct[n, at]
            decay = ahead * decay
            direct[n, at] = value
            suffix[n, at] = decay
            result.append((value, decay, retain[n, at]))
        return tuple(result)

    one = jnp.minimum(retain[0, pl.ds(0, TP)] + 2.0, 1.0)
    last = lax.fori_loop(
        0, rows, step, tuple((jnp.zeros((TP, 128), F32), one, one) for _ in lanes), unroll=8
    )
    for lane, (value, decay, first) in zip(lanes, last):
        ends[net.z, pl.ds(0, TP), lane] = first * decay
        ends[net.z, pl.ds(TP, TP), lane] = first * value
    line.to_all(ends, es, er)
    entering = jnp.zeros((TP, head), F32)
    for z in range(seq - 1, 0, -1):
        earlier = ends[z, pl.ds(0, TP)] * entering + ends[z, pl.ds(TP, TP)]
        entering = jnp.where(z > net.z, earlier, entering)
    carry[...] = entering
    loads[-2].wait()

    def halo(i):
        slot = net.slot(3 - i // 2, 1 - lax.rem(i, 2))
        return remote(
            mixed.at[slot, pl.ds(0, 8)], mixed.at[slot, pl.ds(rows, 8)],
            hs.at[i], hr.at[i], line.before,
        )

    def through_gates(i):
        slot = net.slot(3 - i // 2, 1 - lax.rem(i, 2))
        at = pl.ds(pl.multiple_of(slot * rows, rows), rows)
        grad_states = read_halves(direct, at) + read_halves(suffix, at) * carry[pl.ds(slot, 1), :]
        positions, offset, length, inside, restart, rate, admit, log_retain = gate_parts(slot)
        low = conv[slot].astype(F32)
        kept = jnp.exp(log_retain)
        root = jnp.sqrt(one_minus_exp(2.0 * log_retain))
        scale = jnp.where(restart, 1.0, root)
        grad_admit = grad_states * scale * low
        grad_scale = grad_states * admit * low
        grad_log = grad_states * state[slot, pl.ds(7, rows)] * kept - grad_scale * kept * kept / root
        grad_log = jnp.where(restart, 0.0, grad_log)
        rate_part = grad_log * small_ref[pl.ds(CONV + 3, 1), :] * rate * (1.0 - rate)
        admit_part = grad_admit * admit * (1.0 - admit)
        gpre[at, :head] = rate_part.astype(BF)
        gpre[at, head:] = admit_part.astype(BF)
        grad_mixed = grad_states * scale * admit + dot_nt(gpre[at], gates[...])
        mixed[slot, pl.ds(0, rows)] = grad_mixed

        @pl.when(net.z > 0)
        def _():
            halo(i).start()

        sums = [jnp.sum(grad_mixed * stream[slot, pl.ds(8, rows)], axis=0, keepdims=True)]
        for j in range(1, CONV):
            same = jnp.where(inside == inside_of(positions - j, offset, length), 1.0, 0.0)
            sums.append(
                jnp.sum(
                    grad_mixed * stream[slot, pl.ds(8 - j, rows)] * same, axis=0, keepdims=True
                )
            )
        for term in (grad_mixed, rate_part, admit_part, grad_log * rate):
            sums.append(jnp.sum(term, axis=0, keepdims=True))
        for n, term in enumerate(sums):
            channel_ref[pl.ds(n, 1), :] += term

    def to_input(i):
        m, s = 3 - i // 2, 1 - lax.rem(i, 2)
        slot = net.slot(m, s)
        at = pl.ds(pl.multiple_of(slot * rows, rows), rows)

        @pl.when(net.z < seq - 1)
        def _():
            halo(i).wait_recv()

        positions = net.z * rows + lax.broadcasted_iota(jnp.int32, (rows, head), 0)
        length, offset = slots_ref[slot, 0], slots_ref[slot, 1]
        inside = inside_of(positions, offset, length)
        grad_stream = small_ref[pl.ds(0, 1), :] * mixed[slot, pl.ds(0, rows)]
        for j in range(1, CONV):
            same = jnp.where(inside == inside_of(positions + j, offset, length), 1.0, 0.0)
            grad_stream += small_ref[pl.ds(j, 1), :] * mixed[slot, pl.ds(j, rows)] * same
        both[at, head:] = grad_stream.astype(BF)
        part[s, m] = dot_nt(both[at], col[...]).astype(BF)

    def one_block(i, _):
        @pl.when(i < TP)
        def _():
            through_gates(i)

        @pl.when(i >= LATER)
        def _():
            to_input(i - LATER)

        for n in range(TP):
            @pl.when(i == n + LATER)
            def _():
                after_corner_first(scatter, n)

        return 0

    lax.fori_loop(0, TP + LATER, one_block, 0)
    scatter.edges()
    loads[-1].wait()
    own_rows = width // (TP * seq)
    tile = 2 * seq * own_rows

    def columns(j, _):
        x = xs[:, pl.ds(pl.multiple_of(j * tile, 128), tile)]
        product = dot_tn(x, both[...]).astype(BF)
        for r in range(2):
            for z in range(seq):
                low = (r * seq + z) * own_rows
                at = pl.ds(pl.multiple_of((2 * j + r) * own_rows, own_rows), own_rows)
                gcol_ref[z, at] = product[low : low + own_rows]
        return 0

    lax.fori_loop(0, TP // 2, columns, 0)
    low_conv = conv[...].reshape(TP * rows, head)
    product = dot_tn(low_conv, gpre[...]).astype(BF)
    third, base, part_head = width // 3, width // seq, head // seq
    for z in range(seq):
        low = base + 3 * part_head
        gcol_ref[z, low : low + part_head] = product[z * part_head : (z + 1) * part_head]
    for j in range(3):
        at = pl.ds(j * third, third)
        product = dot_tn(joined[...], full[:, :, at].reshape(TP * rows, third)).astype(BF)
        for z in range(seq):
            low = base + j * part_head
            gcol_ref[z, low : low + part_head] = product[z * part_head : (z + 1) * part_head]

    @pl.when(net.z > 0)
    def _():
        lax.fori_loop(0, TP, lambda i, _: (halo(i).wait_send(), 0)[1], 0)

    scatter.finish()
    if count:
        exchange.finish()
    end_backward(scatter, upstream_ref, values_ref, gain_ref, grad_ref, low_ref, gain_out)
    gather.finish()


def rec_backward(g, upstream, values, gain, pack, small, slots, saved, given):
    rows, width = g.shape
    seq, _, head = pack.shape
    head = head // 2
    tokens = TP * rows
    shape = jax.ShapeDtypeStruct
    dma = pltpu.SemaphoreType.DMA
    x, branch, stream, conv, state = saved
    return pl.pallas_call(
        partial(rec_backward_kernel, len(given)),
        in_specs=[ANY, VM, VM, VM, ANY, VM, pl.BlockSpec(memory_space=pltpu.SMEM)]
        + [ANY] * (5 + len(given)),
        out_specs=[VM] * 5 + [ANY] * len(given),
        out_shape=[
            shape((rows, width), F32),
            shape((rows, width), BF),
            shape((1, width), F32),
            shape(pack.shape, BF),
            shape((8, head), F32),
        ]
        + [shape(array.shape, array.dtype) for array in given],
        scratch_shapes=plane_scratch(rows, width)
        + rec_scratch(pack, width)
        + [
            pltpu.VMEM((tokens, width), BF),
            pltpu.VMEM(branch.shape, F32),
            pltpu.VMEM(stream.shape, F32),
            pltpu.VMEM(conv.shape, BF),
            pltpu.VMEM(state.shape, F32),
            pltpu.VMEM((head // 128, tokens, 128), F32),
            pltpu.VMEM((head // 128, tokens, 128), F32),
            pltpu.VMEM((head // 128, tokens, 128), F32),
            pltpu.VMEM((tokens, head), BF),
            pltpu.VMEM((tokens, 2 * head), BF),
            pltpu.VMEM((tokens, 2 * head), BF),
            pltpu.VMEM((TP, rows + 8, head), F32),
            pltpu.VMEM((seq, 2 * TP, head), F32),
            pltpu.VMEM((TP, head), F32),
            dma((TP,)), dma((TP,)), dma((seq - 1,)), dma((seq - 1,)), dma((9 + 5 * seq,)),
        ]
        + (exchange_scratch(given[:-1], given[-1:]) if given else []),
        compiler_params=pltpu.CompilerParams(
            collective_id=8 if given else 4, has_side_effects=True, vmem_limit_bytes=60 << 20
        ),
        cost_estimate=pl.CostEstimate(
            flops=80 * 10**9, bytes_accessed=30 << 20, transcendentals=0
        ),
        name="rec_backward_exchange" if given else "rec_backward",
    )(
        g, upstream, values, gain.reshape(1, -1), pack, small, slots,
        x.reshape(tokens, width), branch, stream, conv, state, *given,
    )


def open_kernel(
    x_ref, small_ref, gain_ref, slot_ref, pack_ref,
    small_out, gain_out, slot_out, full_out, pack_out,
    full, smalls, gains, slots, gs, gr, ps, pr, sem,
):
    net = Net()
    seq = smalls.shape[0]
    line = Line(net, seq)
    gather = Gather(net, full, gs, gr)
    plane = [net.device(m, s) for m in range(4) for s in range(2)][1:]
    mine = [
        pltpu.make_async_copy(small_ref, smalls.at[net.z], sem.at[0]),
        pltpu.make_async_copy(gain_ref, gains.at[net.z], sem.at[1]),
        pltpu.make_async_copy(slot_ref, slots.at[net.t], sem.at[2]),
    ]
    own_pack = pltpu.make_async_copy(pack_ref, pack_out.at[net.z], sem.at[4])
    for copy in mine + [own_pack]:
        copy.start()
    net.enter(line.others + [net.device(1, 1), net.device(2, 1), net.device(3, 0), net.device(3, 1)])
    for copy in mine:
        copy.wait()

    sends, arrivals = [], []

    def push(ref, own, source, to):
        n = len(sends)
        at, from_at = ref.at[own], ref.at[source]
        sends.append(remote(at, at, ps.at[n], pr.at[n], to))
        arrivals.append(remote(from_at, from_at, ps.at[n], pr.at[n], to))

    for ref in (gains, smalls):
        for d, to in enumerate(line.others):
            push(ref, net.z, lax.rem(net.z + seq - 1 - d, seq), to)
    for n, to in enumerate(plane):
        m, s = (n + 1) // 2, (n + 1) % 2
        push(slots, net.t, net.slot(m, s), to)
    for copy in sends:
        copy.start()
    first = len(sends)

    def hop(way, e):
        n = first + 2 * e + (0 if way > 0 else 1)
        to = (net.base + net.t, net.z + way)
        at = pack_ref if e == 0 else pack_out.at[net.z - way * e]
        lands = pack_out.at[net.z - way * e]
        return remote(at, lands, ps.at[n], pr.at[n], to)

    def forward(way, e):
        place = net.z if way > 0 else seq - 1 - net.z

        @pl.when((place >= e) & (place < seq - 1))
        def _():
            if e > 0:
                landed(way, e - 1)
            hop(way, e).start()

        if e > 0:
            @pl.when((place >= e) & (place == seq - 1))
            def _():
                landed(way, e - 1)

    def landed(way, e):
        n = first + 2 * e + (0 if way > 0 else 1)
        from_at = pack_out.at[net.z - way * (e + 1)]
        remote(from_at, from_at, ps.at[n], pr.at[n], (net.base + net.t, net.z)).wait_recv()

    def last(way):
        place = net.z if way > 0 else seq - 1 - net.z

        @pl.when(place == seq - 1)
        def _():
            landed(way, seq - 2)

        for e in range(seq - 1):
            @pl.when((place >= e) & (place < seq - 1))
            def _():
                hop(way, e).wait_send()

    forward(1, 0)
    forward(-1, 0)
    for copy in arrivals[: seq - 1]:
        copy.wait_recv()
    rows, width = x_ref.shape
    part, chunk = width // seq, 32

    def norm(i, _):
        at = pl.ds(pl.multiple_of(i * chunk, chunk), chunk)
        value = x_ref[at].astype(F32)
        scale = lax.rsqrt(jnp.mean(value * value, axis=-1, keepdims=True) + EPSILON)
        for z in range(seq):
            low = z * part
            full[net.t, at, low : low + part] = (
                value[:, low : low + part] * scale * gains[z, pl.ds(0, 1), :]
            ).astype(BF)
        return 0

    lax.fori_loop(0, rows // chunk, norm, 0)
    gather.begin()
    for copy in arrivals[seq - 1 :]:
        copy.wait_recv()
    saves = [
        pltpu.make_async_copy(a, b, sem.at[n])
        for n, (a, b) in enumerate(((smalls, small_out), (gains, gain_out), (slots, slot_out)))
    ]
    for save in saves:
        save.start()
    for n in range(1, TP):
        gather.before(n)
        if n == 2:
            forward(1, 1)
            forward(-1, 1)
    gather.finish()
    saves.append(pltpu.make_async_copy(full, full_out, sem.at[3]))
    saves[-1].start()
    for e in range(2, seq - 1):
        forward(1, e)
        forward(-1, e)
    last(1)
    last(-1)

    for copy in sends:
        copy.wait_send()
    own_pack.wait()
    for save in saves:
        save.wait()


def opening(seq, x, small, gain, slot, pack):
    rows, width = x.shape
    shape = jax.ShapeDtypeStruct
    dma = pltpu.SemaphoreType.DMA
    pushes = 4 * (seq - 1) + TP - 1
    return pl.pallas_call(
        open_kernel,
        in_specs=[VM] + [ANY] * 4,
        out_specs=[ANY] * 5,
        out_shape=[
            shape((seq,) + small.shape, F32),
            shape((seq,) + gain.shape, F32),
            shape((TP,) + slot.shape, jnp.int32),
            shape((TP, rows, width), BF),
            shape((seq,) + pack.shape, BF),
        ],
        scratch_shapes=[
            pltpu.VMEM((TP, rows, width), BF),
            pltpu.VMEM((seq,) + small.shape, F32),
            pltpu.VMEM((seq,) + gain.shape, F32),
            pltpu.VMEM((TP,) + slot.shape, jnp.int32),
            dma((10,)), dma((10,)), dma((pushes,)), dma((pushes,)), dma((5,)),
        ],
        compiler_params=pltpu.CompilerParams(
            collective_id=6, has_side_effects=True, vmem_limit_bytes=40 << 20
        ),
        cost_estimate=pl.CostEstimate(
            flops=40 * 10**9, bytes_accessed=10 << 20, transcendentals=0
        ),
        name="opening",
    )(x, small, gain, slot, pack)


def close_kernel(layers, gain_ref, channel_ref, *refs):
    rows_in, refs = refs[:layers], refs[layers:]
    count = (len(refs) - 10 - layers) // 2
    blocks, (gain_out, channel_out) = refs[:count], refs[count : count + 2]
    moved, refs = refs[count + 2 : 2 * count + 2], refs[2 * count + 2 :]
    rows_out = refs[:layers]
    plane_gain, line_gain, line_channel, ps, pr, *sems = refs[layers:]
    net = Net()
    seq = line_gain.shape[0]
    line = Line(net, seq)
    plane = [(m, s) for m in range(4) for s in range(2)][1:]
    plane_gain[net.t] = gain_ref[...]
    line_channel[net.z] = channel_ref[...]
    net.enter(line.others + [net.device(1, 1), net.device(2, 1), net.device(3, 0), net.device(3, 1)])
    used = []

    def push(src, dst, landed, to):
        n = len(used)
        used.append(remote(src, dst, ps.at[n], pr.at[n], to))
        used[-1].start()
        return remote(src, landed, ps.at[n], pr.at[n], to)

    gains = [
        push(
            plane_gain.at[net.t], plane_gain.at[net.t], plane_gain.at[net.slot(m, s)],
            net.device(m, s),
        )
        for m, s in plane
    ]
    sources = [lax.rem(net.z + seq - 1 - d, seq) for d in range(seq - 1)]
    rest = [
        push(line_channel.at[net.z], line_channel.at[net.z], line_channel.at[source], to)
        for source, to in zip(sources, line.others)
    ]
    exchange = Exchange(net, seq, blocks, moved, rows_in, rows_out, *sems)
    exchange.begin()
    for copy in gains:
        copy.wait_recv()
    total = plane_gain[0]
    for t in range(1, TP):
        total += plane_gain[t]
    line_gain[net.z] = total
    for source, to in zip(sources, line.others):
        rest.append(push(line_gain.at[net.z], line_gain.at[net.z], line_gain.at[source], to))
    for copy in rest:
        copy.wait_recv()
    total, channel = line_gain[0], line_channel[0]
    for z in range(1, seq):
        total += line_gain[z]
        channel += line_channel[z]
    gain_out[...] = total
    channel_out[...] = channel
    for copy in used:
        copy.wait_send()
    exchange.finish()


def closing(seq, gains, channels, rows, blocks):
    shape = jax.ShapeDtypeStruct
    dma = pltpu.SemaphoreType.DMA
    pushes = TP - 1 + 2 * (seq - 1)
    return pl.pallas_call(
        partial(close_kernel, len(rows)),
        in_specs=[VM, VM] + [ANY] * (len(rows) + len(blocks)),
        out_specs=[VM, VM] + [ANY] * (len(rows) + len(blocks)),
        out_shape=[shape(gains.shape, F32), shape(channels.shape, F32)]
        + [shape(block.shape, block.dtype) for block in blocks + rows],
        scratch_shapes=[
            pltpu.VMEM((TP,) + gains.shape, F32),
            pltpu.VMEM((seq,) + gains.shape, F32),
            pltpu.VMEM((seq,) + channels.shape, F32),
            dma((pushes,)), dma((pushes,)),
        ]
        + exchange_scratch(blocks, rows),
        compiler_params=pltpu.CompilerParams(
            collective_id=7, has_side_effects=True, vmem_limit_bytes=40 << 20
        ),
        cost_estimate=pl.CostEstimate(
            flops=40 * 10**9, bytes_accessed=10 << 20, transcendentals=0
        ),
        name="closing",
    )(gains, channels, *rows, *blocks)


def layer_backward(split, upstream, upstream_low, w, saved, slots, pending):
    residual, kept, middle, kept_two = saved
    pending_mlp, pending_rec = pending
    upstream_low, pending_mlp = lax.optimization_barrier((upstream_low, pending_mlp))
    grad_middle, mid_low, grad_gain_two, g_mlp = mlp_backward(
        upstream_low, upstream, middle, w["gain"][1], w["mlp"], *kept_two
    )
    mlp_share = over_seq(g_mlp)
    mid_low, pending_rec = lax.optimization_barrier((mid_low, pending_rec))
    given = []
    if not isinstance(pending_mlp, tuple):
        (mlp_block, rows), (rec_block, _) = split(pending_mlp), split(pending_rec)
        given = [mlp_block, rec_block, rows]
    grad, grad_low, grad_gain_one, g_rec, channel, *taken = rec_backward(
        mid_low, grad_middle, residual, w["gain"][0], w["rec"], w["small"], slots, kept, given
    )
    g_rec, mlp_share = lax.optimization_barrier((g_rec, mlp_share))
    rec_share = over_seq(g_rec)
    slope = 8.0 * jax.nn.sigmoid(-w["decay"])
    channel = jnp.concatenate([channel[:7], channel[7:] * slope], 0)
    gains = jnp.concatenate([grad_gain_one, grad_gain_two], 0)
    return grad, grad_low, (mlp_share, rec_share), channel, gains, (pending_mlp, pending_rec), taken


def over_seq(value):
    return lax.psum_scatter(value, "seq", scatter_dimension=0, tiled=False)


def columns(parts):
    return jnp.moveaxis(parts, 0, 1).reshape(parts.shape[1], -1)


def unit_columns(parts, seq):
    tp, n, units = parts.shape
    part = units // seq
    places = {}
    for t in range(tp):
        for p in range(seq):
            places[p * tp + t // seq * seq + (t + p) % seq] = (t, p)
    chunks = [places[q] for q in range(tp * seq)]
    return jnp.concatenate([parts[t, :, p * part : (p + 1) * part] for t, p in chunks], 1)


def owned_grads(plan, down_rows, rec_share, mlp, rec, width, head, units):
    base = width // plan.seq
    h, u = head // plan.seq, units // plan.seq
    out = [rec_share[base + i * h : base + (i + 1) * h] for i in range(3)]
    gates = rec_share[base + 3 * h :]
    rest, blocks = mlp_split(width, 2 * units)
    down = [down_rows[u:, i * rest : (i + 1) * rest] for i in range(blocks)]
    grads = [
        columns(rec[:, :, :head]),
        columns(rec[:, :, head:]),
        gates[:, :head],
        gates[:, head:],
        jnp.concatenate(out, 1),
        unit_columns(mlp[:, :, :units], plan.seq),
        unit_columns(mlp[:, :, units:], plan.seq),
        jnp.concatenate([down_rows[:u], jnp.concatenate(down, 0)], 1),
    ]
    return [to_owners(plan, g.astype(F32), 0) for g in grads]


def local(plan, *args):
    (
        block_input, cotangent, lengths, offsets, norm_gains, branch_proj, stream_proj, conv_kernel,
        conv_bias, rate_proj, admit_proj, gate_bias, decay_logit, out_proj, mlp_gate, mlp_up,
        mlp_down,
    ) = args
    tp, dp, seq = plan.tp, plan.dp, plan.seq
    t = lax.axis_index("rep") % tp
    z = lax.axis_index("seq")
    rows = block_input.shape[0]
    head = branch_proj.shape[2] // tp
    units = mlp_gate.shape[2] // tp

    channels = conv_kernel.shape[2]
    small = jnp.concatenate([conv_kernel, conv_bias[:, None], gate_bias, decay_logit[:, None]], 1)
    small = small.reshape(LAYERS * 8, channels).astype(F32)
    slot = jnp.pad(jnp.stack([lengths, offsets], 1), ((0, 7), (0, 126)))
    def col(weight, layer, width, t):
        size = (1, weight.shape[1], width)
        return lax.dynamic_slice(weight, (layer, 0, t * width), size)[0]

    def chunk(weight, layer, t):
        size = weight.shape[1] // tp
        return lax.dynamic_slice(weight, (layer, t * size, 0), (1, size, weight.shape[2]))[0]

    def below(rows, twice):
        rest, blocks = mlp_split(rows.shape[1], twice)
        low = rows.shape[0] // blocks
        side = [rows[i * low : (i + 1) * low, twice:] for i in range(blocks)]
        return jnp.concatenate([rows[:, :twice], jnp.concatenate(side, 1)], 0)

    def rec_rows(l, t):
        out = chunk(out_proj, l, t)
        gates = jnp.concatenate([chunk(rate_proj, l, t), chunk(admit_proj, l, t)], 1)
        out = [out[:, i * 2 * head : (i + 1) * 2 * head] for i in range(3)] + [gates]
        return jnp.concatenate(out, 0)

    def rec_pack(l, rows_of, t):
        rec = jnp.concatenate([col(branch_proj, l, head, t), col(stream_proj, l, head, t)], 1)
        return jnp.concatenate([rec, rows_of], 0)

    def unit_chunk(t, plane):
        return t // seq * seq + (t + plane) % seq

    def mlp_rows(l, t):
        return below(chunk(mlp_down, l, unit_chunk(t, z)), 2 * units)

    def mlp_pack(l, t):
        rows_of, part = mlp_gate.shape[1], units // seq
        cols = [
            lax.dynamic_slice(
                weight, (l, 0, (p * tp + unit_chunk(t, p)) * part), (1, rows_of, part)
            )[0]
            for weight in (mlp_gate, mlp_up)
            for p in range(seq)
        ]
        return jnp.concatenate([jnp.concatenate(cols, 1), mlp_rows(l, t)], 0)

    pack = rec_pack(0, owner_chunks(plan, rec_rows(0, t)), t)
    mlp = mlp_pack(0, t)
    smalls, gains, layout, normed, rec = opening(
        seq, block_input, small, norm_gains.reshape(2 * LAYERS, -1).astype(F32), slot, pack
    )
    t, mlp, rec = lax.optimization_barrier((t, mlp, rec))
    layout = layout[:, 0, :2]
    gains = jnp.moveaxis(gains, 0, 1).reshape(LAYERS, 2, -1)
    smalls = jnp.moveaxis(smalls, 0, 1).reshape(LAYERS, 8, -1)
    smalls = lax.dynamic_slice_in_dim(smalls, t * head, head, 2)


    residual = block_input.astype(F32)
    saved_all, weights = [], []
    for l in range(LAYERS):
        if l > 0:
            mlp, normed = lax.optimization_barrier((mlp, normed))
        w = dict(
            gain=gains[l],
            small=jnp.concatenate([smalls[l, :7], -8.0 * jax.nn.softplus(-smalls[l, 7:])], 0),
            decay=smalls[l, 7:],
            rec=rec,
            mlp=lax.all_gather(mlp, "seq"),
        )
        weights.append(w)
        kept = rec_forward(normed, residual, w["gain"][1], w["rec"], w["small"], layout)
        middle, normed_two, *kept = kept
        if l + 1 < LAYERS:
            t, normed_two = lax.optimization_barrier((t, normed_two))
            pack = rec_pack(l + 1, owner_chunks(plan, rec_rows(l + 1, t)), t)
            mlp, pack, normed_two = lax.optimization_barrier((mlp_pack(l + 1, t), pack, normed_two))
            rec = lax.all_gather(pack, "seq")
        output, normed, *kept_two = mlp_forward(
            normed_two, middle, gains[(l + 1) % LAYERS, 0], w["mlp"]
        )
        saved_all.append((residual, kept, middle, kept_two))
        residual = output
    positions = z * rows + jnp.arange(rows, dtype=jnp.int32)
    inside = (positions >= offsets[0]) & (positions < offsets[0] + lengths[0])
    gradient = cotangent.astype(F32) * inside.astype(F32)[:, None]

    gradient_low = gradient.astype(BF)
    width = block_input.shape[1]
    base = width // seq

    def split(share):
        return share[:base].reshape(tp, -1, share.shape[1]), share[base:]

    shares, mlps, recs, downs = ([None] * LAYERS for _ in range(4))
    channel_all, gain_all = [None] * LAYERS, [None] * LAYERS
    for l in reversed(range(LAYERS)):
        gradient, gradient_low, shares[l], channel_all[l], gain_all[l], pending, taken = layer_backward(
            split, gradient, gradient_low, weights[l], saved_all[l], layout,
            ((), ()) if l + 1 == LAYERS else shares[l + 1],
        )
        if l + 1 < LAYERS:
            shares[l + 1], mlps[l + 1], recs[l + 1], downs[l + 1] = pending, *taken
    mlp_block, rows = split(shares[0][0])
    gains, channel, mlps[0], downs[0] = closing(
        seq, jnp.concatenate(gain_all, 0), jnp.concatenate(channel_all, 0), [rows], [mlp_block]
    )
    recs[0] = lax.all_to_all(
        split(shares[0][1])[0], "rep", split_axis=0, concat_axis=0,
        axis_index_groups=plan.tp_groups,
    )
    outs = [
        owned_grads(plan, downs[l], shares[l][1], mlps[l], recs[l], width, head, units)
        for l in range(LAYERS)
    ]
    big = [jnp.stack([outs[l][i] for l in range(LAYERS)]) for i in range(8)]

    channel = lax.dynamic_slice_in_dim(channel, z * (head // seq), head // seq, 1)
    channel = to_owners(plan, channel, 1).reshape(LAYERS, 8, -1)
    if dp > 1:
        gains = lax.psum(gains, "rep", axis_index_groups=plan.dp_groups)
    own = gains.shape[1] // (plan.rep * seq)
    owner = lax.axis_index(("rep", "seq"))
    gains = lax.dynamic_slice_in_dim(gains, owner * own, own, 1).reshape(LAYERS, 2, own)
    return (
        residual.astype(BF),
        gradient,
        gains,
        big[0],
        big[1],
        channel[:, :CONV],
        channel[:, CONV],
        big[2],
        big[3],
        channel[:, CONV + 1 : CONV + 3],
        channel[:, CONV + 3],
        big[4],
        big[5],
        big[6],
        big[7],
    )


def solution(mesh):
    tokens = P(("rep", "seq"), None)
    rows = P(None, "seq", None)
    last3 = P(None, None, "seq")
    last2 = P(None, "seq")
    own_rows = P(None, ("rep", "seq"), None)
    own3 = P(None, None, ("rep", "seq"))
    own2 = P(None, ("rep", "seq"))

    def whole(*args):
        heads = args[9].shape[1] // args[9].shape[2]
        plan = Plan(mesh, heads)
        return jax.shard_map(
            partial(local, plan),
            mesh=mesh,
            in_specs=(
                tokens, tokens, P("rep"), P("rep"), last3, rows, rows, last3, last2, rows, rows,
                last3, last2, rows, rows, rows, rows,
            ),
            out_specs=(
                tokens, tokens, own3, own_rows, own_rows, own3, own2, own_rows, own_rows, own3,
                own2, own_rows, own_rows, own_rows, own_rows,
            ),
            check_vma=False,
        )(*args)

    return whole
```

```python
from functools import partial

import jax
import jax.numpy as jnp
from jax import lax
from jax.experimental import pallas as pl
from jax.experimental.pallas import tpu as pltpu
from jax.sharding import PartitionSpec as P

CONV = 4
LAYERS = 2
EPSILON = 1e-06
BF = jnp.bfloat16
F32 = jnp.float32


def dot(a, b):
    return jnp.dot(a, b, preferred_element_type=F32)


def dot_tn(a, b):
    return lax.dot_general(a, b, (((0,), (0,)), ((), ())), preferred_element_type=F32)


def dot_nt(a, b):
    return lax.dot_general(a, b, (((1,), (1,)), ((), ())), preferred_element_type=F32)


def glu_product(gate_in, value_in):
    return jax.nn.gelu(gate_in, approximate=True) * value_in


class Plan:
    def __init__(self, mesh, heads):
        self.rep = mesh.shape["rep"]
        self.seq = mesh.shape["seq"]
        self.tp = min(heads, self.rep)
        self.dp = self.rep // self.tp
        tp, dp = self.tp, self.dp
        self.tp_groups = None if dp == 1 else [[d * tp + t for t in range(tp)] for d in range(dp)]
        self.dp_groups = [[d * tp + t for d in range(dp)] for t in range(tp)]


def owner_chunks(plan, value):
    tp, seq = plan.tp, plan.seq
    pairs = []
    for d in range(plan.dp):
        for j in range(tp):
            for z in range(seq):
                o = tp * z + j
                pairs.append(((d * tp + j) * seq + z, (d * tp + o // seq) * seq + o % seq))
    return lax.ppermute(value, ("rep", "seq"), pairs)


def to_owners(plan, chunk, axis):
    if plan.dp == 1:
        return chunk
    part = lax.psum_scatter(
        chunk, "rep", scatter_dimension=axis, tiled=True, axis_index_groups=plan.dp_groups
    )
    tp, seq, dp = plan.tp, plan.seq, plan.dp
    pairs = [
        ((d * tp + t) * seq + z, (t * seq + z) * dp + d)
        for d in range(dp)
        for t in range(tp)
        for z in range(seq)
    ]
    return lax.ppermute(part, ("rep", "seq"), pairs)


MESH = pl.DeviceIdType.MESH
ANY = pl.BlockSpec(memory_space=pl.ANY)
VM = pl.BlockSpec(memory_space=pltpu.VMEM)
TP = 8
LATER = 3


class Net:
    def __init__(self):
        rep = lax.axis_index("rep")
        self.z = lax.axis_index("seq")
        self.t = lax.rem(rep, TP)
        self.base = rep - self.t
        chip = self.t // 2
        self.k = lax.rem(self.t, 2)
        self.b0 = lax.rem(chip, 2)
        self.b1 = chip // 2

    def slot(self, m, s):
        b0 = lax.rem(self.b0 + m % 2, 2)
        b1 = lax.rem(self.b1 + m // 2, 2)
        return (b1 * 2 + b0) * 2 + lax.rem(self.k + s, 2)

    def device(self, m, s):
        return (self.base + self.slot(m, s), self.z)

    def enter(self, extra=()):
        barrier = pltpu.get_barrier_semaphore()
        devices = [self.device(1, 0), self.device(2, 0), self.device(0, 1)] + list(extra)
        for device in devices:
            pl.semaphore_signal(barrier, inc=1, device_id=device, device_id_type=MESH)
        pl.semaphore_wait(barrier, len(devices))


def remote(src, dst, send, recv, device):
    return pltpu.make_async_remote_copy(
        src_ref=src, dst_ref=dst, send_sem=send, recv_sem=recv, device_id=device,
        device_id_type=MESH,
    )


class Gather:
    def __init__(self, net, full, send, recv):
        self.net, self.full, self.send, self.recv = net, full, send, recv
        half = full.shape[1] // 2
        a, b, whole = pl.ds(0, half), pl.ds(half, half), pl.ds(0, 2 * half)
        x, y, sib = net.device(1, 0), net.device(2, 0), net.device(0, 1)
        self.plan = [
            (0, a, x, 1), (0, b, y, 2), (0, b, x, 1), (0, a, y, 2), (2, b, x, 3), (1, a, y, 3),
            (0, whole, sib, 0), (1, whole, sib, 1), (2, whole, sib, 2), (3, whole, sib, 3),
        ]

    def copy(self, i):
        m, rows, to, _ = self.plan[i]
        at = self.full.at[self.net.slot(m, 0), rows]
        return remote(at, at, self.send.at[i], self.recv.at[i], to)

    def arrived(self, i):
        _, rows, to, m = self.plan[i]
        at = self.full.at[self.net.slot(m, 0 if i < 6 else 1), rows]
        remote(at, at, self.send.at[i], self.recv.at[i], to).wait_recv()

    def begin(self):
        for i in (0, 1, 2, 3, 6):
            self.copy(i).start()

    def before(self, n):
        if n == 1:
            self.arrived(6)
        if n == 2:
            self.arrived(0)
            self.copy(5).start()
            self.arrived(1)
            self.copy(4).start()
            self.arrived(2)
            self.copy(7).start()
        if n == 3:
            self.arrived(7)
        if n == 4:
            self.arrived(3)
            self.copy(8).start()
        if n == 5:
            self.arrived(8)
        if n == 6:
            self.arrived(4)
            self.arrived(5)
            self.copy(9).start()
        if n == 7:
            self.arrived(9)

    def finish(self):
        for i in range(10):
            self.copy(i).wait_send()


class Scatter:
    def __init__(self, net, part, near, wide, far, send, recv):
        self.net, self.part, self.near = net, part, near
        self.wide, self.far, self.send, self.recv = wide, far, send, recv
        self.rows = part.shape[2]
        half = self.rows // 2
        a, b, whole = pl.ds(0, half), pl.ds(half, half), pl.ds(0, 2 * half)
        self.a, self.b = a, b
        x, y, sib = net.device(1, 0), net.device(2, 0), net.device(0, 1)
        self.plan = [
            (part.at[1, m], near.at[m], sib) for m in range(4)
        ] + [
            (part.at[0, 3, a], wide.at[0], x),
            (part.at[0, 3, b], wide.at[1], y),
            (part.at[0, 1, a], far.at[0, a], x),
            (part.at[0, 2, b], far.at[1, b], y),
            (part.at[0, 1, b], far.at[0, b], x),
            (part.at[0, 2, a], far.at[1, a], y),
        ]

    def copy(self, i):
        src, dst, to = self.plan[i]
        return remote(src, dst, self.send.at[i], self.recv.at[i], to)

    def add(self, m, start, count, other):
        def some(i, carry):
            at = pl.ds(pl.multiple_of(start + i * 64, 64), 64)
            from_at = pl.ds(pl.multiple_of(i * 64, 64), 64)
            total = self.part[0, m, at].astype(F32) + other[from_at].astype(F32)
            self.part[0, m, at] = total.astype(BF)
            return carry

        lax.fori_loop(0, count // 64, some, 0)

    def after(self, n):
        if n == 1:
            self.copy(0).start()
        if n == 3:
            self.copy(1).start()
        if n == 4:
            self.copy(1).wait_recv()
            self.add(1, 0, self.rows, self.near.at[1])
            self.copy(6).start()
        if n == 5:
            self.copy(2).start()
        if n == 6:
            self.copy(2).wait_recv()
            self.add(2, 0, self.rows, self.near.at[2])
            self.copy(7).start()
        if n == 7:
            self.copy(3).start()

    def corner(self):
        self.copy(3).wait_recv()
        self.add(3, 0, self.rows, self.near.at[3])
        self.copy(4).start()
        self.copy(5).start()

    def edges(self):
        half = self.rows // 2
        self.copy(4).wait_recv()
        self.add(2, 0, half, self.wide.at[0])
        self.copy(9).start()
        self.copy(5).wait_recv()
        self.add(1, half, half, self.wide.at[1])
        self.copy(8).start()
        self.copy(0).wait_recv()

    def finish(self):
        for i in (6, 7, 8, 9):
            self.copy(i).wait_recv()
        for i in range(10):
            self.copy(i).wait_send()

    def total(self, at):
        own = self.part[0, 0, at].astype(F32) + self.near[0, at].astype(F32)
        return own + self.far[0, at].astype(F32) + self.far[1, at].astype(F32)


class Exchange:
    def __init__(self, net, seq, blocks, moved, rows_in, rows_out, send, recv, own):
        self.net = net
        self.blocks, self.moved, self.rows_in, self.rows_out = blocks, moved, rows_in, rows_out
        self.send, self.recv, self.own = send, recv, own
        self.others = [(m, s) for m in range(4) for s in range(2)][1:]
        each = TP // seq
        self.owner = lax.rem(net.z + TP - net.t, seq) * each + net.t // seq
        self.giver = lax.rem(net.t, each) * seq + lax.rem(net.z + TP - net.t // each, seq)

    def pushes(self, arriving=False):
        copies = []
        for block, out in zip(self.blocks, self.moved):
            for m, s in self.others:
                n, slot = len(copies), self.net.slot(m, s)
                copies.append(
                    remote(
                        block.at[slot], out.at[slot if arriving else self.net.t],
                        self.send.at[n], self.recv.at[n], self.net.device(m, s),
                    )
                )
        return copies

    def rows(self):
        first = len(self.blocks) * len(self.others)
        to = (self.net.base + self.owner, self.net.z)
        return [
            remote(src, dst, self.send.at[first + n], self.recv.at[first + n], to)
            for n, (src, dst) in enumerate(zip(self.rows_in, self.rows_out))
        ]

    def kept(self):
        copies = []
        for block, out in zip(self.blocks, self.moved):
            at = self.own.at[len(copies)]
            copies.append(pltpu.make_async_copy(block.at[self.net.t], out.at[self.net.t], at))
        return copies

    def rows_kept(self):
        first = len(self.blocks)
        return [
            pltpu.make_async_copy(src, dst, self.own.at[first + n])
            for n, (src, dst) in enumerate(zip(self.rows_in, self.rows_out))
        ]

    def begin(self):
        for copy in self.kept() + self.pushes():
            copy.start()

        @pl.when(self.owner != self.net.t)
        def _():
            for copy in self.rows():
                copy.start()

        @pl.when(self.owner == self.net.t)
        def _():
            for copy in self.rows_kept():
                copy.start()

    def finish(self):
        for copy in self.pushes(arriving=True):
            copy.wait_recv()
        for copy in self.pushes():
            copy.wait_send()
        for copy in self.kept():
            copy.wait()

        @pl.when(self.owner != self.net.t)
        def _():
            for copy in self.rows():
                copy.wait_send()

        @pl.when(self.owner == self.net.t)
        def _():
            for copy in self.rows_kept():
                copy.wait()

        @pl.when(self.giver != self.net.t)
        def _():
            for copy in self.rows():
                copy.wait_recv()


def exchange_scratch(blocks, rows):
    dma, count = pltpu.SemaphoreType.DMA, (TP - 1) * len(blocks) + len(rows)
    return [dma((count,)), dma((count,)), dma((len(blocks) + len(rows),))]


def plane_scratch(rows, width):
    dma = pltpu.SemaphoreType.DMA
    return [
        pltpu.VMEM((TP, rows, width), BF),
        pltpu.VMEM((2, 4, rows, width), BF),
        pltpu.VMEM((4, rows, width), BF),
        pltpu.VMEM((2, rows // 2, width), BF),
        pltpu.VMEM((2, rows, width), BF),
        dma((10,)), dma((10,)), dma((10,)), dma((10,)),
    ]


def steps(gather, scatter, compute):
    def one(i, carry):
        for n in range(1, 2 * 4):
            @pl.when(i == n)
            def _():
                if gather is not None:
                    gather.before(n)

        compute(i // 2, lax.rem(i, 2))
        for n in range(2 * 4):
            @pl.when(i == n)
            def _():
                if scatter is not None:
                    scatter.after(n)

        return carry

    lax.fori_loop(0, 2 * 4, one, 0)


def end_forward(scatter, residual, gain, out, normed):
    rows, chunk = out.shape[0], 32

    def some(i, carry):
        at = pl.ds(pl.multiple_of(i * chunk, chunk), chunk)
        value = residual[at] + scatter.total(at)
        out[at] = value
        scale = lax.rsqrt(jnp.mean(value * value, axis=-1, keepdims=True) + EPSILON)
        normed[at] = (value * scale * gain[...]).astype(BF)
        return carry

    lax.fori_loop(0, rows // chunk, some, 0)


def end_backward(scatter, upstream, values, gain, grad, grad_low, grad_gain):
    rows, chunk = grad.shape[0], 32
    grad_gain[...] = jnp.zeros_like(grad_gain)

    def some(i, carry):
        at = pl.ds(pl.multiple_of(i * chunk, chunk), chunk)
        value, given = values[at], scatter.total(at)
        scale = lax.rsqrt(jnp.mean(value * value, axis=-1, keepdims=True) + EPSILON)
        scaled = given * gain[...]
        mean = jnp.mean(value * scaled, axis=-1, keepdims=True)
        result = upstream[at] + scale * scaled - value * (scale * scale * scale * mean)
        grad[at] = result
        grad_low[at] = result.astype(BF)
        grad_gain[...] += jnp.sum(given * value * scale, axis=0, keepdims=True)
        return carry

    lax.fori_loop(0, rows // chunk, some, 0)


GELU_A = 0.7978845608028654
GELU_B = 0.044715


def gelu_parts(v):
    square = v * v
    tanh = jnp.tanh(GELU_A * (v + GELU_B * v * square))
    half = 0.5 * (1.0 + tanh)
    slope = half + 0.5 * v * (1.0 - tanh * tanh) * (GELU_A * (1.0 + 3.0 * GELU_B * square))
    return v * half, slope


def copy_list(pairs, sem, first):
    return [
        pltpu.make_async_copy(src, dst, sem.at[first + n]) for n, (src, dst) in enumerate(pairs)
    ]


def unpack_rec(pack, col, wout, gates, sem, first):
    seq, both = pack.shape[0], pack.shape[2]
    rows, part = col.shape[0] // seq, gates.shape[0] // seq
    pairs = []
    for z in range(seq):
        pairs.append((pack.at[z, pl.ds(0, rows)], col.at[pl.ds(z * rows, rows)]))
        own = pl.ds(z * part, part)
        for j in range(3):
            pairs.append(
                (pack.at[z, pl.ds(rows + j * part, part)], wout.at[own, pl.ds(j * both, both)])
            )
        pairs.append((pack.at[z, pl.ds(rows + 3 * part, part)], gates.at[own]))
    return copy_list(pairs, sem, first)


def mlp_split(width, twice):
    rest = width - twice
    return rest, twice // rest


def unpack_mlp(pack, col, down, sem, first):
    seq, twice = pack.shape[0], pack.shape[2]
    rows, part = col.shape[0] // seq, down.shape[0] // seq
    rest, blocks = mlp_split(down.shape[1], twice)
    low = part // blocks
    pairs = []
    for z in range(seq):
        pairs.append((pack.at[z, pl.ds(0, rows)], col.at[pl.ds(z * rows, rows)]))
        pairs.append(
            (pack.at[z, pl.ds(rows, part)], down.at[pl.ds(z * part, part), pl.ds(0, twice)])
        )
        for n in range(blocks):
            pairs.append(
                (
                    pack.at[z, pl.ds(rows + part, low), pl.ds(n * rest, rest)],
                    down.at[pl.ds(z * part + n * low, low), pl.ds(twice, rest)],
                )
            )
    return copy_list(pairs, sem, first)


def mlp_forward_kernel(
    x_ref, residual_ref, gain_ref, pack_ref,
    out_ref, normed_ref, full_out, up_out,
    full, part, near, wide, far, gs, gr, ss, sr, col, wd, ups, sem,
):
    net = Net()
    gather = Gather(net, full, gs, gr)
    scatter = Scatter(net, part, near, wide, far, ss, sr)
    n = 5 * pack_ref.shape[0]
    own = pltpu.make_async_copy(x_ref, full.at[net.t], sem.at[n])
    own.start()
    weights = unpack_mlp(pack_ref, col, wd, sem, 0)
    for copy in weights:
        copy.start()
    net.enter()
    own.wait()
    gather.begin()
    for copy in weights:
        copy.wait()

    units = wd.shape[0]

    def compute(m, s):
        slot = net.slot(m, s)
        x = full[slot]
        up = dot(x, col[...])
        ups[slot] = up.astype(BF)
        hidden = glu_product(up[:, :units], up[:, units:]).astype(BF)
        part[s, m] = dot(hidden, wd[...]).astype(BF)

    steps(gather, scatter, compute)
    saves = [
        pltpu.make_async_copy(full, full_out, sem.at[n + 1]),
        pltpu.make_async_copy(ups, up_out, sem.at[n + 2]),
    ]
    for copy in saves:
        copy.start()
    scatter.corner()
    scatter.edges()
    scatter.finish()
    end_forward(scatter, residual_ref, gain_ref, out_ref, normed_ref)
    gather.finish()
    for copy in saves:
        copy.wait()


def mlp_forward(x, residual, gain, pack):
    rows, width = x.shape
    seq, _, twice = pack.shape
    shape = jax.ShapeDtypeStruct
    return pl.pallas_call(
        mlp_forward_kernel,
        in_specs=[ANY, VM, VM, ANY],
        out_specs=[VM, VM, ANY, ANY],
        out_shape=[
            shape((rows, width), F32),
            shape((rows, width), BF),
            shape((TP, rows, width), BF),
            shape((TP, rows, twice), BF),
        ],
        scratch_shapes=plane_scratch(rows, width)
        + [
            pltpu.VMEM((width, twice), BF),
            pltpu.VMEM((twice // 2, width), BF),
            pltpu.VMEM((TP, rows, twice), BF),
            pltpu.SemaphoreType.DMA((5 * seq + 4,)),
        ],
        compiler_params=pltpu.CompilerParams(
            collective_id=1, has_side_effects=True, vmem_limit_bytes=58 << 20
        ),
        cost_estimate=pl.CostEstimate(
            flops=60 * 10**9, bytes_accessed=30 << 20, transcendentals=0
        ),
        name="mlp_forward",
    )(x, residual, gain.reshape(1, -1), pack)


def mlp_backward_kernel(
    g_ref, upstream_ref, values_ref, gain_ref, pack_ref, x_ref, up_ref,
    grad_ref, low_ref, gain_out, gcol_ref,
    full, part, near, wide, far, gs, gr, ss, sr, col, wd, xs, ups, hid, sem,
):
    net = Net()
    gather = Gather(net, full, gs, gr)
    scatter = Scatter(net, part, near, wide, far, ss, sr)
    seq = pack_ref.shape[0]
    n = 5 * seq
    own = pltpu.make_async_copy(g_ref, full.at[net.t], sem.at[n])
    own.start()
    loads = unpack_mlp(pack_ref, col, wd, sem, 0) + [
        pltpu.make_async_copy(up_ref, ups, sem.at[n + 1]),
    ]
    late = pltpu.make_async_copy(x_ref, xs, sem.at[n + 3])
    for copy in loads + [late]:
        copy.start()
    net.enter()
    own.wait()
    gather.begin()
    for copy in loads:
        copy.wait()
    rows, units = full.shape[1], wd.shape[0]

    def compute(m, s):
        slot = net.slot(m, s)
        at = pl.ds(pl.multiple_of(slot * rows, rows), rows)
        grad_hidden = dot_nt(full[slot], wd[...])
        up = ups[at].astype(F32)
        act, slope = gelu_parts(up[:, :units])
        up_value = up[:, units:]
        hid[at] = (act * up_value).astype(BF)
        grads = jnp.concatenate([grad_hidden * up_value * slope, grad_hidden * act], 1).astype(BF)
        ups[at] = grads
        part[s, m] = dot_nt(grads, col[...]).astype(BF)

    steps(gather, scatter, compute)
    late.wait()
    scatter.corner()
    width = full.shape[2]
    own_rows = width // (TP * seq)
    tile = 2 * seq * own_rows
    base = width // seq

    def columns(j, carry):
        x = xs[:, pl.ds(pl.multiple_of(j * tile, 128), tile)]
        product = dot_tn(x, ups[...]).astype(BF)
        for r in range(2):
            for z in range(seq):
                low = (r * seq + z) * own_rows
                at = pl.ds(pl.multiple_of((2 * j + r) * own_rows, own_rows), own_rows)
                gcol_ref[z, at] = product[low : low + own_rows]
        return carry

    lax.fori_loop(0, TP // 2, columns, 0)
    scatter.edges()

    tokens = full.shape[0] * rows
    part_units = units // seq
    rest, blocks = mlp_split(width, 2 * units)
    low = part_units // blocks
    hidden = hid[...]
    for first in range(0, width, width // 2):
        at = pl.ds(first, width // 2)
        product = dot_tn(hidden, full[:, :, at].reshape(tokens, width // 2)).astype(BF)
        beside = min(2 * units - first, width // 2)
        for z in range(seq):
            own = product[z * part_units : (z + 1) * part_units]
            to = lax.rem(net.t + z, seq)
            gcol_ref[to, base : base + part_units, first : first + beside] = own[:, :beside]
            if beside < width // 2:
                for n in range(blocks):
                    gcol_ref[to, base + part_units :, n * rest : (n + 1) * rest] = own[
                        n * low : (n + 1) * low, beside:
                    ]
    scatter.finish()
    end_backward(scatter, upstream_ref, values_ref, gain_ref, grad_ref, low_ref, gain_out)
    gather.finish()


def mlp_backward(g, upstream, values, gain, pack, x, up):
    rows, width = g.shape
    seq, _, twice = pack.shape
    tokens = TP * rows
    shape = jax.ShapeDtypeStruct
    return pl.pallas_call(
        mlp_backward_kernel,
        in_specs=[ANY, VM, VM, VM, ANY, ANY, ANY],
        out_specs=[VM, VM, VM, VM],
        out_shape=[
            shape((rows, width), F32),
            shape((rows, width), BF),
            shape((1, width), F32),
            shape(pack.shape, BF),
        ],
        scratch_shapes=plane_scratch(rows, width)
        + [
            pltpu.VMEM((width, twice), BF),
            pltpu.VMEM((twice // 2, width), BF),
            pltpu.VMEM((tokens, width), BF),
            pltpu.VMEM((tokens, twice), BF),
            pltpu.VMEM((tokens, twice // 2), BF),
            pltpu.SemaphoreType.DMA((5 * seq + 4,)),
        ],
        compiler_params=pltpu.CompilerParams(
            collective_id=2, has_side_effects=True, vmem_limit_bytes=60 << 20
        ),
        cost_estimate=pl.CostEstimate(
            flops=70 * 10**9, bytes_accessed=30 << 20, transcendentals=0
        ),
        name="mlp_backward",
    )(
        g, upstream, values, gain.reshape(1, -1), pack, x.reshape(tokens, width),
        up.reshape(tokens, twice),
    )


def after_corner_first(scatter, n):
    if n % 2 == 0:
        scatter.copy(3 - n // 2).start()
    if n == 3:
        scatter.corner()
    if n == 5:
        scatter.copy(2).wait_recv()
        scatter.add(2, 0, scatter.rows, scatter.near.at[2])
        scatter.copy(7).start()
    if n == 7:
        scatter.copy(1).wait_recv()
        scatter.add(1, 0, scatter.rows, scatter.near.at[1])
        scatter.copy(6).start()


class Line:
    def __init__(self, net, count):
        self.net, self.count = net, count
        self.others = [(net.base + net.t, lax.rem(net.z + d, count)) for d in range(1, count)]
        self.next = (net.base + net.t, net.z + 1)
        self.before = (net.base + net.t, net.z - 1)

    def to_all(self, ends, send, recv):
        at = ends.at[self.net.z]
        copies = [
            remote(at, at, send.at[d], recv.at[d], to) for d, to in enumerate(self.others)
        ]
        for copy in copies:
            copy.start()
        for d, copy in enumerate(copies):
            source = lax.rem(self.net.z + self.count - 1 - d, self.count)
            from_at = ends.at[source]
            remote(from_at, from_at, send.at[d], recv.at[d], self.others[d]).wait_recv()
        for copy in copies:
            copy.wait_send()


def inside_of(positions, offset, length):
    return jnp.where((positions >= offset) & (positions < offset + length), 1.0, 0.0)


def read_halves(ref, at):
    return jnp.concatenate([ref[n, at] for n in range(ref.shape[0])], 1)


def write_halves(ref, at, value):
    for n in range(ref.shape[0]):
        ref[n, at] = value[:, n * 128 : (n + 1) * 128]


def one_minus_exp(v):
    series = 1.0 + v * (1.0 / 7.0)
    for n in (6.0, 5.0, 4.0, 3.0, 2.0):
        series = 1.0 + v * (1.0 / n) * series
    return jnp.where(v > -0.35, -v * series, 1.0 - jnp.exp(v))


def sigmoid(v):
    return 1.0 / (1.0 + jnp.exp(-v))


def rec_forward_kernel(
    gathered,
    x_ref, residual_ref, gain_ref, pack_ref, small_ref, slots_ref,
    out_ref, normed_ref, full_out, branch_out, stream_out, conv_out, state_out,
    full, part, near, wide, far, gs, gr, ss, sr,
    col, gates, wout, branch, stream, conv, state, retain, inflow, ends, carry, hs, hr, es, er, sem,
):
    net = Net()
    seq = ends.shape[0]
    line = Line(net, seq)
    gather = Gather(net, full, gs, gr)
    scatter = Scatter(net, part, near, wide, far, ss, sr)
    rows = full.shape[1]
    head = gates.shape[0]
    own = pltpu.make_async_copy(x_ref, full if gathered else full.at[net.t], sem.at[0])
    loads = unpack_rec(pack_ref, col, wout, gates, sem, 9)
    for load in [own] + loads:
        load.start()
    net.enter(line.others)
    own.wait()
    if not gathered:
        gather.begin()

    @pl.when(net.z == 0)
    def _():
        stream[:, pl.ds(0, 8), :] = jnp.zeros((TP, 8, head), F32)

    for load in loads:
        load.wait()

    def halo(i):
        slot = net.slot(i // 2, lax.rem(i, 2))
        return remote(
            stream.at[slot, pl.ds(rows, 8)], stream.at[slot, pl.ds(0, 8)],
            hs.at[i], hr.at[i], line.next,
        )

    def project(i):
        slot = net.slot(i // 2, lax.rem(i, 2))
        both = dot(full[slot], col[...])
        branch[slot] = both[:, :head]
        stream[slot, pl.ds(8, rows)] = both[:, head:]

        @pl.when(net.z < seq - 1)
        def _():
            halo(i).start()

    def gate(i):
        slot = net.slot(i // 2, lax.rem(i, 2))

        @pl.when(net.z > 0)
        def _():
            halo(i).wait_recv()

        length, offset = slots_ref[slot, 0], slots_ref[slot, 1]
        positions = net.z * rows + lax.broadcasted_iota(jnp.int32, (rows, head), 0)
        inside = inside_of(positions, offset, length)
        mixed = small_ref[pl.ds(CONV, 1), :] + small_ref[pl.ds(0, 1), :] * stream[slot, pl.ds(8, rows)]
        restart = positions == 0
        for j in range(1, CONV):
            same = jnp.where(inside == inside_of(positions - j, offset, length), 1.0, 0.0)
            if j == 1:
                restart = restart | (same == 0.0)
            mixed += small_ref[pl.ds(j, 1), :] * stream[slot, pl.ds(8 - j, rows)] * same
        low = mixed.astype(BF)
        conv[slot] = low
        pre = dot(low, gates[...])
        rate = sigmoid(pre[:, :head] + small_ref[pl.ds(CONV + 1, 1), :])
        admit = sigmoid(pre[:, head:] + small_ref[pl.ds(CONV + 2, 1), :])
        log_retain = rate * small_ref[pl.ds(CONV + 3, 1), :]
        at = pl.ds(pl.multiple_of(slot * rows, rows), rows)
        write_halves(retain, at, jnp.where(restart, 0.0, jnp.exp(log_retain)))
        scale = jnp.where(restart, 1.0, jnp.sqrt(one_minus_exp(2.0 * log_retain)))
        write_halves(inflow, at, scale * admit * low.astype(F32))

    def one(i, _):
        for n in range(1, TP):
            @pl.when(i == n)
            def _():
                if not gathered:
                    gather.before(n)

        @pl.when(i < TP)
        def _():
            project(i)

        @pl.when(i >= LATER)
        def _():
            gate(i - LATER)

        return 0

    lax.fori_loop(0, TP + LATER, one, 0)
    saves = [
        pltpu.make_async_copy(branch, branch_out, sem.at[5]),
        pltpu.make_async_copy(stream, stream_out, sem.at[6]),
        pltpu.make_async_copy(conv, conv_out, sem.at[7]),
    ]
    if not gathered:
        saves.append(pltpu.make_async_copy(full, full_out, sem.at[4]))
    for save in saves:
        save.start()

    lanes = [pl.ds(i, 128) for i in range(0, head, 128)]

    def step(p, carried):
        at = pl.ds(p, TP, stride=rows)
        result = []
        for n, (value, decay) in enumerate(carried):
            a = retain[n, at]
            value = a * value + inflow[n, at]
            decay = a * decay
            inflow[n, at] = value
            retain[n, at] = decay
            result.append((value, decay))
        return tuple(result)

    start = tuple((jnp.zeros((TP, 128), F32), jnp.ones((TP, 128), F32)) for _ in lanes)
    last = lax.fori_loop(0, rows, step, start, unroll=8)
    for lane, (value, decay) in zip(lanes, last):
        ends[net.z, pl.ds(0, TP), lane] = decay
        ends[net.z, pl.ds(TP, TP), lane] = value
    line.to_all(ends, es, er)
    entering = jnp.zeros((TP, head), F32)
    for z in range(seq - 1):
        later = ends[z, pl.ds(0, TP)] * entering + ends[z, pl.ds(TP, TP)]
        entering = jnp.where(z < net.z, later, entering)
    carry[...] = entering

    def join(i, _):
        m, s = 3 - i // 2, 1 - lax.rem(i, 2)
        slot = net.slot(m, s)
        at = pl.ds(pl.multiple_of(slot * rows, rows), rows)
        first = carry[pl.ds(slot, 1), :]
        states = read_halves(inflow, at) + read_halves(retain, at) * first
        state[slot, pl.ds(0, 8)] = jnp.broadcast_to(first, (8, head))
        state[slot, pl.ds(8, rows)] = states
        joined = glu_product(branch[slot], states).astype(BF)
        part[s, m] = dot(joined, wout[...]).astype(BF)
        for n in range(TP):
            @pl.when(i == n)
            def _():
                after_corner_first(scatter, n)

        return 0

    lax.fori_loop(0, TP, join, 0)
    saves.append(pltpu.make_async_copy(state, state_out, sem.at[8]))
    saves[-1].start()
    scatter.edges()

    @pl.when(net.z < seq - 1)
    def _():
        lax.fori_loop(0, TP, lambda i, _: (halo(i).wait_send(), 0)[1], 0)

    scatter.finish()
    end_forward(scatter, residual_ref, gain_ref, out_ref, normed_ref)
    if not gathered:
        gather.finish()
    for save in saves:
        save.wait()


def rec_scratch(pack, width):
    seq, _, both = pack.shape
    return [
        pltpu.VMEM((width, both), BF),
        pltpu.VMEM((both // 2, both), BF),
        pltpu.VMEM((both // 2, width), BF),
    ]


def rec_forward(x, residual, gain, pack, small, slots):
    gathered = x.ndim == 3
    rows, width = residual.shape
    seq, _, head = pack.shape
    head = head // 2
    shape = jax.ShapeDtypeStruct
    dma = pltpu.SemaphoreType.DMA
    tokens = TP * rows
    result = list(pl.pallas_call(
        partial(rec_forward_kernel, gathered),
        in_specs=[ANY, VM, VM, ANY, VM, pl.BlockSpec(memory_space=pltpu.SMEM)],
        out_specs=[VM, VM, ANY, ANY, ANY, ANY, ANY],
        out_shape=[
            shape((rows, width), F32),
            shape((rows, width), BF),
            shape((8, 128) if gathered else (TP, rows, width), BF),
            shape((TP, rows, head), F32),
            shape((TP, rows + 8, head), F32),
            shape((TP, rows, head), BF),
            shape((TP, rows + 8, head), F32),
        ],
        scratch_shapes=plane_scratch(rows, width)
        + rec_scratch(pack, width)
        + [
            pltpu.VMEM((TP, rows, head), F32),
            pltpu.VMEM((TP, rows + 8, head), F32),
            pltpu.VMEM((TP, rows, head), BF),
            pltpu.VMEM((TP, rows + 8, head), F32),
            pltpu.VMEM((head // 128, tokens, 128), F32),
            pltpu.VMEM((head // 128, tokens, 128), F32),
            pltpu.VMEM((seq, 2 * TP, head), F32),
            pltpu.VMEM((TP, head), F32),
            dma((TP,)), dma((TP,)), dma((seq - 1,)), dma((seq - 1,)), dma((9 + 5 * seq,)),
        ],
        compiler_params=pltpu.CompilerParams(
            collective_id=5 if gathered else 3, has_side_effects=True, vmem_limit_bytes=58 << 20
        ),
        cost_estimate=pl.CostEstimate(
            flops=70 * 10**9, bytes_accessed=30 << 20, transcendentals=0
        ),
        name="rec_forward_first" if gathered else "rec_forward",
    )(x, residual, gain.reshape(1, -1), pack, small, slots))
    if gathered:
        result[2] = x
    return result


def rec_backward_kernel(
    count, g_ref, upstream_ref, values_ref, gain_ref, pack_ref, small_ref, slots_ref,
    x_ref, branch_ref, stream_ref, conv_ref, state_ref, *refs
):
    given, refs = refs[:count], refs[count:]
    grad_ref, low_ref, gain_out, gcol_ref, channel_ref, *refs = refs
    taken, refs = refs[:count], refs[count:]
    (
        full, part, near, wide, far, gs, gr, ss, sr,
    col, gates, wout, xs, branch, stream, conv, state,
    retain, direct, suffix, joined, both, gpre, mixed, ends, carry, hs, hr, es, er, sem, *sems,
    ) = refs
    net = Net()
    seq = ends.shape[0]
    line = Line(net, seq)
    gather = Gather(net, full, gs, gr)
    scatter = Scatter(net, part, near, wide, far, ss, sr)
    rows, width = full.shape[1], full.shape[2]
    head = gates.shape[0]
    own = pltpu.make_async_copy(g_ref, full.at[net.t], sem.at[0])
    loads = [
        pltpu.make_async_copy(a, b, sem.at[1 + n])
        for n, (a, b) in enumerate(
            (
                (branch_ref, branch), (state_ref, state), (conv_ref, conv), (stream_ref, stream),
                (x_ref, xs),
            )
        )
    ]
    loads = unpack_rec(pack_ref, col, wout, gates, sem, 9) + loads
    for load in [own] + loads:
        load.start()
    if count:
        exchange = Exchange(
            net, seq, given[:-1], taken[:-1], given[-1:], taken[-1:], *sems
        )
        net.enter(
            line.others + [net.device(1, 1), net.device(2, 1), net.device(3, 0), net.device(3, 1)]
        )
    else:
        net.enter(line.others)
    own.wait()
    gather.begin()

    @pl.when(net.z == seq - 1)
    def _():
        mixed[:, pl.ds(rows, 8), :] = jnp.zeros((TP, 8, head), F32)

    channel_ref[...] = jnp.zeros_like(channel_ref)
    for load in loads[:-2]:
        load.wait()

    def gate_parts(slot):
        positions = net.z * rows + lax.broadcasted_iota(jnp.int32, (rows, head), 0)
        length, offset = slots_ref[slot, 0], slots_ref[slot, 1]
        inside = inside_of(positions, offset, length)
        restart = (positions == 0) | (inside != inside_of(positions - 1, offset, length))
        pre = dot(conv[slot], gates[...])
        rate = sigmoid(pre[:, :head] + small_ref[pl.ds(CONV + 1, 1), :])
        admit = sigmoid(pre[:, head:] + small_ref[pl.ds(CONV + 2, 1), :])
        log_retain = rate * small_ref[pl.ds(CONV + 3, 1), :]
        return positions, offset, length, inside, restart, rate, admit, log_retain

    def open_block(m, s):
        slot = net.slot(m, s)
        at = pl.ds(pl.multiple_of(slot * rows, rows), rows)
        grad_joined = dot_nt(full[slot], wout[...])
        act, slope = gelu_parts(branch[slot])
        states = state[slot, pl.ds(8, rows)]
        joined[at] = (act * states).astype(BF)
        both[at, :head] = (grad_joined * states * slope).astype(BF)
        write_halves(direct, at, grad_joined * act)
        _, _, _, _, restart, _, _, log_retain = gate_parts(slot)
        write_halves(retain, at, jnp.where(restart, 0.0, jnp.exp(log_retain)))

    steps(gather, None, open_block)
    if count:
        exchange.begin()
    lanes = [pl.ds(i, 128) for i in range(0, head, 128)]

    def step(i, carried):
        at = pl.ds(rows - 1 - i, TP, stride=rows)
        result = []
        for n, (value, decay, ahead) in enumerate(carried):
            value = ahead * value + direct[n, at]
            decay = ahead * decay
            direct[n, at] = value
            suffix[n, at] = decay
            result.append((value, decay, retain[n, at]))
        return tuple(result)

    one = jnp.minimum(retain[0, pl.ds(0, TP)] + 2.0, 1.0)
    last = lax.fori_loop(
        0, rows, step, tuple((jnp.zeros((TP, 128), F32), one, one) for _ in lanes), unroll=8
    )
    for lane, (value, decay, first) in zip(lanes, last):
        ends[net.z, pl.ds(0, TP), lane] = first * decay
        ends[net.z, pl.ds(TP, TP), lane] = first * value
    line.to_all(ends, es, er)
    entering = jnp.zeros((TP, head), F32)
    for z in range(seq - 1, 0, -1):
        earlier = ends[z, pl.ds(0, TP)] * entering + ends[z, pl.ds(TP, TP)]
        entering = jnp.where(z > net.z, earlier, entering)
    carry[...] = entering
    loads[-2].wait()

    def halo(i):
        slot = net.slot(3 - i // 2, 1 - lax.rem(i, 2))
        return remote(
            mixed.at[slot, pl.ds(0, 8)], mixed.at[slot, pl.ds(rows, 8)],
            hs.at[i], hr.at[i], line.before,
        )

    def through_gates(i):
        slot = net.slot(3 - i // 2, 1 - lax.rem(i, 2))
        at = pl.ds(pl.multiple_of(slot * rows, rows), rows)
        grad_states = read_halves(direct, at) + read_halves(suffix, at) * carry[pl.ds(slot, 1), :]
        positions, offset, length, inside, restart, rate, admit, log_retain = gate_parts(slot)
        low = conv[slot].astype(F32)
        kept = jnp.exp(log_retain)
        root = jnp.sqrt(one_minus_exp(2.0 * log_retain))
        scale = jnp.where(restart, 1.0, root)
        grad_admit = grad_states * scale * low
        grad_scale = grad_states * admit * low
        grad_log = grad_states * state[slot, pl.ds(7, rows)] * kept - grad_scale * kept * kept / root
        grad_log = jnp.where(restart, 0.0, grad_log)
        rate_part = grad_log * small_ref[pl.ds(CONV + 3, 1), :] * rate * (1.0 - rate)
        admit_part = grad_admit * admit * (1.0 - admit)
        gpre[at, :head] = rate_part.astype(BF)
        gpre[at, head:] = admit_part.astype(BF)
        grad_mixed = grad_states * scale * admit + dot_nt(gpre[at], gates[...])
        mixed[slot, pl.ds(0, rows)] = grad_mixed

        @pl.when(net.z > 0)
        def _():
            halo(i).start()

        sums = [jnp.sum(grad_mixed * stream[slot, pl.ds(8, rows)], axis=0, keepdims=True)]
        for j in range(1, CONV):
            same = jnp.where(inside == inside_of(positions - j, offset, length), 1.0, 0.0)
            sums.append(
                jnp.sum(
                    grad_mixed * stream[slot, pl.ds(8 - j, rows)] * same, axis=0, keepdims=True
                )
            )
        for term in (grad_mixed, rate_part, admit_part, grad_log * rate):
            sums.append(jnp.sum(term, axis=0, keepdims=True))
        for n, term in enumerate(sums):
            channel_ref[pl.ds(n, 1), :] += term

    def to_input(i):
        m, s = 3 - i // 2, 1 - lax.rem(i, 2)
        slot = net.slot(m, s)
        at = pl.ds(pl.multiple_of(slot * rows, rows), rows)

        @pl.when(net.z < seq - 1)
        def _():
            halo(i).wait_recv()

        positions = net.z * rows + lax.broadcasted_iota(jnp.int32, (rows, head), 0)
        length, offset = slots_ref[slot, 0], slots_ref[slot, 1]
        inside = inside_of(positions, offset, length)
        grad_stream = small_ref[pl.ds(0, 1), :] * mixed[slot, pl.ds(0, rows)]
        for j in range(1, CONV):
            same = jnp.where(inside == inside_of(positions + j, offset, length), 1.0, 0.0)
            grad_stream += small_ref[pl.ds(j, 1), :] * mixed[slot, pl.ds(j, rows)] * same
        both[at, head:] = grad_stream.astype(BF)
        part[s, m] = dot_nt(both[at], col[...]).astype(BF)

    def one_block(i, _):
        @pl.when(i < TP)
        def _():
            through_gates(i)

        @pl.when(i >= LATER)
        def _():
            to_input(i - LATER)

        for n in range(TP):
            @pl.when(i == n + LATER)
            def _():
                after_corner_first(scatter, n)

        return 0

    lax.fori_loop(0, TP + LATER, one_block, 0)
    scatter.edges()
    loads[-1].wait()
    own_rows = width // (TP * seq)
    tile = 2 * seq * own_rows

    def columns(j, _):
        x = xs[:, pl.ds(pl.multiple_of(j * tile, 128), tile)]
        product = dot_tn(x, both[...]).astype(BF)
        for r in range(2):
            for z in range(seq):
                low = (r * seq + z) * own_rows
                at = pl.ds(pl.multiple_of((2 * j + r) * own_rows, own_rows), own_rows)
                gcol_ref[z, at] = product[low : low + own_rows]
        return 0

    lax.fori_loop(0, TP // 2, columns, 0)
    low_conv = conv[...].reshape(TP * rows, head)
    product = dot_tn(low_conv, gpre[...]).astype(BF)
    third, base, part_head = width // 3, width // seq, head // seq
    for z in range(seq):
        low = base + 3 * part_head
        gcol_ref[z, low : low + part_head] = product[z * part_head : (z + 1) * part_head]
    for j in range(3):
        at = pl.ds(j * third, third)
        product = dot_tn(joined[...], full[:, :, at].reshape(TP * rows, third)).astype(BF)
        for z in range(seq):
            low = base + j * part_head
            gcol_ref[z, low : low + part_head] = product[z * part_head : (z + 1) * part_head]

    @pl.when(net.z > 0)
    def _():
        lax.fori_loop(0, TP, lambda i, _: (halo(i).wait_send(), 0)[1], 0)

    scatter.finish()
    if count:
        exchange.finish()
    end_backward(scatter, upstream_ref, values_ref, gain_ref, grad_ref, low_ref, gain_out)
    gather.finish()


def rec_backward(g, upstream, values, gain, pack, small, slots, saved, given):
    rows, width = g.shape
    seq, _, head = pack.shape
    head = head // 2
    tokens = TP * rows
    shape = jax.ShapeDtypeStruct
    dma = pltpu.SemaphoreType.DMA
    x, branch, stream, conv, state = saved
    return pl.pallas_call(
        partial(rec_backward_kernel, len(given)),
        in_specs=[ANY, VM, VM, VM, ANY, VM, pl.BlockSpec(memory_space=pltpu.SMEM)]
        + [ANY] * (5 + len(given)),
        out_specs=[VM] * 5 + [ANY] * len(given),
        out_shape=[
            shape((rows, width), F32),
            shape((rows, width), BF),
            shape((1, width), F32),
            shape(pack.shape, BF),
            shape((8, head), F32),
        ]
        + [shape(array.shape, array.dtype) for array in given],
        scratch_shapes=plane_scratch(rows, width)
        + rec_scratch(pack, width)
        + [
            pltpu.VMEM((tokens, width), BF),
            pltpu.VMEM(branch.shape, F32),
            pltpu.VMEM(stream.shape, F32),
            pltpu.VMEM(conv.shape, BF),
            pltpu.VMEM(state.shape, F32),
            pltpu.VMEM((head // 128, tokens, 128), F32),
            pltpu.VMEM((head // 128, tokens, 128), F32),
            pltpu.VMEM((head // 128, tokens, 128), F32),
            pltpu.VMEM((tokens, head), BF),
            pltpu.VMEM((tokens, 2 * head), BF),
            pltpu.VMEM((tokens, 2 * head), BF),
            pltpu.VMEM((TP, rows + 8, head), F32),
            pltpu.VMEM((seq, 2 * TP, head), F32),
            pltpu.VMEM((TP, head), F32),
            dma((TP,)), dma((TP,)), dma((seq - 1,)), dma((seq - 1,)), dma((9 + 5 * seq,)),
        ]
        + (exchange_scratch(given[:-1], given[-1:]) if given else []),
        compiler_params=pltpu.CompilerParams(
            collective_id=8 if given else 4, has_side_effects=True, vmem_limit_bytes=60 << 20
        ),
        cost_estimate=pl.CostEstimate(
            flops=80 * 10**9, bytes_accessed=30 << 20, transcendentals=0
        ),
        name="rec_backward_exchange" if given else "rec_backward",
    )(
        g, upstream, values, gain.reshape(1, -1), pack, small, slots,
        x.reshape(tokens, width), branch, stream, conv, state, *given,
    )


def open_kernel(
    x_ref, small_ref, gain_ref, slot_ref, pack_ref,
    small_out, gain_out, slot_out, full_out, pack_out,
    full, smalls, gains, slots, gs, gr, ps, pr, sem,
):
    net = Net()
    seq = smalls.shape[0]
    line = Line(net, seq)
    gather = Gather(net, full, gs, gr)
    plane = [net.device(m, s) for m in range(4) for s in range(2)][1:]
    mine = [
        pltpu.make_async_copy(small_ref, smalls.at[net.z], sem.at[0]),
        pltpu.make_async_copy(gain_ref, gains.at[net.z], sem.at[1]),
        pltpu.make_async_copy(slot_ref, slots.at[net.t], sem.at[2]),
    ]
    own_pack = pltpu.make_async_copy(pack_ref, pack_out.at[net.z], sem.at[4])
    for copy in mine + [own_pack]:
        copy.start()
    net.enter(line.others + [net.device(1, 1), net.device(2, 1), net.device(3, 0), net.device(3, 1)])
    for copy in mine:
        copy.wait()

    sends, arrivals = [], []

    def push(ref, own, source, to):
        n = len(sends)
        at, from_at = ref.at[own], ref.at[source]
        sends.append(remote(at, at, ps.at[n], pr.at[n], to))
        arrivals.append(remote(from_at, from_at, ps.at[n], pr.at[n], to))

    for ref in (gains, smalls):
        for d, to in enumerate(line.others):
            push(ref, net.z, lax.rem(net.z + seq - 1 - d, seq), to)
    for n, to in enumerate(plane):
        m, s = (n + 1) // 2, (n + 1) % 2
        push(slots, net.t, net.slot(m, s), to)
    for copy in sends:
        copy.start()
    first = len(sends)

    def hop(way, e):
        n = first + 2 * e + (0 if way > 0 else 1)
        to = (net.base + net.t, net.z + way)
        at = pack_ref if e == 0 else pack_out.at[net.z - way * e]
        lands = pack_out.at[net.z - way * e]
        return remote(at, lands, ps.at[n], pr.at[n], to)

    def forward(way, e):
        place = net.z if way > 0 else seq - 1 - net.z

        @pl.when((place >= e) & (place < seq - 1))
        def _():
            if e > 0:
                landed(way, e - 1)
            hop(way, e).start()

        if e > 0:
            @pl.when((place >= e) & (place == seq - 1))
            def _():
                landed(way, e - 1)

    def landed(way, e):
        n = first + 2 * e + (0 if way > 0 else 1)
        from_at = pack_out.at[net.z - way * (e + 1)]
        remote(from_at, from_at, ps.at[n], pr.at[n], (net.base + net.t, net.z)).wait_recv()

    def last(way):
        place = net.z if way > 0 else seq - 1 - net.z

        @pl.when(place == seq - 1)
        def _():
            landed(way, seq - 2)

        for e in range(seq - 1):
            @pl.when((place >= e) & (place < seq - 1))
            def _():
                hop(way, e).wait_send()

    forward(1, 0)
    forward(-1, 0)
    for copy in arrivals[: seq - 1]:
        copy.wait_recv()
    rows, width = x_ref.shape
    part, chunk = width // seq, 32

    def norm(i, _):
        at = pl.ds(pl.multiple_of(i * chunk, chunk), chunk)
        value = x_ref[at].astype(F32)
        scale = lax.rsqrt(jnp.mean(value * value, axis=-1, keepdims=True) + EPSILON)
        for z in range(seq):
            low = z * part
            full[net.t, at, low : low + part] = (
                value[:, low : low + part] * scale * gains[z, pl.ds(0, 1), :]
            ).astype(BF)
        return 0

    lax.fori_loop(0, rows // chunk, norm, 0)
    gather.begin()
    for copy in arrivals[seq - 1 :]:
        copy.wait_recv()
    saves = [
        pltpu.make_async_copy(a, b, sem.at[n])
        for n, (a, b) in enumerate(((smalls, small_out), (gains, gain_out), (slots, slot_out)))
    ]
    for save in saves:
        save.start()
    for n in range(1, TP):
        gather.before(n)
        if n == 2:
            forward(1, 1)
            forward(-1, 1)
    gather.finish()
    saves.append(pltpu.make_async_copy(full, full_out, sem.at[3]))
    saves[-1].start()
    for e in range(2, seq - 1):
        forward(1, e)
        forward(-1, e)
    last(1)
    last(-1)

    for copy in sends:
        copy.wait_send()
    own_pack.wait()
    for save in saves:
        save.wait()


def opening(seq, x, small, gain, slot, pack):
    rows, width = x.shape
    shape = jax.ShapeDtypeStruct
    dma = pltpu.SemaphoreType.DMA
    pushes = 4 * (seq - 1) + TP - 1
    return pl.pallas_call(
        open_kernel,
        in_specs=[VM] + [ANY] * 4,
        out_specs=[ANY] * 5,
        out_shape=[
            shape((seq,) + small.shape, F32),
            shape((seq,) + gain.shape, F32),
            shape((TP,) + slot.shape, jnp.int32),
            shape((TP, rows, width), BF),
            shape((seq,) + pack.shape, BF),
        ],
        scratch_shapes=[
            pltpu.VMEM((TP, rows, width), BF),
            pltpu.VMEM((seq,) + small.shape, F32),
            pltpu.VMEM((seq,) + gain.shape, F32),
            pltpu.VMEM((TP,) + slot.shape, jnp.int32),
            dma((10,)), dma((10,)), dma((pushes,)), dma((pushes,)), dma((5,)),
        ],
        compiler_params=pltpu.CompilerParams(
            collective_id=6, has_side_effects=True, vmem_limit_bytes=40 << 20
        ),
        cost_estimate=pl.CostEstimate(
            flops=40 * 10**9, bytes_accessed=10 << 20, transcendentals=0
        ),
        name="opening",
    )(x, small, gain, slot, pack)


def close_kernel(layers, gain_ref, channel_ref, *refs):
    rows_in, refs = refs[:layers], refs[layers:]
    count = (len(refs) - 10 - layers) // 2
    blocks, (gain_out, channel_out) = refs[:count], refs[count : count + 2]
    moved, refs = refs[count + 2 : 2 * count + 2], refs[2 * count + 2 :]
    rows_out = refs[:layers]
    plane_gain, line_gain, line_channel, ps, pr, *sems = refs[layers:]
    net = Net()
    seq = line_gain.shape[0]
    line = Line(net, seq)
    plane = [(m, s) for m in range(4) for s in range(2)][1:]
    plane_gain[net.t] = gain_ref[...]
    line_channel[net.z] = channel_ref[...]
    net.enter(line.others + [net.device(1, 1), net.device(2, 1), net.device(3, 0), net.device(3, 1)])
    used = []

    def push(src, dst, landed, to):
        n = len(used)
        used.append(remote(src, dst, ps.at[n], pr.at[n], to))
        used[-1].start()
        return remote(src, landed, ps.at[n], pr.at[n], to)

    gains = [
        push(
            plane_gain.at[net.t], plane_gain.at[net.t], plane_gain.at[net.slot(m, s)],
            net.device(m, s),
        )
        for m, s in plane
    ]
    sources = [lax.rem(net.z + seq - 1 - d, seq) for d in range(seq - 1)]
    rest = [
        push(line_channel.at[net.z], line_channel.at[net.z], line_channel.at[source], to)
        for source, to in zip(sources, line.others)
    ]
    exchange = Exchange(net, seq, blocks, moved, rows_in, rows_out, *sems)
    exchange.begin()
    for copy in gains:
        copy.wait_recv()
    total = plane_gain[0]
    for t in range(1, TP):
        total += plane_gain[t]
    line_gain[net.z] = total
    for source, to in zip(sources, line.others):
        rest.append(push(line_gain.at[net.z], line_gain.at[net.z], line_gain.at[source], to))
    for copy in rest:
        copy.wait_recv()
    total, channel = line_gain[0], line_channel[0]
    for z in range(1, seq):
        total += line_gain[z]
        channel += line_channel[z]
    gain_out[...] = total
    channel_out[...] = channel
    for copy in used:
        copy.wait_send()
    exchange.finish()


def closing(seq, gains, channels, rows, blocks):
    shape = jax.ShapeDtypeStruct
    dma = pltpu.SemaphoreType.DMA
    pushes = TP - 1 + 2 * (seq - 1)
    return pl.pallas_call(
        partial(close_kernel, len(rows)),
        in_specs=[VM, VM] + [ANY] * (len(rows) + len(blocks)),
        out_specs=[VM, VM] + [ANY] * (len(rows) + len(blocks)),
        out_shape=[shape(gains.shape, F32), shape(channels.shape, F32)]
        + [shape(block.shape, block.dtype) for block in blocks + rows],
        scratch_shapes=[
            pltpu.VMEM((TP,) + gains.shape, F32),
            pltpu.VMEM((seq,) + gains.shape, F32),
            pltpu.VMEM((seq,) + channels.shape, F32),
            dma((pushes,)), dma((pushes,)),
        ]
        + exchange_scratch(blocks, rows),
        compiler_params=pltpu.CompilerParams(
            collective_id=7, has_side_effects=True, vmem_limit_bytes=40 << 20
        ),
        cost_estimate=pl.CostEstimate(
            flops=40 * 10**9, bytes_accessed=10 << 20, transcendentals=0
        ),
        name="closing",
    )(gains, channels, *rows, *blocks)


def layer_backward(split, upstream, upstream_low, w, saved, slots, pending):
    residual, kept, middle, kept_two = saved
    pending_mlp, pending_rec = pending
    upstream_low, pending_mlp = lax.optimization_barrier((upstream_low, pending_mlp))
    grad_middle, mid_low, grad_gain_two, g_mlp = mlp_backward(
        upstream_low, upstream, middle, w["gain"][1], w["mlp"], *kept_two
    )
    mlp_share = over_seq(g_mlp)
    mid_low, pending_rec = lax.optimization_barrier((mid_low, pending_rec))
    given = []
    if not isinstance(pending_mlp, tuple):
        (mlp_block, rows), (rec_block, _) = split(pending_mlp), split(pending_rec)
        given = [mlp_block, rec_block, rows]
    grad, grad_low, grad_gain_one, g_rec, channel, *taken = rec_backward(
        mid_low, grad_middle, residual, w["gain"][0], w["rec"], w["small"], slots, kept, given
    )
    g_rec, mlp_share = lax.optimization_barrier((g_rec, mlp_share))
    rec_share = over_seq(g_rec)
    slope = 8.0 * jax.nn.sigmoid(-w["decay"])
    channel = jnp.concatenate([channel[:7], channel[7:] * slope], 0)
    gains = jnp.concatenate([grad_gain_one, grad_gain_two], 0)
    return grad, grad_low, (mlp_share, rec_share), channel, gains, (pending_mlp, pending_rec), taken


def over_seq(value):
    return lax.psum_scatter(value, "seq", scatter_dimension=0, tiled=False)


def columns(parts):
    return jnp.moveaxis(parts, 0, 1).reshape(parts.shape[1], -1)


def unit_columns(parts, seq):
    tp, n, units = parts.shape
    part = units // seq
    places = {}
    for t in range(tp):
        for p in range(seq):
            places[p * tp + t // seq * seq + (t + p) % seq] = (t, p)
    chunks = [places[q] for q in range(tp * seq)]
    return jnp.concatenate([parts[t, :, p * part : (p + 1) * part] for t, p in chunks], 1)


def owned_grads(plan, down_rows, rec_share, mlp, rec, width, head, units):
    base = width // plan.seq
    h, u = head // plan.seq, units // plan.seq
    out = [rec_share[base + i * h : base + (i + 1) * h] for i in range(3)]
    gates = rec_share[base + 3 * h :]
    rest, blocks = mlp_split(width, 2 * units)
    down = [down_rows[u:, i * rest : (i + 1) * rest] for i in range(blocks)]
    grads = [
        columns(rec[:, :, :head]),
        columns(rec[:, :, head:]),
        gates[:, :head],
        gates[:, head:],
        jnp.concatenate(out, 1),
        unit_columns(mlp[:, :, :units], plan.seq),
        unit_columns(mlp[:, :, units:], plan.seq),
        jnp.concatenate([down_rows[:u], jnp.concatenate(down, 0)], 1),
    ]
    return [to_owners(plan, g.astype(F32), 0) for g in grads]


def local(plan, *args):
    (
        block_input, cotangent, lengths, offsets, norm_gains, branch_proj, stream_proj, conv_kernel,
        conv_bias, rate_proj, admit_proj, gate_bias, decay_logit, out_proj, mlp_gate, mlp_up,
        mlp_down,
    ) = args
    tp, dp, seq = plan.tp, plan.dp, plan.seq
    t = lax.axis_index("rep") % tp
    z = lax.axis_index("seq")
    rows = block_input.shape[0]
    head = branch_proj.shape[2] // tp
    units = mlp_gate.shape[2] // tp

    channels = conv_kernel.shape[2]
    small = jnp.concatenate([conv_kernel, conv_bias[:, None], gate_bias, decay_logit[:, None]], 1)
    small = small.reshape(LAYERS * 8, channels).astype(F32)
    slot = jnp.pad(jnp.stack([lengths, offsets], 1), ((0, 7), (0, 126)))
    def col(weight, layer, width, t):
        size = (1, weight.shape[1], width)
        return lax.dynamic_slice(weight, (layer, 0, t * width), size)[0]

    def chunk(weight, layer, t):
        size = weight.shape[1] // tp
        return lax.dynamic_slice(weight, (layer, t * size, 0), (1, size, weight.shape[2]))[0]

    def below(rows, twice):
        rest, blocks = mlp_split(rows.shape[1], twice)
        low = rows.shape[0] // blocks
        side = [rows[i * low : (i + 1) * low, twice:] for i in range(blocks)]
        return jnp.concatenate([rows[:, :twice], jnp.concatenate(side, 1)], 0)

    def rec_rows(l, t):
        out = chunk(out_proj, l, t)
        gates = jnp.concatenate([chunk(rate_proj, l, t), chunk(admit_proj, l, t)], 1)
        out = [out[:, i * 2 * head : (i + 1) * 2 * head] for i in range(3)] + [gates]
        return jnp.concatenate(out, 0)

    def rec_pack(l, rows_of, t):
        rec = jnp.concatenate([col(branch_proj, l, head, t), col(stream_proj, l, head, t)], 1)
        return jnp.concatenate([rec, rows_of], 0)

    def unit_chunk(t, plane):
        return t // seq * seq + (t + plane) % seq

    def mlp_rows(l, t):
        return below(chunk(mlp_down, l, unit_chunk(t, z)), 2 * units)

    def mlp_pack(l, t):
        rows_of, part = mlp_gate.shape[1], units // seq
        cols = [
            lax.dynamic_slice(
                weight, (l, 0, (p * tp + unit_chunk(t, p)) * part), (1, rows_of, part)
            )[0]
            for weight in (mlp_gate, mlp_up)
            for p in range(seq)
        ]
        return jnp.concatenate([jnp.concatenate(cols, 1), mlp_rows(l, t)], 0)

    pack = rec_pack(0, owner_chunks(plan, rec_rows(0, t)), t)
    mlp = mlp_pack(0, t)
    smalls, gains, layout, normed, rec = opening(
        seq, block_input, small, norm_gains.reshape(2 * LAYERS, -1).astype(F32), slot, pack
    )
    t, mlp, rec = lax.optimization_barrier((t, mlp, rec))
    layout = layout[:, 0, :2]
    gains = jnp.moveaxis(gains, 0, 1).reshape(LAYERS, 2, -1)
    smalls = jnp.moveaxis(smalls, 0, 1).reshape(LAYERS, 8, -1)
    smalls = lax.dynamic_slice_in_dim(smalls, t * head, head, 2)


    residual = block_input.astype(F32)
    saved_all, weights = [], []
    for l in range(LAYERS):
        w = dict(
            gain=gains[l],
            small=jnp.concatenate([smalls[l, :7], -8.0 * jax.nn.softplus(-smalls[l, 7:])], 0),
            decay=smalls[l, 7:],
            rec=rec,
            mlp=lax.all_gather(mlp, "seq"),
        )
        weights.append(w)
        kept = rec_forward(normed, residual, w["gain"][1], w["rec"], w["small"], layout)
        middle, normed_two, *kept = kept
        if l + 1 < LAYERS:
            t, normed_two = lax.optimization_barrier((t, normed_two))
            pack = rec_pack(l + 1, owner_chunks(plan, rec_rows(l + 1, t)), t)
            mlp, pack, normed_two = lax.optimization_barrier((mlp_pack(l + 1, t), pack, normed_two))
            rec = lax.all_gather(pack, "seq")
        output, normed, *kept_two = mlp_forward(
            normed_two, middle, gains[(l + 1) % LAYERS, 0], w["mlp"]
        )
        saved_all.append((residual, kept, middle, kept_two))
        residual = output
    positions = z * rows + jnp.arange(rows, dtype=jnp.int32)
    inside = (positions >= offsets[0]) & (positions < offsets[0] + lengths[0])
    gradient = cotangent.astype(F32) * inside.astype(F32)[:, None]

    gradient_low = gradient.astype(BF)
    width = block_input.shape[1]
    base = width // seq

    def split(share):
        return share[:base].reshape(tp, -1, share.shape[1]), share[base:]

    shares, mlps, recs, downs = ([None] * LAYERS for _ in range(4))
    channel_all, gain_all = [None] * LAYERS, [None] * LAYERS
    for l in reversed(range(LAYERS)):
        gradient, gradient_low, shares[l], channel_all[l], gain_all[l], pending, taken = layer_backward(
            split, gradient, gradient_low, weights[l], saved_all[l], layout,
            ((), ()) if l + 1 == LAYERS else shares[l + 1],
        )
        if l + 1 < LAYERS:
            shares[l + 1], mlps[l + 1], recs[l + 1], downs[l + 1] = pending, *taken
    mlp_block, rows = split(shares[0][0])
    gains, channel, mlps[0], downs[0] = closing(
        seq, jnp.concatenate(gain_all, 0), jnp.concatenate(channel_all, 0), [rows], [mlp_block]
    )
    recs[0] = lax.all_to_all(
        split(shares[0][1])[0], "rep", split_axis=0, concat_axis=0,
        axis_index_groups=plan.tp_groups,
    )
    outs = [
        owned_grads(plan, downs[l], shares[l][1], mlps[l], recs[l], width, head, units)
        for l in range(LAYERS)
    ]
    big = [jnp.stack([outs[l][i] for l in range(LAYERS)]) for i in range(8)]

    channel = lax.dynamic_slice_in_dim(channel, z * (head // seq), head // seq, 1)
    channel = to_owners(plan, channel, 1).reshape(LAYERS, 8, -1)
    if dp > 1:
        gains = lax.psum(gains, "rep", axis_index_groups=plan.dp_groups)
    own = gains.shape[1] // (plan.rep * seq)
    owner = lax.axis_index(("rep", "seq"))
    gains = lax.dynamic_slice_in_dim(gains, owner * own, own, 1).reshape(LAYERS, 2, own)
    return (
        residual.astype(BF),
        gradient,
        gains,
        big[0],
        big[1],
        channel[:, :CONV],
        channel[:, CONV],
        big[2],
        big[3],
        channel[:, CONV + 1 : CONV + 3],
        channel[:, CONV + 3],
        big[4],
        big[5],
        big[6],
        big[7],
    )


def solution(mesh):
    tokens = P(("rep", "seq"), None)
    rows = P(None, "seq", None)
    last3 = P(None, None, "seq")
    last2 = P(None, "seq")
    own_rows = P(None, ("rep", "seq"), None)
    own3 = P(None, None, ("rep", "seq"))
    own2 = P(None, ("rep", "seq"))

    def whole(*args):
        heads = args[9].shape[1] // args[9].shape[2]
        plan = Plan(mesh, heads)
        return jax.shard_map(
            partial(local, plan),
            mesh=mesh,
            in_specs=(
                tokens, tokens, P("rep"), P("rep"), last3, rows, rows, last3, last2, rows, rows,
                last3, last2, rows, rows, rows, rows,
            ),
            out_specs=(
                tokens, tokens, own3, own_rows, own_rows, own3, own2, own_rows, own_rows, own3,
                own2, own_rows, own_rows, own_rows, own_rows,
            ),
            check_vma=False,
        )(*args)

    return whole
```
